256 devices in a mesh: wide: 64 (over x, z, core), narrow: 4 (over y).
Axes of the slice: x: 4, y: 4, z: 8, core: 2. Of those that a mesh axis runs over, the one named last changes fastest.
Arguments:
- grid_latent: bfloat16 [131072, 512], P(('wide', 'narrow')), may hold values from -24 to 24
- enc_edge_latent: bfloat16 [131072, 512], P(('wide', 'narrow')), may hold values from -24 to 24
- enc_source: int32 [131072], P(('wide', 'narrow')), may hold values from 0 to 511
- enc_target_device: int32 [131072, 1], P(('wide', 'narrow')), may hold values from 0 to 255; in each aligned block of 512 rows (0 to 511, 512 to 1023, ...) at most 4 rows name the same one
- enc_target_row: int32 [131072], P(('wide', 'narrow')), may hold values from 0 to 159
- mesh_static: bfloat16 [40960, 512], P(('wide', 'narrow')), may hold values from -6 to 6
- mesh_edge_latent: bfloat16 [327680, 512], P(('wide', 'narrow')), may hold values from -24 to 24
- mesh_source: int32 [327680], P(('wide', 'narrow')), may hold values from 0 to 479
- mesh_target: int32 [327680], P(('wide', 'narrow')), may hold values from 0 to 159
- w_enc_edge: bfloat16 [512, 512], replicated, may hold values from -0.25 to 0.25
- w_enc_grid: bfloat16 [512, 512], replicated, may hold values from -0.25 to 0.25
- w_enc_out: bfloat16 [512, 512], replicated, may hold values from -0.25 to 0.25
- w_proc_edge: bfloat16 [512, 512], replicated, may hold values from -0.25 to 0.25
- w_proc_src: bfloat16 [512, 512], replicated, may hold values from -0.25 to 0.25
- w_proc_dst: bfloat16 [512, 512], replicated, may hold values from -0.25 to 0.25
- w_proc_out: bfloat16 [512, 512], replicated, may hold values from -0.25 to 0.25
- w_node_self: bfloat16 [512, 512], replicated, may hold values from -0.25 to 0.25
- w_node_agg: bfloat16 [512, 512], replicated, may hold values from -0.25 to 0.25
- w_node_out: bfloat16 [512, 512], replicated, may hold values from -0.25 to 0.25
- cotangent: bfloat16 [40960, 512], P(('wide', 'narrow')), may hold values from -6 to 6
Outputs:
- mesh_out: bfloat16 [40960, 512], P(('wide', 'narrow'))
- grid_grad: float32 [131072, 512], P(('wide', 'narrow'))
- weight_grads: float32 [2621440], P(('wide', 'narrow'))
- mesh_grad: float32 [40960, 512], P(('wide', 'narrow'))
The draws below stay inside these ranges and needn't reach their ends.
Inputs may be any that keep to these rules, and one draw needn't show every extreme that they name: `enc_target_device`: among the 512 rows of one device no device is named more than 4 times, and that many in some device's rows. `mesh_source`: table rows 0 to 159 are the mesh rows of the device one index lower along wide (wrapping), the next 160 the device's own, the last 160 those of the device one index higher.
All inputs are finite; a program needn't handle non-finite values.
Results may differ from the reference program's by a relative error of at most 0.029.
Values may be sent and summed in bfloat16 or wider, within the bound.
No kernel may reach another device: no remote copies, remote signals or barrier semaphores. Data moves between devices by JAX's collectives and lax.ppermute only.
A program may use at most 128 MiB of HBM per device.

```python
import math
import jax
import jax.numpy as jnp
import numpy as np

L = 512
MDEG = 8
G_DEV = 512
M_DEV = 160
CAP = 4
GRID = 131072
EDGES = 131072
MESH = 40960
MEDGES = 327680
N_WIDE = 64
N_NARROW = 4
DEVICES = 256


def place_ends(result, stream_key, least, largest):
    spot = [jax.random.randint(jax.random.fold_in(stream_key, axis), (), 0, length) for axis, length in enumerate(result.shape)]
    main_axis = result.shape.index(max(result.shape))
    next_to = spot[:main_axis] + [(spot[main_axis] + 1) % result.shape[main_axis]] + spot[main_axis + 1:]
    return result.at[tuple(spot)].set(least).at[tuple(next_to)].set(largest)


def with_spikes(entries, stream_key, source, target, parts, factor):
    def block_of(dim):
        return (jnp.arange(entries.shape[dim]) // (entries.shape[dim] // parts)).reshape((-1,) + (1,) * (entries.ndim - 1 - dim))

    first = jax.random.permutation(stream_key, parts)[block_of(target)]
    far = (block_of(target) + parts // 2) % parts
    return jnp.where((block_of(source) == first) | (block_of(source) == far), factor * entries, entries)


def block_levels(own_key, shape, split, smallest, largest):
    def one(axis_at, shards_of):
        steps = jax.random.uniform(jax.random.fold_in(jax.random.fold_in(own_key, 6), axis_at), (shards_of,), jnp.float32, smallest / len(split), largest / len(split))
        return jnp.repeat(jnp.exp(steps), shape[axis_at] // shards_of).reshape((-1,) + (1,) * (len(shape) - axis_at - 1))

    factor_of = one(*split[0])
    for cut in split[1:]:
        factor_of = factor_of * one(*cut)
    return factor_of


def deal_out(key, own, number, rows, count, top, most, lean):
    order = jax.random.permutation(key, count)
    crowded, usual = load_shares(count, rows * top, most, lean, True), load_shares(count, rows * top, most, lean, False)
    places = jnp.arange(count)

    def named(tallies, turn):
        used = int((tallies > 0).sum())
        fixed = max(1, used // 4)
        passed = fixed + (places - fixed + turn * (used - fixed)) % max(1, count - fixed)
        return jnp.zeros((count,), jnp.int32).at[order[jnp.where(places < fixed, places, passed)]].set(jnp.asarray(tallies, jnp.int32))

    tallies = jnp.where(number % 4 == 0, named(crowded, number // 4), named(usual, number - number // 4 - 1))
    mixed = jax.random.permutation(jax.random.fold_in(own, 3), count)
    source_of, sink = mixed[0:count // 2 * 2:2], mixed[1:count // 2 * 2:2]
    margin = jnp.minimum(tallies[source_of] - 1, most - tallies[sink]) // 2
    margin = jnp.where((source_of == order[0]) | (sink == order[0]) | (tallies[sink] == 0), 0, jnp.maximum(margin, 0))
    passed = jax.random.randint(jax.random.fold_in(own, 4), (count // 2,), 0, 1 << 20) % (margin + 1)
    tallies = tallies.at[source_of].add(-passed).at[sink].add(passed)
    members = jnp.searchsorted(jnp.cumsum(tallies), jnp.arange(rows * top), side="right").astype(jnp.int32)
    grid = members.reshape(top, rows).T
    grid = grid[jax.random.permutation(jax.random.fold_in(own, 1), rows)]
    turn = jax.random.randint(jax.random.fold_in(own, 2), (rows, 1), 0, top)
    return jnp.take_along_axis(grid, (jnp.arange(top)[None, :] + turn) % top, axis=1)


def load_shares(count, total, most, lean, full):
    portions = [(1 << 20) // math.isqrt(grade ** lean) + 1 for grade in range(1, count + 1)]
    largest = most if full else min(most, max(-(-total // count), total * portions[0] // sum(portions)))
    least = 1 if total - largest >= count - 1 else 0
    holding, rest = [largest] + [least] * (count - 1), total - largest - least * (count - 1)
    while rest > 0:
        free = [i for i in range(1, count) if holding[i] < largest] or [i for i in range(1, count) if holding[i] < most]
        pool, remaining = sum([portions[i] for i in free]), rest
        for i in free:
            addition = min(most - holding[i], max(1, remaining * portions[i] // pool), rest)
            holding[i] = holding[i] + addition
            rest = rest - addition
    return np.array(holding)


def normal_values(rng, dims, deviation, reach, pieces=(), kind=jnp.bfloat16):
    entries = deviation * jax.random.normal(rng, dims, jnp.float32)
    if pieces:
        entries = entries * block_levels(rng, dims, pieces, -0.22, 0.18)
    return jnp.clip(entries, -reach, reach).astype(kind)


def bell_draw_with(stream_key, shape, spread, limit, shards, heavy, held_as=jnp.bfloat16):
    values = spread * jax.random.normal(stream_key, shape, jnp.float32)
    if shards:
        values = values * block_levels(stream_key, shape, shards, -0.22, 0.18)
    return jnp.clip(with_spikes(values, jax.random.fold_in(stream_key, 3), *heavy), -limit, limit).astype(held_as)


def setup_inputs(seed: int = 0) -> dict:
    keys = jax.random.split(jax.random.key(seed), 21)
    grid_latent = bell_draw_with(keys[0], (GRID, L), 1.0, 24.0, ((0, 256),), (0, 1, 256, 6.0))
    enc_edge_latent = bell_draw_with(keys[1], (EDGES, L), 1.0, 24.0, ((0, 256),), (0, 1, 256, 6.0))
    enc_source = place_ends(jax.random.randint(keys[2], (EDGES,), 0, G_DEV), jax.random.fold_in(keys[2], 1), 0, G_DEV - 1).astype(jnp.int32)
    enc_target_device_keys = jax.random.split(jax.random.fold_in(keys[3], 1), EDGES // G_DEV)
    enc_target_device_turns = jax.random.permutation(jax.random.fold_in(keys[3], 3), EDGES // G_DEV)
    enc_target_device = jax.vmap(lambda own, number: deal_out(jax.random.fold_in(keys[3], 2), own, number, G_DEV, DEVICES, 1, CAP, 2))(enc_target_device_keys, enc_target_device_turns).reshape((EDGES, 1))
    enc_target_row = place_ends(jax.random.randint(keys[4], (EDGES,), 0, M_DEV), jax.random.fold_in(keys[4], 1), 0, M_DEV - 1).astype(jnp.int32)
    mesh_static = normal_values(keys[5], (MESH, L), 1.0, 6.0, ((0, 256),))
    mesh_edge_latent = bell_draw_with(keys[6], (MEDGES, L), 1.0, 24.0, ((0, 256),), (0, 1, 256, 6.0))
    mesh_source = place_ends(jax.random.randint(keys[7], (MEDGES,), 0, 3 * M_DEV), jax.random.fold_in(keys[7], 1), 0, (3 * M_DEV) - 1).astype(jnp.int32)
    mesh_target = place_ends(jax.random.randint(keys[8], (MEDGES,), 0, M_DEV), jax.random.fold_in(keys[8], 1), 0, M_DEV - 1).astype(jnp.int32)
    w_enc_edge = normal_values(keys[9], (L, L), L ** -0.5, 0.25)
    w_enc_grid = normal_values(keys[10], (L, L), L ** -0.5, 0.25)
    w_enc_out = normal_values(keys[11], (L, L), L ** -0.5, 0.25)
    w_proc_edge = normal_values(keys[12], (L, L), L ** -0.5, 0.25)
    w_proc_src = normal_values(keys[13], (L, L), L ** -0.5, 0.25)
    w_proc_dst = normal_values(keys[14], (L, L), L ** -0.5, 0.25)
    w_proc_out = normal_values(keys[15], (L, L), L ** -0.5, 0.25)
    w_node_self = normal_values(keys[16], (L, L), L ** -0.5, 0.25)
    w_node_agg = normal_values(keys[17], (L, L), L ** -0.5, 0.25)
    w_node_out = normal_values(keys[18], (L, L), L ** -0.5, 0.25)
    cotangent = normal_values(keys[19], (MESH, L), 1.0, 6.0, ((0, 256),))
    return dict(grid_latent=grid_latent, enc_edge_latent=enc_edge_latent, enc_source=enc_source, enc_target_device=enc_target_device, enc_target_row=enc_target_row, mesh_static=mesh_static, mesh_edge_latent=mesh_edge_latent, mesh_source=mesh_source, mesh_target=mesh_target, w_enc_edge=w_enc_edge, w_enc_grid=w_enc_grid, w_enc_out=w_enc_out, w_proc_edge=w_proc_edge, w_proc_src=w_proc_src, w_proc_dst=w_proc_dst, w_proc_out=w_proc_out, w_node_self=w_node_self, w_node_agg=w_node_agg, w_node_out=w_node_out, cotangent=cotangent)


def silu_grad(value):
    sig = jax.nn.sigmoid(value)
    return sig + value * sig * (1.0 - sig)

def mdot(left, right):
    return jnp.dot(left, right, preferred_element_type=jnp.float32)

def reference(grid_latent, enc_edge_latent, enc_source, enc_target_device, enc_target_row, mesh_static, mesh_edge_latent, mesh_source, mesh_target, w_enc_edge, w_enc_grid, w_enc_out, w_proc_edge, w_proc_src, w_proc_dst, w_proc_out, w_node_self, w_node_agg, w_node_out, cotangent):
    bf = jnp.bfloat16
    f32 = jnp.float32
    edge_dev = (jnp.arange(EDGES) // G_DEV).astype(jnp.int32)
    grow = (edge_dev * G_DEV + enc_source).astype(jnp.int32)
    mrow = (enc_target_device[:, 0] * M_DEV + enc_target_row).astype(jnp.int32)
    gathered = grid_latent[grow]
    pre_enc = mdot(enc_edge_latent, w_enc_edge) + mdot(gathered, w_enc_grid)
    act_enc = jax.nn.silu(pre_enc).astype(bf)
    message = mdot(act_enc, w_enc_out).astype(bf)
    agg0 = jax.ops.segment_sum(message.astype(f32), mrow, num_segments=MESH)
    h0 = (mesh_static.astype(f32) + agg0).astype(bf)
    per_dev = MDEG * M_DEV
    mesh_dev = (jnp.arange(MEDGES) // per_dev).astype(jnp.int32)
    trow = (mesh_dev * M_DEV + mesh_target).astype(jnp.int32)
    ids = jnp.arange(DEVICES * 3 * M_DEV).astype(jnp.int32)
    tdev = ids // (3 * M_DEV)
    tpos = ids % (3 * M_DEV)
    twide = tdev // N_NARROW
    tnar = tdev % N_NARROW
    tblk = tpos // M_DEV
    trem = tpos % M_DEV
    table_row = (((twide + tblk - 1) % N_WIDE * N_NARROW + tnar) * M_DEV + trem).astype(jnp.int32)
    table_id = (mesh_dev * (3 * M_DEV) + mesh_source).astype(jnp.int32)
    srow = table_row[table_id]
    h_src = h0[srow]
    h_dst = h0[trow]
    pre_proc = mdot(mesh_edge_latent, w_proc_edge) + mdot(h_src, w_proc_src) + mdot(h_dst, w_proc_dst)
    zeta = jax.nn.silu(pre_proc).astype(bf)
    update = mdot(zeta, w_proc_out).astype(bf)
    agg = jax.ops.segment_sum(update.astype(f32), trow, num_segments=MESH).astype(bf)
    pre_node = mdot(h0, w_node_self) + mdot(agg, w_node_agg)
    unit = jax.nn.silu(pre_node).astype(bf)
    mesh_out = (h0.astype(f32) + mdot(unit, w_node_out)).astype(bf)
    g_node_out = mdot(unit.T, cotangent)
    d_node = (mdot(cotangent, w_node_out.T) * silu_grad(pre_node)).astype(bf)
    g_node_self = mdot(h0.T, d_node)
    g_node_agg = mdot(agg.T, d_node)
    d_agg = mdot(d_node, w_node_agg.T).astype(bf)
    d_edge = d_agg[trow]
    d_proc = (mdot(d_edge, w_proc_out.T) * silu_grad(pre_proc)).astype(bf)
    g_proc_out = mdot(zeta.T, d_edge)
    g_proc_edge = mdot(mesh_edge_latent.T, d_proc)
    g_proc_src = mdot(h_src.T, d_proc)
    g_proc_dst = mdot(h_dst.T, d_proc)
    src_part = jax.ops.segment_sum(d_proc.astype(f32), table_id, num_segments=DEVICES * 3 * M_DEV).astype(bf)
    src_back = jax.ops.segment_sum(mdot(src_part, w_proc_src.T), table_row, num_segments=MESH)
    dst_sum = jax.ops.segment_sum(d_proc.astype(f32), trow, num_segments=MESH).astype(bf)
    mesh_grad = cotangent.astype(f32) + mdot(d_node, w_node_self.T) + mdot(dst_sum, w_proc_dst.T) + src_back
    d_mesh = mesh_grad.astype(bf)
    d_msg = d_mesh[mrow]
    g_enc_out = mdot(act_enc.T, d_msg)
    d_enc = (mdot(d_msg, w_enc_out.T) * silu_grad(pre_enc)).astype(bf)
    g_enc_edge = mdot(enc_edge_latent.T, d_enc)
    g_enc_grid = mdot(gathered.T, d_enc)
    grid_sum = jax.ops.segment_sum(d_enc.astype(f32), grow, num_segments=GRID).astype(bf)
    grid_grad = mdot(grid_sum, w_enc_grid.T)
    enc_scale = float(EDGES) ** (-0.5)
    proc_scale = float(MEDGES) ** (-0.5)
    node_scale = float(MESH) ** (-0.5)
    stacked = jnp.stack([g_enc_edge * enc_scale, g_enc_grid * enc_scale, g_enc_out * enc_scale, g_proc_edge * proc_scale, g_proc_src * proc_scale, g_proc_dst * proc_scale, g_proc_out * proc_scale, g_node_self * node_scale, g_node_agg * node_scale, g_node_out * node_scale])
    return (mesh_out, grid_grad, stacked.reshape(-1), mesh_grad)
```

```python
import functools

import jax
import jax.numpy as jnp
from jax import lax
from jax.experimental import pallas as pl
from jax.experimental.pallas import tpu as pltpu
from jax.sharding import PartitionSpec as P

BF = jnp.bfloat16
F32 = jnp.float32
I32 = jnp.int32
LANE = 128


def dot(left, right):
    return jnp.dot(left, right, preferred_element_type=F32)


def dot_rt(left, right):
    return lax.dot_general(left, right, (((1,), (1,)), ((), ())), preferred_element_type=F32)


def dot_lt(left, right):
    return lax.dot_general(left, right, (((0,), (0,)), ((), ())), preferred_element_type=F32)


def silu_pair(value):
    sig = jax.nn.sigmoid(value)
    act = value * sig
    return act, sig + act * (1.0 - sig)


def columns(row):
    return jnp.broadcast_to(row.astype(F32), (LANE, row.shape[1])).T


def same(cols, width, shift=0):
    wide = jnp.concatenate([cols] * (-(-width // LANE)), axis=1)
    lane = lax.broadcasted_iota(I32, wide.shape, 1) + shift
    return jnp.where(wide == lane.astype(F32), 1.0, 0.0).astype(BF)


def same_t(row, height, shift=0):
    sub = lax.broadcasted_iota(I32, (height, row.shape[1]), 0) + shift
    return jnp.where(sub == row, 1.0, 0.0).astype(BF)


def enc_forward(
    capacity, grid_ref, edge_ref, src_ref, tdev_ref, trow_ref, we_ref, wg_ref, out_ref, sg_ref, slot_ref
):
    edges, width = edge_ref.shape
    slots = out_ref.shape[0]
    tdev = tdev_ref[...]
    member = same_t(tdev, slots // capacity)
    before = lax.broadcasted_iota(I32, (edges, edges), 0) < lax.broadcasted_iota(
        I32, (edges, edges), 1
    )
    ahead = dot(member, jnp.where(before, 1.0, 0.0).astype(BF))
    rank = jnp.sum(member.astype(F32) * ahead, axis=0, keepdims=True)
    slot = tdev * capacity + rank.astype(I32)
    slot_ref[...] = slot
    tag = columns(trow_ref[...] + 1).astype(BF)
    gathered = dot(same(columns(src_ref[...]), grid_ref.shape[0]), grid_ref[...]).astype(BF)
    pre = dot(edge_ref[...], we_ref[...]) + dot(gathered, wg_ref[...])
    act, grad = silu_pair(pre)
    sg_ref[...] = grad.astype(BF)
    payload = jnp.concatenate([act.astype(BF), tag], axis=1)
    step = 256
    for at in range(0, slots, step):
        place = same_t(slot, step, at)
        out_ref[pl.ds(at, step), :] = dot(place, payload).astype(BF)


def mesh_forward(
    recv_ref, static_ref, wout_ref, wsrc_ref, wdst_ref, h0_ref, a0_ref, psrc_ref, pdst_ref, pick_ref
):
    rows, width = static_ref.shape
    padded = pick_ref.shape[1]
    tag = recv_ref[:, width:].astype(F32)
    pick = same(tag, padded, 1)
    pick_ref[...] = pick
    a0 = dot_lt(pick, recv_ref[:, :width])[:rows].astype(BF)
    a0_ref[...] = a0
    h0 = (static_ref[...].astype(F32) + dot(a0, wout_ref[...])).astype(BF)
    h0_ref[...] = h0
    psrc_ref[...] = dot(h0, wsrc_ref[...]).astype(BF)
    pdst_ref[...] = dot(h0, wdst_ref[...]).astype(BF)


def processor(
    scales,
    mel_ref,
    msrc_ref,
    mtgt_ref,
    pb_ref,
    po_ref,
    pa_ref,
    pd_ref,
    h0_ref,
    cot_ref,
    we_ref,
    wpo_ref,
    wns_ref,
    wna_ref,
    wno_ref,
    wdst_ref,
    out_ref,
    sb_ref,
    so_ref,
    sa_ref,
    mg_ref,
    gpe_ref,
    gpd_ref,
    gpo_ref,
    gns_ref,
    gna_ref,
    gno_ref,
    table,
    hot,
    sg,
    zsum,
    back,
    gacc,
):
    proc_scale, node_scale = scales
    edges, width = mel_ref.shape
    rows = h0_ref.shape[0]
    reach = table.shape[0]
    first = reach - 256
    step = 256
    steps = edges // step
    table[pl.ds(0, rows), :] = pb_ref[...]
    table[pl.ds(rows, rows), :] = po_ref[...]
    table[pl.ds(2 * rows, rows), :] = pa_ref[...]
    table[pl.ds(3 * rows, reach - 3 * rows), :] = jnp.zeros((reach - 3 * rows, width), BF)
    table[pl.ds(first, rows), :] = pd_ref[...]
    zsum[...] = jnp.zeros_like(zsum)

    def ahead(i, carry):
        at = pl.multiple_of(i * step, step)
        src = columns(msrc_ref[pl.ds(i, 1), :])
        tgt = columns(mtgt_ref[pl.ds(i, 1), :] + first)
        src = jnp.concatenate([src] * (reach // LANE), axis=1)
        tgt = jnp.concatenate([tgt] * (reach // LANE), axis=1)
        lane = lax.broadcasted_iota(I32, (step, reach), 1).astype(F32)
        chosen = jnp.where((src == lane) | (tgt == lane), 1.0, 0.0).astype(BF)
        hot[pl.ds(at, step), :] = chosen
        pre = dot(mel_ref[pl.ds(at, step), :], we_ref[...]) + dot(chosen, table[...])
        act, grad = silu_pair(pre)
        sg[pl.ds(at, step), :] = grad.astype(BF)
        zsum[...] += dot_lt(chosen[:, first:], act.astype(BF))
        return carry

    lax.fori_loop(0, steps, ahead, 0)
    zeta = zsum[pl.ds(0, rows), :].astype(BF)
    h0 = h0_ref[...]
    cot = cot_ref[...]
    agg = dot(zeta, wpo_ref[...]).astype(BF)
    pre_node = dot(h0, wns_ref[...]) + dot(agg, wna_ref[...])
    act, grad = silu_pair(pre_node)
    unit = act.astype(BF)
    out_ref[...] = (h0.astype(F32) + dot(unit, wno_ref[...])).astype(BF)
    gno_ref[...] = (dot_lt(unit, cot) * node_scale).astype(BF)
    d_node = (dot_rt(cot, wno_ref[...]) * grad).astype(BF)
    gns_ref[...] = (dot_lt(h0, d_node) * node_scale).astype(BF)
    gna_ref[...] = (dot_lt(agg, d_node) * node_scale).astype(BF)
    d_agg = dot_rt(d_node, wna_ref[...]).astype(BF)
    gpo_ref[...] = (dot_lt(zeta, d_agg) * proc_scale).astype(BF)
    d_zeta = dot_rt(d_agg, wpo_ref[...]).astype(BF)
    mg_ref[...] = cot.astype(F32) + dot_rt(d_node, wns_ref[...])
    back[...] = jnp.zeros_like(back)
    gacc[...] = jnp.zeros_like(gacc)
    table[pl.ds(first, rows), :] = d_zeta

    def behind(i, carry):
        at = pl.multiple_of(i * step, step)
        chosen = hot[pl.ds(at, step), :]
        d_edge = dot(chosen[:, first:], table[pl.ds(first, 256), :])
        d_proc = (d_edge * sg[pl.ds(at, step), :].astype(F32)).astype(BF)
        back[...] += dot_lt(chosen, d_proc)
        gacc[...] += dot_lt(mel_ref[pl.ds(at, step), :], d_proc)
        return carry

    lax.fori_loop(0, steps, behind, 0)
    gpe_ref[...] = (gacc[...] * proc_scale).astype(BF)
    sb_ref[...] = back[pl.ds(0, rows), :].astype(BF)
    so_ref[...] = back[pl.ds(rows, rows), :].astype(BF)
    sa_ref[...] = back[pl.ds(2 * rows, rows), :].astype(BF)
    dst_sum = back[pl.ds(first, rows), :].astype(BF)
    mg_ref[...] += dot_rt(dst_sum, wdst_ref[...])
    gpd_ref[...] = (dot_lt(h0, dst_sum) * proc_scale).astype(BF)


def mesh_backward(
    scales, so_ref, sb_ref, sa_ref, mg_ref, h0_ref, a0_ref, pick_ref, wsrc_ref, wout_ref,
    out_ref, ret_ref, gps_ref, geo_ref, padded,
):
    proc_scale, enc_scale = scales
    rows = h0_ref.shape[0]
    total = (so_ref[...].astype(F32) + sb_ref[...].astype(F32) + sa_ref[...].astype(F32)).astype(BF)
    grad = mg_ref[...] + dot_rt(total, wsrc_ref[...])
    out_ref[...] = grad
    d_mesh = grad.astype(BF)
    padded[...] = jnp.zeros_like(padded)
    padded[pl.ds(0, rows), :] = dot_rt(d_mesh, wout_ref[...]).astype(BF)
    step = 256
    for at in range(0, ret_ref.shape[0], step):
        ret_ref[pl.ds(at, step), :] = dot(pick_ref[pl.ds(at, step), :], padded[...]).astype(BF)
    gps_ref[...] = (dot_lt(h0_ref[...], total) * proc_scale).astype(BF)
    geo_ref[...] = (dot_lt(a0_ref[...], d_mesh) * enc_scale).astype(BF)


def enc_backward(
    enc_scale, ret_ref, slot_ref, src_ref, sg_ref, edge_ref, grid_ref, wg_ref,
    out_ref, gee_ref, geg_ref,
):
    chosen = same(columns(slot_ref[...]), ret_ref.shape[0])
    d_enc = (dot(chosen, ret_ref[...]) * sg_ref[...].astype(F32)).astype(BF)
    gee_ref[...] = (dot_lt(edge_ref[...], d_enc) * enc_scale).astype(BF)
    grid_sum = dot(same_t(src_ref[...], grid_ref.shape[0]), d_enc).astype(BF)
    geg_ref[...] = (dot_lt(grid_ref[...], grid_sum) * enc_scale).astype(BF)
    out_ref[...] = dot_rt(grid_sum, wg_ref[...])


def call(body, outs, scratch=(), flops=0, moved=0, limit=48 << 20):
    return pl.pallas_call(
        body,
        out_shape=[jax.ShapeDtypeStruct(shape, kind) for shape, kind in outs],
        scratch_shapes=[pltpu.VMEM(shape, kind) for shape, kind in scratch],
        compiler_params=pltpu.CompilerParams(vmem_limit_bytes=limit),
        cost_estimate=pl.CostEstimate(flops=flops, bytes_accessed=moved, transcendentals=0),
    )


def partner_sum(grads, core, wide):
    kept = lax.dynamic_index_in_dim(grads, core, 1, keepdims=False)
    sent = lax.dynamic_index_in_dim(grads, 1 - core, 1, keepdims=False)
    came = lax.ppermute(sent, "wide", [(i, i ^ 1) for i in range(wide)])
    return (kept.astype(F32) + came.astype(F32)).astype(BF)


def on_device(
    grid_latent,
    enc_edge_latent,
    enc_source,
    enc_target_device,
    enc_target_row,
    mesh_static,
    mesh_edge_latent,
    mesh_source,
    mesh_target,
    w_enc_edge,
    w_enc_grid,
    w_enc_out,
    w_proc_edge,
    w_proc_src,
    w_proc_dst,
    w_proc_out,
    w_node_self,
    w_node_agg,
    w_node_out,
    cotangent,
):
    wide = lax.axis_size("wide")
    narrow = lax.axis_size("narrow")
    devices = wide * narrow
    edges, width = enc_edge_latent.shape
    grid_rows = grid_latent.shape[0]
    rows = mesh_static.shape[0]
    mesh_edges = mesh_source.shape[0]
    capacity = 2 * edges // devices
    slots = devices * capacity
    enc_scale = float(edges * devices) ** (-0.5)
    proc_scale = float(mesh_edges * devices) ** (-0.5)
    node_scale = float(rows * devices) ** (-0.5)
    core = lax.axis_index("wide") % 2

    source = enc_source.reshape(1, edges)
    payload, enc_sg, slot = call(
        functools.partial(enc_forward, capacity),
        [((slots, width + LANE), BF), ((edges, width), BF), ((1, edges), I32)],
    )(
        grid_latent,
        enc_edge_latent,
        source,
        enc_target_device.reshape(1, edges),
        enc_target_row.reshape(1, edges),
        w_enc_edge,
        w_enc_grid,
    )
    received = lax.all_to_all(
        payload.reshape(devices, capacity, width + LANE),
        ("wide", "narrow"),
        split_axis=0,
        concat_axis=0,
        tiled=True,
    ).reshape(slots, width + LANE)
    h0, a0, p_src, p_dst, pick = call(
        mesh_forward,
        [((rows, width), BF)] * 4 + [((slots, 256), BF)],
    )(received, mesh_static, w_enc_out, w_proc_src, w_proc_dst)
    up = [(i, (i + 1) % wide) for i in range(wide)]
    down = [(j, i) for i, j in up]
    p_before = lax.ppermute(p_src, "wide", up)
    p_after = lax.ppermute(p_src, "wide", down)
    square = ((width, width), BF)
    block = ((rows, width), BF)
    reach = -(-3 * rows // LANE) * LANE + 256
    mesh_out, s_before, s_own, s_after, partial_grad, gpe, gpd, gpo, gns, gna, gno = call(
        functools.partial(processor, (proc_scale, node_scale)),
        [block] * 4 + [((rows, width), F32)] + [square] * 6,
        [
            ((reach, width), BF),
            ((mesh_edges, reach), BF),
            ((mesh_edges, width), BF),
            ((256, width), F32),
            ((reach, width), F32),
            ((width, width), F32),
        ],
    )(
        mesh_edge_latent,
        mesh_source.reshape(-1, 256),
        mesh_target.reshape(-1, 256),
        p_before,
        p_src,
        p_after,
        p_dst,
        h0,
        cotangent,
        w_proc_edge,
        w_proc_out,
        w_node_self,
        w_node_agg,
        w_node_out,
        w_proc_dst,
    )
    from_after = lax.ppermute(s_before, "wide", down)
    from_before = lax.ppermute(s_after, "wide", up)
    mesh_grad, returning, gps, geo = call(
        functools.partial(mesh_backward, (proc_scale, enc_scale)),
        [((rows, width), F32), ((slots, width), BF), square, square],
        [((256, width), BF)],
    )(s_own, from_after, from_before, partial_grad, h0, a0, pick, w_proc_src, w_enc_out)

    pair = 2 * narrow
    chunk = 10 * width // devices
    span = pair * chunk
    late = 2 * width
    late_groups = -(-late // span)
    first = late // span
    early = jnp.concatenate([geo, gpe, gps, gpd, gpo, gns, gna, gno], axis=0)
    early = jnp.pad(early, ((late - first * span, 0), (0, 0)))
    groups = wide // 2 - first
    early = partner_sum(early.reshape(groups, 2, narrow * chunk, width), core, wide)
    early = early.reshape(groups, narrow, chunk, width).transpose(1, 0, 2, 3)
    early = lax.psum_scatter(
        early.reshape(narrow, groups * chunk, width), "narrow", scatter_dimension=0, tiled=True
    ).reshape(groups, chunk, width)

    returned = lax.all_to_all(
        returning.reshape(devices, capacity, width),
        ("wide", "narrow"),
        split_axis=0,
        concat_axis=0,
        tiled=True,
    ).reshape(slots, width)
    grid_grad, gee, geg = call(
        functools.partial(enc_backward, enc_scale),
        [((grid_rows, width), F32), square, square],
    )(returned, slot, source, enc_sg, enc_edge_latent, grid_latent, w_enc_grid)

    last = jnp.concatenate([gee, geg], axis=0)
    last = jnp.pad(last, ((0, late_groups * span - late), (0, 0)))
    last = partner_sum(last.reshape(late_groups, 2, narrow * chunk, width), core, wide)
    last = last.reshape(late_groups, narrow, chunk, width).transpose(1, 0, 2, 3)
    last = lax.all_to_all(
        last.reshape(narrow, late_groups * chunk, width),
        "narrow",
        split_axis=0,
        concat_axis=0,
        tiled=True,
    )
    last = jnp.sum(last.astype(F32), axis=0).reshape(late_groups, chunk, width)
    shared = late_groups - first
    both = jnp.concatenate(
        [last[:first], last[first:] + early[:shared].astype(F32), early[shared:].astype(F32)], axis=0
    ).astype(BF)
    both = lax.all_to_all(
        both,
        "wide",
        split_axis=0,
        concat_axis=0,
        tiled=True,
        axis_index_groups=[[i for i in range(wide) if i % 2 == c] for c in range(2)],
    )
    summed = jnp.sum(both.astype(F32), axis=0).reshape(-1)
    return (mesh_out, grid_grad, summed, mesh_grad)


def solution(mesh):
    in_specs = (
        P(("wide", "narrow"), None),
        P(("wide", "narrow"), None),
        P(("wide", "narrow")),
        P(("wide", "narrow"), None),
        P(("wide", "narrow")),
        P(("wide", "narrow"), None),
        P(("wide", "narrow"), None),
        P(("wide", "narrow")),
        P(("wide", "narrow")),
        P(),
        P(),
        P(),
        P(),
        P(),
        P(),
        P(),
        P(),
        P(),
        P(),
        P(("wide", "narrow"), None),
    )
    out_specs = (
        P(("wide", "narrow"), None),
        P(("wide", "narrow"), None),
        P(("wide", "narrow")),
        P(("wide", "narrow"), None),
    )
    return jax.shard_map(
        on_device, mesh=mesh, in_specs=in_specs, out_specs=out_specs, check_vma=False
    )
```

```python
import functools

import jax
import jax.numpy as jnp
import numpy as np
from jax import lax
from jax.experimental import pallas as pl
from jax.experimental.pallas import tpu as pltpu
from jax.sharding import PartitionSpec as P

BF = jnp.bfloat16
F32 = jnp.float32
I32 = jnp.int32
LANE = 128


def dot(left, right):
    return jnp.dot(left, right, preferred_element_type=F32)


def dot_rt(left, right):
    return lax.dot_general(left, right, (((1,), (1,)), ((), ())), preferred_element_type=F32)


def dot_lt(left, right):
    return lax.dot_general(left, right, (((0,), (0,)), ((), ())), preferred_element_type=F32)


def silu_pair(value):
    sig = jax.nn.sigmoid(value)
    act = value * sig
    return act, sig + act * (1.0 - sig)


def columns(row):
    return jnp.broadcast_to(row.astype(F32), (LANE, row.shape[1])).T


def same(cols, width, shift=0):
    wide = jnp.concatenate([cols] * (-(-width // LANE)), axis=1)
    lane = lax.broadcasted_iota(I32, wide.shape, 1) + shift
    return jnp.where(wide == lane.astype(F32), 1.0, 0.0).astype(BF)


def same_t(row, height, shift=0):
    sub = lax.broadcasted_iota(I32, (height, row.shape[1]), 0) + shift
    return jnp.where(sub == row, 1.0, 0.0).astype(BF)


def enc_forward(
    capacity, grid_ref, edge_ref, src_ref, tdev_ref, trow_ref, we_ref, wg_ref, out_ref, sg_ref, slot_ref
):
    edges, width = edge_ref.shape
    slots = out_ref.shape[0]
    tdev = tdev_ref[...]
    member = same_t(tdev, slots // capacity)
    before = lax.broadcasted_iota(I32, (edges, edges), 0) < lax.broadcasted_iota(
        I32, (edges, edges), 1
    )
    ahead = dot(member, jnp.where(before, 1.0, 0.0).astype(BF))
    rank = jnp.sum(member.astype(F32) * ahead, axis=0, keepdims=True)
    slot = tdev * capacity + rank.astype(I32)
    slot_ref[...] = slot
    tag = columns(trow_ref[...] + 1).astype(BF)
    gathered = dot(same(columns(src_ref[...]), grid_ref.shape[0]), grid_ref[...]).astype(BF)
    pre = dot(edge_ref[...], we_ref[...]) + dot(gathered, wg_ref[...])
    act, grad = silu_pair(pre)
    sg_ref[...] = grad.astype(BF)
    payload = jnp.concatenate([act.astype(BF), tag], axis=1)
    step = 256
    for at in range(0, slots, step):
        place = same_t(slot, step, at)
        out_ref[pl.ds(at, step), :] = dot(place, payload).astype(BF)


def mesh_forward(
    recv_ref, static_ref, wout_ref, wsrc_ref, wdst_ref, h0_ref, a0_ref, psrc_ref, pdst_ref, pick_ref
):
    rows, width = static_ref.shape
    padded = pick_ref.shape[1]
    tag = recv_ref[:, width:].astype(F32)
    pick = same(tag, padded, 1)
    pick_ref[...] = pick
    a0 = dot_lt(pick, recv_ref[:, :width])[:rows].astype(BF)
    a0_ref[...] = a0
    h0 = (static_ref[...].astype(F32) + dot(a0, wout_ref[...])).astype(BF)
    h0_ref[...] = h0
    psrc_ref[...] = dot(h0, wsrc_ref[...]).astype(BF)
    pdst_ref[...] = dot(h0, wdst_ref[...]).astype(BF)


def processor(
    scales,
    mel_ref,
    msrc_ref,
    mtgt_ref,
    pb_ref,
    po_ref,
    pa_ref,
    pd_ref,
    h0_ref,
    cot_ref,
    we_ref,
    wpo_ref,
    wns_ref,
    wna_ref,
    wno_ref,
    wdst_ref,
    out_ref,
    sb_ref,
    so_ref,
    sa_ref,
    mg_ref,
    gpe_ref,
    gpd_ref,
    gpo_ref,
    gns_ref,
    gna_ref,
    gno_ref,
    table,
    hot,
    sg,
    zsum,
    back,
    gacc,
):
    proc_scale, node_scale = scales
    edges, width = mel_ref.shape
    rows = h0_ref.shape[0]
    reach = table.shape[0]
    first = reach - 256
    step = 256
    steps = edges // step
    table[pl.ds(0, rows), :] = pb_ref[...]
    table[pl.ds(rows, rows), :] = po_ref[...]
    table[pl.ds(2 * rows, rows), :] = pa_ref[...]
    table[pl.ds(3 * rows, reach - 3 * rows), :] = jnp.zeros((reach - 3 * rows, width), BF)
    table[pl.ds(first, rows), :] = pd_ref[...]
    zsum[...] = jnp.zeros_like(zsum)

    def ahead(i, carry):
        at = pl.multiple_of(i * step, step)
        src = columns(msrc_ref[pl.ds(i, 1), :])
        tgt = columns(mtgt_ref[pl.ds(i, 1), :] + first)
        src = jnp.concatenate([src] * (reach // LANE), axis=1)
        tgt = jnp.concatenate([tgt] * (reach // LANE), axis=1)
        lane = lax.broadcasted_iota(I32, (step, reach), 1).astype(F32)
        chosen = jnp.where((src == lane) | (tgt == lane), 1.0, 0.0).astype(BF)
        hot[pl.ds(at, step), :] = chosen
        pre = dot(mel_ref[pl.ds(at, step), :], we_ref[...]) + dot(chosen, table[...])
        act, grad = silu_pair(pre)
        sg[pl.ds(at, step), :] = grad.astype(BF)
        zsum[...] += dot_lt(chosen[:, first:], act.astype(BF))
        return carry

    lax.fori_loop(0, steps, ahead, 0)
    zeta = zsum[pl.ds(0, rows), :].astype(BF)
    h0 = h0_ref[...]
    cot = cot_ref[...]
    agg = dot(zeta, wpo_ref[...]).astype(BF)
    pre_node = dot(h0, wns_ref[...]) + dot(agg, wna_ref[...])
    act, grad = silu_pair(pre_node)
    unit = act.astype(BF)
    out_ref[...] = (h0.astype(F32) + dot(unit, wno_ref[...])).astype(BF)
    gno_ref[...] = (dot_lt(unit, cot) * node_scale).astype(BF)
    d_node = (dot_rt(cot, wno_ref[...]) * grad).astype(BF)
    gns_ref[...] = (dot_lt(h0, d_node) * node_scale).astype(BF)
    gna_ref[...] = (dot_lt(agg, d_node) * node_scale).astype(BF)
    d_agg = dot_rt(d_node, wna_ref[...]).astype(BF)
    gpo_ref[...] = (dot_lt(zeta, d_agg) * proc_scale).astype(BF)
    d_zeta = dot_rt(d_agg, wpo_ref[...]).astype(BF)
    mg_ref[...] = cot.astype(F32) + dot_rt(d_node, wns_ref[...])
    back[...] = jnp.zeros_like(back)
    gacc[...] = jnp.zeros_like(gacc)
    table[pl.ds(first, rows), :] = d_zeta

    def behind(i, carry):
        at = pl.multiple_of(i * step, step)
        chosen = hot[pl.ds(at, step), :]
        d_edge = dot(chosen[:, first:], table[pl.ds(first, 256), :])
        d_proc = (d_edge * sg[pl.ds(at, step), :].astype(F32)).astype(BF)
        back[...] += dot_lt(chosen, d_proc)
        gacc[...] += dot_lt(mel_ref[pl.ds(at, step), :], d_proc)
        return carry

    lax.fori_loop(0, steps, behind, 0)
    gpe_ref[...] = (gacc[...] * proc_scale).astype(BF)
    sb_ref[...] = back[pl.ds(0, rows), :].astype(BF)
    so_ref[...] = back[pl.ds(rows, rows), :].astype(BF)
    sa_ref[...] = back[pl.ds(2 * rows, rows), :].astype(BF)
    dst_sum = back[pl.ds(first, rows), :].astype(BF)
    mg_ref[...] += dot_rt(dst_sum, wdst_ref[...])
    gpd_ref[...] = (dot_lt(h0, dst_sum) * proc_scale).astype(BF)


def split_halves(core, held, layout, kept_ref, sent_ref):
    first, groups, half = layout
    width = kept_ref.shape[1]
    even = core == 0
    step = 16

    def piece(row):
        ref = held[row // width] if row < 10 * width else None
        return jnp.zeros((step, width), BF) if ref is None else ref[pl.ds(row % width, step), :]

    for group in range(groups):
        for part in range(0, half, step):
            row = (first + group) * 2 * half + part
            at = pl.ds(group * half + part, step)
            left, right = piece(row), piece(row + half)
            kept_ref[at, :] = jnp.where(even, left, right)
            sent_ref[at, :] = jnp.where(even, right, left)


def mesh_backward(
    scales, layout, core_ref, so_ref, sb_ref, sa_ref, mg_ref, h0_ref, a0_ref, pick_ref, wsrc_ref,
    wout_ref, gpe_ref, gpd_ref, gpo_ref, gns_ref, gna_ref, gno_ref,
    out_ref, ret_ref, kept_ref, sent_ref, padded, geo, gps,
):
    proc_scale, enc_scale = scales
    rows = h0_ref.shape[0]
    total = (so_ref[...].astype(F32) + sb_ref[...].astype(F32) + sa_ref[...].astype(F32)).astype(BF)
    grad = mg_ref[...] + dot_rt(total, wsrc_ref[...])
    out_ref[...] = grad
    d_mesh = grad.astype(BF)
    padded[pl.ds(rows, 256 - rows), :] = jnp.zeros((256 - rows, padded.shape[1]), BF)
    padded[pl.ds(0, rows), :] = dot_rt(d_mesh, wout_ref[...]).astype(BF)
    step = 256
    for at in range(0, ret_ref.shape[0], step):
        ret_ref[pl.ds(at, step), :] = dot(pick_ref[pl.ds(at, step), :], padded[...]).astype(BF)
    gps[...] = (dot_lt(h0_ref[...], total) * proc_scale).astype(BF)
    geo[...] = (dot_lt(a0_ref[...], d_mesh) * enc_scale).astype(BF)
    held = [None, None, geo, gpe_ref, gps, gpd_ref, gpo_ref, gns_ref, gna_ref, gno_ref]
    split_halves(core_ref[0], held, layout, kept_ref, sent_ref)


def enc_backward(
    enc_scale, layout, core_ref, ret_ref, slot_ref, src_ref, sg_ref, edge_ref, grid_ref, wg_ref,
    out_ref, kept_ref, sent_ref, gee, geg,
):
    chosen = same(columns(slot_ref[...]), ret_ref.shape[0])
    d_enc = (dot(chosen, ret_ref[...]) * sg_ref[...].astype(F32)).astype(BF)
    gee[...] = (dot_lt(edge_ref[...], d_enc) * enc_scale).astype(BF)
    grid_sum = dot(same_t(src_ref[...], grid_ref.shape[0]), d_enc).astype(BF)
    geg[...] = (dot_lt(grid_ref[...], grid_sum) * enc_scale).astype(BF)
    out_ref[...] = dot_rt(grid_sum, wg_ref[...])
    split_halves(core_ref[0], [gee, geg] + [None] * 8, layout, kept_ref, sent_ref)


def add_halves(chunk, turn_ref, kept_ref, came_ref, out_ref):
    narrow, length, width = out_ref.shape
    blocks = turn_ref.shape[0]
    step = blocks // narrow
    skip = length - kept_ref.shape[0] // narrow
    if skip:
        for y in range(narrow):
            out_ref[y, pl.ds(0, skip), :] = jnp.zeros((skip, width), BF)
    for at in range(0, kept_ref.shape[0], blocks):
        total = kept_ref[pl.ds(at, blocks), :].astype(F32) + came_ref[pl.ds(at, blocks), :].astype(F32)
        total = total.astype(BF)
        if step > chunk:
            total = dot(turn_ref[...], total).astype(BF)
        for y in range(narrow):
            out_ref[y, pl.ds(skip + at // narrow, step), :] = total[y * step : (y + 1) * step]


def turned(narrow, chunk, groups):
    rows = np.arange(groups * narrow * chunk).reshape(groups, narrow, chunk)
    rows = rows.transpose(1, 0, 2).reshape(-1)
    return jnp.asarray(rows[:, None] == np.arange(rows.size)[None, :], BF)


def call(body, outs, scratch=(), flops=0, moved=0, limit=16, scalars=0):
    ins = {}
    if scalars:
        ins["in_specs"] = [pl.BlockSpec(memory_space=pltpu.SMEM)] + [
            pl.BlockSpec(memory_space=pltpu.VMEM)
        ] * scalars
    return pl.pallas_call(
        body,
        **ins,
        out_shape=[jax.ShapeDtypeStruct(shape, kind) for shape, kind in outs],
        scratch_shapes=[pltpu.VMEM(shape, kind) for shape, kind in scratch],
        compiler_params=pltpu.CompilerParams(vmem_limit_bytes=limit << 20),
        cost_estimate=pl.CostEstimate(flops=flops, bytes_accessed=moved, transcendentals=0),
    )


def on_device(
    grid_latent,
    enc_edge_latent,
    enc_source,
    enc_target_device,
    enc_target_row,
    mesh_static,
    mesh_edge_latent,
    mesh_source,
    mesh_target,
    w_enc_edge,
    w_enc_grid,
    w_enc_out,
    w_proc_edge,
    w_proc_src,
    w_proc_dst,
    w_proc_out,
    w_node_self,
    w_node_agg,
    w_node_out,
    cotangent,
):
    wide = lax.axis_size("wide")
    narrow = lax.axis_size("narrow")
    devices = wide * narrow
    edges, width = enc_edge_latent.shape
    grid_rows = grid_latent.shape[0]
    rows = mesh_static.shape[0]
    mesh_edges = mesh_source.shape[0]
    capacity = 2 * edges // devices
    slots = devices * capacity
    enc_scale = float(edges * devices) ** (-0.5)
    proc_scale = float(mesh_edges * devices) ** (-0.5)
    node_scale = float(rows * devices) ** (-0.5)
    core = lax.axis_index("wide") % 2

    source = enc_source.reshape(1, edges)
    payload, enc_sg, slot = call(
        functools.partial(enc_forward, capacity),
        [((slots, width + LANE), BF), ((edges, width), BF), ((1, edges), I32)],
    )(
        grid_latent,
        enc_edge_latent,
        source,
        enc_target_device.reshape(1, edges),
        enc_target_row.reshape(1, edges),
        w_enc_edge,
        w_enc_grid,
    )
    received = lax.all_to_all(
        payload.reshape(devices, capacity, width + LANE),
        ("wide", "narrow"),
        split_axis=0,
        concat_axis=0,
        tiled=True,
    ).reshape(slots, width + LANE)
    h0, a0, p_src, p_dst, pick = call(
        mesh_forward,
        [((rows, width), BF)] * 4 + [((slots, 256), BF)],
    )(received, mesh_static, w_enc_out, w_proc_src, w_proc_dst)
    up = [(i, (i + 1) % wide) for i in range(wide)]
    down = [(j, i) for i, j in up]
    p_before = lax.ppermute(p_src, "wide", up)
    p_after = lax.ppermute(p_src, "wide", down)
    square = ((width, width), BF)
    block = ((rows, width), BF)
    reach = -(-3 * rows // LANE) * LANE + 256
    mesh_out, s_before, s_own, s_after, partial_grad, gpe, gpd, gpo, gns, gna, gno = call(
        functools.partial(processor, (proc_scale, node_scale)),
        [block] * 4 + [((rows, width), F32)] + [square] * 6,
        [
            ((reach, width), BF),
            ((mesh_edges, reach), BF),
            ((mesh_edges, width), BF),
            ((256, width), F32),
            ((reach, width), F32),
            ((width, width), F32),
        ],
        limit=24,
    )(
        mesh_edge_latent,
        mesh_source.reshape(-1, 256),
        mesh_target.reshape(-1, 256),
        p_before,
        p_src,
        p_after,
        p_dst,
        h0,
        cotangent,
        w_proc_edge,
        w_proc_out,
        w_node_self,
        w_node_agg,
        w_node_out,
        w_proc_dst,
    )
    from_after = lax.ppermute(s_before, "wide", down)
    from_before = lax.ppermute(s_after, "wide", up)
    chips = wide // 2
    chunk = 10 * width // devices
    half = narrow * chunk
    late = 2 * width
    block = 4 if chunk % 16 else 1
    span = 2 * half * block
    late_layout = (0, -(-late // span) * block, half)
    early_layout = (late // span * block, chips - late // span * block, half)
    turn = turned(narrow, chunk, block)
    late_block = ((late_layout[1] * half, width), BF)
    early_block = ((early_layout[1] * half, width), BF)
    where = core.reshape(1)
    swap = [(i, i ^ 1) for i in range(wide)]
    mesh_grad, returning, kept, sent = call(
        functools.partial(mesh_backward, (proc_scale, enc_scale), early_layout),
        [((rows, width), F32), ((slots, width), BF), early_block, early_block],
        [((256, width), BF), square, square],
        scalars=15,
    )(
        where, s_own, from_after, from_before, partial_grad, h0, a0, pick, w_proc_src, w_enc_out,
        gpe, gpd, gpo, gns, gna, gno,
    )
    came = lax.ppermute(sent, "wide", swap)
    far = 4 if chips > 4 else 2
    near = chips // far
    line = [[i + j * 2 * near for j in range(far)] for i in range(2 * near)]
    plane = [[i * 2 * near + 2 * j + c for j in range(near)] for i in range(far) for c in range(2)]
    turning = functools.partial(add_halves, chunk)
    (early,) = call(turning, [((narrow, chips * chunk, width), BF)])(turn, kept, came)
    early = lax.psum_scatter(early, "narrow", scatter_dimension=0, tiled=True)
    early = lax.psum_scatter(
        early.reshape(far, near * chunk, width),
        "wide",
        scatter_dimension=0,
        tiled=True,
        axis_index_groups=line,
    ).reshape(near * chunk, width)
    returned = lax.all_to_all(
        returning.reshape(devices, capacity, width),
        ("wide", "narrow"),
        split_axis=0,
        concat_axis=0,
        tiled=True,
    ).reshape(slots, width)
    grid_grad, kept, sent = call(
        functools.partial(enc_backward, enc_scale, late_layout),
        [((grid_rows, width), F32), late_block, late_block],
        [square, square],
        scalars=7,
    )(where, returned, slot, source, enc_sg, enc_edge_latent, grid_latent, w_enc_grid)
    came = lax.ppermute(sent, "wide", swap)
    spread = late_layout[1] * chunk
    (last,) = call(turning, [((narrow, spread, width), BF)])(turn, kept, came)
    last = lax.all_to_all(last, "narrow", split_axis=0, concat_axis=0, tiled=True)
    last = jnp.sum(last.astype(F32), axis=0).astype(BF)
    parts = [
        lax.ppermute(last, "wide", [(j * 2 * near + i, i) for i in range(2 * near)])
        for j in range(1, far)
    ]
    at_first = lax.axis_index("wide") < 2 * near
    last = jnp.where(at_first, last.astype(F32), 0.0) + sum(p.astype(F32) for p in parts)
    both = early.astype(F32) + last[: near * chunk]
    both = lax.all_to_all(
        both.astype(BF).reshape(near, chunk, width),
        "wide",
        split_axis=0,
        concat_axis=0,
        tiled=True,
        axis_index_groups=plane,
    )
    summed = jnp.sum(both.astype(F32), axis=0).reshape(-1)
    return (mesh_out, grid_grad, summed, mesh_grad)


def solution(mesh):
    in_specs = (
        P(("wide", "narrow"), None),
        P(("wide", "narrow"), None),
        P(("wide", "narrow")),
        P(("wide", "narrow"), None),
        P(("wide", "narrow")),
        P(("wide", "narrow"), None),
        P(("wide", "narrow"), None),
        P(("wide", "narrow")),
        P(("wide", "narrow")),
        P(),
        P(),
        P(),
        P(),
        P(),
        P(),
        P(),
        P(),
        P(),
        P(),
        P(("wide", "narrow"), None),
    )
    out_specs = (
        P(("wide", "narrow"), None),
        P(("wide", "narrow"), None),
        P(("wide", "narrow")),
        P(("wide", "narrow"), None),
    )
    return jax.shard_map(
        on_device, mesh=mesh, in_specs=in_specs, out_specs=out_specs, check_vma=False
    )
```

```python
import functools

import jax
import jax.numpy as jnp
import numpy as np
from jax import lax
from jax.experimental import pallas as pl
from jax.experimental.pallas import tpu as pltpu
from jax.sharding import PartitionSpec as P

BF = jnp.bfloat16
F32 = jnp.float32
I32 = jnp.int32
LANE = 128


def dot(left, right):
    return jnp.dot(left, right, preferred_element_type=F32)


def dot_rt(left, right):
    return lax.dot_general(left, right, (((1,), (1,)), ((), ())), preferred_element_type=F32)


def dot_lt(left, right):
    return lax.dot_general(left, right, (((0,), (0,)), ((), ())), preferred_element_type=F32)


def silu_pair(value):
    sig = jax.nn.sigmoid(value)
    act = value * sig
    return act, sig + act * (1.0 - sig)


def columns(row):
    return jnp.broadcast_to(row.astype(F32), (LANE, row.shape[1])).T


def same(cols, width, shift=0):
    wide = jnp.concatenate([cols] * (-(-width // LANE)), axis=1)
    lane = lax.broadcasted_iota(I32, wide.shape, 1) + shift
    return jnp.where(wide == lane.astype(F32), 1.0, 0.0).astype(BF)


def same_t(row, height, shift=0):
    sub = lax.broadcasted_iota(I32, (height, row.shape[1]), 0) + shift
    return jnp.where(sub == row, 1.0, 0.0).astype(BF)


def enc_forward(
    capacity, tdev_ref, trow_ref, src_ref, grid_ref, edge_ref, we_ref, wg_ref, out_ref, sg_ref, slot_ref
):
    edges, width = edge_ref.buffer.shape
    slots = out_ref.buffer.shape[0]
    tdev = tdev_ref.get()[...]
    member = same_t(tdev, slots // capacity)
    before = lax.broadcasted_iota(I32, (edges, edges), 0) < lax.broadcasted_iota(
        I32, (edges, edges), 1
    )
    ahead = dot(member, jnp.where(before, 1.0, 0.0).astype(BF))
    rank = jnp.sum(member.astype(F32) * ahead, axis=0, keepdims=True)
    slot = tdev * capacity + rank.astype(I32)
    slot_ref.buffer[...] = slot
    slot_ref.send()
    tag = columns(trow_ref.get()[...] + 1).astype(BF)
    grid = grid_ref.get()[...]
    gathered = dot(same(columns(src_ref.get()[...]), grid.shape[0]), grid).astype(BF)
    pre = dot(edge_ref.get()[...], we_ref.get()[...]) + dot(gathered, wg_ref.get()[...])
    act, grad = silu_pair(pre)
    sg_ref.buffer[...] = grad.astype(BF)
    sg_ref.send()
    payload = jnp.concatenate([act.astype(BF), tag], axis=1)
    step = 256
    for at in range(0, slots, step):
        place = same_t(slot, step, at)
        out_ref.buffer[pl.ds(at, step), :] = dot(place, payload).astype(BF)


def mesh_forward(
    recv_ref, wout_ref, static_ref, wsrc_ref, wdst_ref, h0_ref, a0_ref, psrc_ref, pdst_ref, pick_ref
):
    rows, width = static_ref.buffer.shape
    padded = pick_ref.buffer.shape[1]
    tag = recv_ref.get()[:, width:].astype(F32)
    pick = same(tag, padded, 1)
    pick_ref.buffer[...] = pick
    pick_ref.send()
    a0 = dot_lt(pick, recv_ref.get()[:, :width])[:rows].astype(BF)
    a0_ref.buffer[...] = a0
    h0 = (static_ref.get()[...].astype(F32) + dot(a0, wout_ref.get()[...])).astype(BF)
    h0_ref.buffer[...] = h0
    psrc_ref.buffer[...] = dot(h0, wsrc_ref.get()[...]).astype(BF)
    pdst_ref.buffer[...] = dot(h0, wdst_ref.get()[...]).astype(BF)


def processor(
    scales,
    msrc_ref,
    mtgt_ref,
    pb_ref,
    po_ref,
    pa_ref,
    pd_ref,
    we_ref,
    mel_ref,
    wpo_ref,
    h0_ref,
    wns_ref,
    wna_ref,
    wno_ref,
    cot_ref,
    wdst_ref,
    out_ref,
    sb_ref,
    so_ref,
    sa_ref,
    mg_ref,
    gpe_ref,
    gpd_ref,
    gpo_ref,
    gns_ref,
    gna_ref,
    gno_ref,
    table,
    hot,
    sg,
    zsum,
    back,
    gacc,
):
    proc_scale, node_scale = scales
    edges, width = mel_ref.buffer.shape
    rows = h0_ref.buffer.shape[0]
    reach = table.shape[0]
    first = reach - 256
    step = 256
    steps = edges // step
    table[pl.ds(0, rows), :] = pb_ref.get()[...]
    table[pl.ds(rows, rows), :] = po_ref.get()[...]
    table[pl.ds(2 * rows, rows), :] = pa_ref.get()[...]
    table[pl.ds(3 * rows, reach - 3 * rows), :] = jnp.zeros((reach - 3 * rows, width), BF)
    table[pl.ds(first, rows), :] = pd_ref.get()[...]
    zsum[...] = jnp.zeros_like(zsum)
    for ref in (msrc_ref, mtgt_ref, we_ref, mel_ref):
        ref.get()

    def ahead(i, carry):
        at = pl.multiple_of(i * step, step)
        src = columns(msrc_ref.get()[pl.ds(i, 1), :])
        tgt = columns(mtgt_ref.get()[pl.ds(i, 1), :] + first)
        src = jnp.concatenate([src] * (reach // LANE), axis=1)
        tgt = jnp.concatenate([tgt] * (reach // LANE), axis=1)
        lane = lax.broadcasted_iota(I32, (step, reach), 1).astype(F32)
        chosen = jnp.where((src == lane) | (tgt == lane), 1.0, 0.0).astype(BF)
        hot[pl.ds(at, step), :] = chosen
        pre = dot(mel_ref.get()[pl.ds(at, step), :], we_ref.get()[...]) + dot(chosen, table[...])
        act, grad = silu_pair(pre)
        sg[pl.ds(at, step), :] = grad.astype(BF)
        zsum[...] += dot_lt(chosen[:, first:], act.astype(BF))
        return carry

    lax.fori_loop(0, steps, ahead, 0)
    zeta = zsum[pl.ds(0, rows), :].astype(BF)
    h0 = h0_ref.get()[...]
    cot = cot_ref.get()[...]
    agg = dot(zeta, wpo_ref.get()[...]).astype(BF)
    pre_node = dot(h0, wns_ref.get()[...]) + dot(agg, wna_ref.get()[...])
    act, grad = silu_pair(pre_node)
    unit = act.astype(BF)
    out_ref.buffer[...] = (h0.astype(F32) + dot(unit, wno_ref.get()[...])).astype(BF)
    out_ref.send()
    gno_ref.buffer[...] = (dot_lt(unit, cot) * node_scale).astype(BF)
    gno_ref.send()
    d_node = (dot_rt(cot, wno_ref.get()[...]) * grad).astype(BF)
    gns_ref.buffer[...] = (dot_lt(h0, d_node) * node_scale).astype(BF)
    gns_ref.send()
    gna_ref.buffer[...] = (dot_lt(agg, d_node) * node_scale).astype(BF)
    gna_ref.send()
    d_agg = dot_rt(d_node, wna_ref.get()[...]).astype(BF)
    gpo_ref.buffer[...] = (dot_lt(zeta, d_agg) * proc_scale).astype(BF)
    gpo_ref.send()
    d_zeta = dot_rt(d_agg, wpo_ref.get()[...]).astype(BF)
    mg_ref.buffer[...] = cot.astype(F32) + dot_rt(d_node, wns_ref.get()[...])
    back[...] = jnp.zeros_like(back)
    gacc[...] = jnp.zeros_like(gacc)
    table[pl.ds(first, rows), :] = d_zeta

    def behind(i, carry):
        at = pl.multiple_of(i * step, step)
        chosen = hot[pl.ds(at, step), :]
        d_edge = dot(chosen[:, first:], table[pl.ds(first, 256), :])
        d_proc = (d_edge * sg[pl.ds(at, step), :].astype(F32)).astype(BF)
        back[...] += dot_lt(chosen, d_proc)
        gacc[...] += dot_lt(mel_ref.get()[pl.ds(at, step), :], d_proc)
        return carry

    lax.fori_loop(0, steps, behind, 0)
    gpe_ref.buffer[...] = (gacc[...] * proc_scale).astype(BF)
    gpe_ref.send()
    sb_ref.buffer[...] = back[pl.ds(0, rows), :].astype(BF)
    so_ref.buffer[...] = back[pl.ds(rows, rows), :].astype(BF)
    sa_ref.buffer[...] = back[pl.ds(2 * rows, rows), :].astype(BF)
    sa_ref.send()
    sb_ref.send()
    so_ref.send()
    dst_sum = back[pl.ds(first, rows), :].astype(BF)
    mg_ref.buffer[...] += dot_rt(dst_sum, wdst_ref.get()[...])
    gpd_ref.buffer[...] = (dot_lt(h0, dst_sum) * proc_scale).astype(BF)


def split_halves(core, held, layout, kept_ref, sent_ref):
    first, groups, half = layout
    width = kept_ref.shape[1]
    even = core == 0
    step = 16

    def piece(row):
        ref = held[row // width] if row < 10 * width else None
        return jnp.zeros((step, width), BF) if ref is None else ref[pl.ds(row % width, step), :]

    for group in range(groups):
        for part in range(0, half, step):
            row = (first + group) * 2 * half + part
            at = pl.ds(group * half + part, step)
            left, right = piece(row), piece(row + half)
            kept_ref[at, :] = jnp.where(even, left, right)
            sent_ref[at, :] = jnp.where(even, right, left)


def mesh_backward(
    scales, layout, core_ref, so_ref, sb_ref, sa_ref, wsrc_ref, mg_ref, wout_ref, pick_ref, h0_ref,
    a0_ref, gpe_ref, gpd_ref, gpo_ref, gns_ref, gna_ref, gno_ref,
    out_ref, ret_ref, kept_ref, sent_ref, padded, geo, gps,
):
    proc_scale, enc_scale = scales
    rows = h0_ref.buffer.shape[0]
    total = sum(ref.get()[...].astype(F32) for ref in (so_ref, sb_ref, sa_ref)).astype(BF)
    grad = mg_ref.get()[...] + dot_rt(total, wsrc_ref.get()[...])
    out_ref.buffer[...] = grad
    out_ref.send()
    d_mesh = grad.astype(BF)
    padded[pl.ds(rows, 256 - rows), :] = jnp.zeros((256 - rows, padded.shape[1]), BF)
    padded[pl.ds(0, rows), :] = dot_rt(d_mesh, wout_ref.get()[...]).astype(BF)
    step = 256
    for at in range(0, ret_ref.buffer.shape[0], step):
        ret_ref.buffer[pl.ds(at, step), :] = dot(pick_ref.get()[pl.ds(at, step), :], padded[...]).astype(BF)
    ret_ref.send()
    gps[...] = (dot_lt(h0_ref.get()[...], total) * proc_scale).astype(BF)
    geo[...] = (dot_lt(a0_ref.get()[...], d_mesh) * enc_scale).astype(BF)
    held = [None, None, geo, gpe_ref.get(), gps, gpd_ref.get()] + [
        ref.get() for ref in (gpo_ref, gns_ref, gna_ref, gno_ref)
    ]
    split_halves(core_ref[0], held, layout, kept_ref.buffer, sent_ref.buffer)


def enc_backward(
    enc_scale, layout, core_ref, slot_ref, src_ref, ret_ref, sg_ref, edge_ref, grid_ref, wg_ref,
    out_ref, kept_ref, sent_ref, gee, geg,
):
    chosen = same(columns(slot_ref.get()[...]), ret_ref.buffer.shape[0])
    d_enc = (dot(chosen, ret_ref.get()[...]) * sg_ref.get()[...].astype(F32)).astype(BF)
    gee[...] = (dot_lt(edge_ref.get()[...], d_enc) * enc_scale).astype(BF)
    grid_sum = dot(same_t(src_ref.get()[...], grid_ref.buffer.shape[0]), d_enc).astype(BF)
    geg[...] = (dot_lt(grid_ref.get()[...], grid_sum) * enc_scale).astype(BF)
    out_ref.buffer[...] = dot_rt(grid_sum, wg_ref.get()[...])
    out_ref.send()
    split_halves(core_ref[0], [gee, geg] + [None] * 8, layout, kept_ref.buffer, sent_ref.buffer)


def add_halves(chunk, turn_ref, kept_ref, came_ref, out_ref):
    narrow, length, width = out_ref.buffer.shape
    blocks = turn_ref.buffer.shape[0]
    step = blocks // narrow
    skip = length - kept_ref.buffer.shape[0] // narrow
    if skip:
        for y in range(narrow):
            out_ref.buffer[y, pl.ds(0, skip), :] = jnp.zeros((skip, width), BF)
    for at in range(0, kept_ref.buffer.shape[0], blocks):
        total = kept_ref.get()[pl.ds(at, blocks), :].astype(F32) + came_ref.get()[pl.ds(at, blocks), :].astype(F32)
        total = total.astype(BF)
        if step > chunk:
            total = dot(turn_ref.get()[...], total).astype(BF)
        for y in range(narrow):
            out_ref.buffer[y, pl.ds(skip + at // narrow, step), :] = total[y * step : (y + 1) * step]


def turned(narrow, chunk, groups):
    rows = np.arange(groups * narrow * chunk).reshape(groups, narrow, chunk)
    rows = rows.transpose(1, 0, 2).reshape(-1)
    return jnp.asarray(rows[:, None] == np.arange(rows.size)[None, :], BF)


class Inward:
    def __init__(self, source, buffer, sem):
        self.copy = pltpu.make_async_copy(source, buffer, sem)
        self.copy.start()
        self.buffer = buffer
        self.waited = False

    def get(self):
        if not self.waited:
            self.copy.wait()
            self.waited = True
        return self.buffer


class Outward:
    def __init__(self, buffer, target, sem):
        self.copy = pltpu.make_async_copy(buffer, target, sem)
        self.buffer = buffer
        self.started = False

    def send(self):
        self.copy.start()
        self.started = True

    def finish(self):
        if not self.started:
            self.send()
        self.copy.wait()


def call(body, ins, outs, scratch=(), limit=16, scalar=None):
    count, made, extra = len(ins), len(outs), int(scalar is not None)

    def kernel(*refs):
        lead, refs = refs[:extra], refs[extra:]
        source, target, refs = refs[:count], refs[count : count + made], refs[count + made :]
        here, there, refs = refs[:count], refs[count : count + made], refs[count + made :]
        in_sem, out_sem = refs[:2]
        got = [Inward(source[i], here[i], in_sem.at[i]) for i in range(count)]
        put = [Outward(there[i], target[i], out_sem.at[i]) for i in range(made)]
        body(*lead, *got, *put, *refs[2:])
        for one in got:
            one.get()
        for one in put:
            one.finish()

    hbm = pl.BlockSpec(memory_space=pl.ANY)
    return pl.pallas_call(
        kernel,
        in_specs=[pl.BlockSpec(memory_space=pltpu.SMEM)] * extra + [hbm] * count,
        out_specs=[hbm] * made,
        out_shape=[jax.ShapeDtypeStruct(shape, kind) for shape, kind in outs],
        scratch_shapes=[pltpu.VMEM(one.shape, one.dtype) for one in ins]
        + [pltpu.VMEM(shape, kind) for shape, kind in outs]
        + [pltpu.SemaphoreType.DMA((count,)), pltpu.SemaphoreType.DMA((made,))]
        + [pltpu.VMEM(shape, kind) for shape, kind in scratch],
        compiler_params=pltpu.CompilerParams(vmem_limit_bytes=limit << 20),
    )(*([scalar] * extra), *ins)


def on_device(
    grid_latent,
    enc_edge_latent,
    enc_source,
    enc_target_device,
    enc_target_row,
    mesh_static,
    mesh_edge_latent,
    mesh_source,
    mesh_target,
    w_enc_edge,
    w_enc_grid,
    w_enc_out,
    w_proc_edge,
    w_proc_src,
    w_proc_dst,
    w_proc_out,
    w_node_self,
    w_node_agg,
    w_node_out,
    cotangent,
):
    wide = lax.axis_size("wide")
    narrow = lax.axis_size("narrow")
    devices = wide * narrow
    edges, width = enc_edge_latent.shape
    grid_rows = grid_latent.shape[0]
    rows = mesh_static.shape[0]
    mesh_edges = mesh_source.shape[0]
    capacity = 2 * edges // devices
    slots = devices * capacity
    enc_scale = float(edges * devices) ** (-0.5)
    proc_scale = float(mesh_edges * devices) ** (-0.5)
    node_scale = float(rows * devices) ** (-0.5)
    core = lax.axis_index("wide") % 2

    source = enc_source.reshape(1, edges)
    payload, enc_sg, slot = call(
        functools.partial(enc_forward, capacity),
        [
            enc_target_device.reshape(1, edges),
            enc_target_row.reshape(1, edges),
            source,
            grid_latent,
            enc_edge_latent,
            w_enc_edge,
            w_enc_grid,
        ],
        [((slots, width + LANE), BF), ((edges, width), BF), ((1, edges), I32)],
    )
    received = lax.all_to_all(
        payload.reshape(devices, capacity, width + LANE),
        ("wide", "narrow"),
        split_axis=0,
        concat_axis=0,
        tiled=True,
    ).reshape(slots, width + LANE)
    h0, a0, p_src, p_dst, pick = call(
        mesh_forward,
        [received, w_enc_out, mesh_static, w_proc_src, w_proc_dst],
        [((rows, width), BF)] * 4 + [((slots, 256), BF)],
    )
    up = [(i, (i + 1) % wide) for i in range(wide)]
    down = [(j, i) for i, j in up]
    p_before = lax.ppermute(p_src, "wide", up)
    p_after = lax.ppermute(p_src, "wide", down)
    square = ((width, width), BF)
    block = ((rows, width), BF)
    reach = -(-3 * rows // LANE) * LANE + 256
    mesh_out, s_before, s_own, s_after, partial_grad, gpe, gpd, gpo, gns, gna, gno = call(
        functools.partial(processor, (proc_scale, node_scale)),
        [
            mesh_source.reshape(-1, 256),
            mesh_target.reshape(-1, 256),
            p_before,
            p_src,
            p_after,
            p_dst,
            w_proc_edge,
            mesh_edge_latent,
            w_proc_out,
            h0,
            w_node_self,
            w_node_agg,
            w_node_out,
            cotangent,
            w_proc_dst,
        ],
        [block] * 4 + [((rows, width), F32)] + [square] * 6,
        [
            ((reach, width), BF),
            ((mesh_edges, reach), BF),
            ((mesh_edges, width), BF),
            ((256, width), F32),
            ((reach, width), F32),
            ((width, width), F32),
        ],
        limit=32,
    )
    from_after = lax.ppermute(s_before, "wide", down)
    from_before = lax.ppermute(s_after, "wide", up)
    chips = wide // 2
    chunk = 10 * width // devices
    half = narrow * chunk
    late = 2 * width
    block = 4 if chunk % 16 else 1
    span = 2 * half * block
    late_layout = (0, -(-late // span) * block, half)
    early_layout = (late // span * block, chips - late // span * block, half)
    turn = turned(narrow, chunk, block)
    late_block = ((late_layout[1] * half, width), BF)
    early_block = ((early_layout[1] * half, width), BF)
    where = core.reshape(1)
    swap = [(i, i ^ 1) for i in range(wide)]
    mesh_grad, returning, kept, sent = call(
        functools.partial(mesh_backward, (proc_scale, enc_scale), early_layout),
        [s_own, from_after, from_before, w_proc_src, partial_grad, w_enc_out, pick, h0, a0]
        + [gpe, gpd, gpo, gns, gna, gno],
        [((rows, width), F32), ((slots, width), BF), early_block, early_block],
        [((256, width), BF), square, square],
        limit=24,
        scalar=where,
    )
    came = lax.ppermute(sent, "wide", swap)
    far = 4 if chips > 4 else 2
    near = chips // far
    line = [[i + j * 2 * near for j in range(far)] for i in range(2 * near)]
    plane = [[i * 2 * near + 2 * j + c for j in range(near)] for i in range(far) for c in range(2)]
    turning = functools.partial(add_halves, chunk)
    (early,) = call(turning, [turn, kept, came], [((narrow, chips * chunk, width), BF)])
    early = lax.psum_scatter(early, "narrow", scatter_dimension=0, tiled=True)
    early = lax.psum_scatter(
        early.reshape(far, near * chunk, width),
        "wide",
        scatter_dimension=0,
        tiled=True,
        axis_index_groups=line,
    ).reshape(near * chunk, width)
    returned = lax.all_to_all(
        returning.reshape(devices, capacity, width),
        ("wide", "narrow"),
        split_axis=0,
        concat_axis=0,
        tiled=True,
    ).reshape(slots, width)
    grid_grad, kept, sent = call(
        functools.partial(enc_backward, enc_scale, late_layout),
        [slot, source, returned, enc_sg, enc_edge_latent, grid_latent, w_enc_grid],
        [((grid_rows, width), F32), late_block, late_block],
        [square, square],
        limit=24,
        scalar=where,
    )
    came = lax.ppermute(sent, "wide", swap)
    spread = late_layout[1] * chunk
    (last,) = call(turning, [turn, kept, came], [((narrow, spread, width), BF)])
    last = lax.all_to_all(last, "narrow", split_axis=0, concat_axis=0, tiled=True)
    last = jnp.sum(last.astype(F32), axis=0).astype(BF)
    parts = [
        lax.ppermute(last, "wide", [(j * 2 * near + i, i) for i in range(2 * near)])
        for j in range(1, far)
    ]
    at_first = lax.axis_index("wide") < 2 * near
    last = jnp.where(at_first, last.astype(F32), 0.0) + sum(p.astype(F32) for p in parts)
    both = early.astype(F32) + last[: near * chunk]
    both = lax.all_to_all(
        both.astype(BF).reshape(near, chunk, width),
        "wide",
        split_axis=0,
        concat_axis=0,
        tiled=True,
        axis_index_groups=plane,
    )
    summed = jnp.sum(both.astype(F32), axis=0).reshape(-1)
    return (mesh_out, grid_grad, summed, mesh_grad)


def solution(mesh):
    in_specs = (
        P(("wide", "narrow"), None),
        P(("wide", "narrow"), None),
        P(("wide", "narrow")),
        P(("wide", "narrow"), None),
        P(("wide", "narrow")),
        P(("wide", "narrow"), None),
        P(("wide", "narrow"), None),
        P(("wide", "narrow")),
        P(("wide", "narrow")),
        P(),
        P(),
        P(),
        P(),
        P(),
        P(),
        P(),
        P(),
        P(),
        P(),
        P(("wide", "narrow"), None),
    )
    out_specs = (
        P(("wide", "narrow"), None),
        P(("wide", "narrow"), None),
        P(("wide", "narrow")),
        P(("wide", "narrow"), None),
    )
    return jax.shard_map(
        on_device, mesh=mesh, in_specs=in_specs, out_specs=out_specs, check_vma=False
    )
```

```python
import functools

import jax
import jax.numpy as jnp
import numpy as np
from jax import lax
from jax.experimental import pallas as pl
from jax.experimental.pallas import tpu as pltpu
from jax.sharding import PartitionSpec as P

BF = jnp.bfloat16
F32 = jnp.float32
I32 = jnp.int32
LANE = 128


def dot(left, right):
    return jnp.dot(left, right, preferred_element_type=F32)


def dot_rt(left, right):
    return lax.dot_general(left, right, (((1,), (1,)), ((), ())), preferred_element_type=F32)


def dot_lt(left, right):
    return lax.dot_general(left, right, (((0,), (0,)), ((), ())), preferred_element_type=F32)


def silu_pair(value):
    sig = jax.nn.sigmoid(value)
    act = value * sig
    return act, sig + act * (1.0 - sig)


def columns(row):
    return jnp.broadcast_to(row.astype(F32), (LANE, row.shape[1])).T


def same(cols, width, shift=0):
    wide = jnp.concatenate([cols] * (-(-width // LANE)), axis=1)
    lane = lax.broadcasted_iota(I32, wide.shape, 1) + shift
    return jnp.where(wide == lane.astype(F32), 1.0, 0.0).astype(BF)


def same_t(row, height, shift=0):
    sub = lax.broadcasted_iota(I32, (height, row.shape[1]), 0) + shift
    return jnp.where(sub == row, 1.0, 0.0).astype(BF)


def enc_forward(
    capacity, tdev_ref, trow_ref, src_ref, grid_ref, edge_ref, we_ref, wg_ref, out_ref, sg_ref, slot_ref
):
    edges, width = edge_ref.buffer.shape
    slots = out_ref.buffer.shape[0]
    tdev = tdev_ref.get()[...]
    member = same_t(tdev, slots // capacity)
    before = lax.broadcasted_iota(I32, (edges, edges), 0) < lax.broadcasted_iota(
        I32, (edges, edges), 1
    )
    ahead = dot(member, jnp.where(before, 1.0, 0.0).astype(BF))
    rank = jnp.sum(member.astype(F32) * ahead, axis=0, keepdims=True)
    slot = tdev * capacity + rank.astype(I32)
    slot_ref.buffer[...] = slot
    slot_ref.send()
    tag = columns(trow_ref.get()[...] + 1).astype(BF)
    grid = grid_ref.get()[...]
    gathered = dot(same(columns(src_ref.get()[...]), grid.shape[0]), grid).astype(BF)
    pre = dot(edge_ref.get()[...], we_ref.get()[...]) + dot(gathered, wg_ref.get()[...])
    act, grad = silu_pair(pre)
    sg_ref.buffer[...] = grad.astype(BF)
    sg_ref.send()
    payload = jnp.concatenate([act.astype(BF), tag], axis=1)
    step = 256
    for at in range(0, slots, step):
        place = same_t(slot, step, at)
        out_ref.buffer[pl.ds(at, step), :] = dot(place, payload).astype(BF)


def mesh_forward(
    recv_ref, wout_ref, static_ref, wsrc_ref, wdst_ref, h0_ref, a0_ref, psrc_ref, pdst_ref, pick_ref
):
    rows, width = static_ref.buffer.shape
    padded = pick_ref.buffer.shape[1]
    tag = recv_ref.get()[:, width:].astype(F32)
    pick = same(tag, padded, 1)
    pick_ref.buffer[...] = pick
    pick_ref.send()
    a0 = dot_lt(pick, recv_ref.get()[:, :width])[:rows].astype(BF)
    a0_ref.buffer[...] = a0
    h0 = (static_ref.get()[...].astype(F32) + dot(a0, wout_ref.get()[...])).astype(BF)
    h0_ref.buffer[...] = h0
    psrc_ref.buffer[...] = dot(h0, wsrc_ref.get()[...]).astype(BF)
    pdst_ref.buffer[...] = dot(h0, wdst_ref.get()[...]).astype(BF)


def processor(
    scales,
    msrc_ref,
    mtgt_ref,
    pb_ref,
    po_ref,
    pa_ref,
    pd_ref,
    we_ref,
    mel_ref,
    wpo_ref,
    h0_ref,
    wns_ref,
    wna_ref,
    wno_ref,
    cot_ref,
    wdst_ref,
    out_ref,
    sb_ref,
    so_ref,
    sa_ref,
    mg_ref,
    gpe_ref,
    gpd_ref,
    gpo_ref,
    gns_ref,
    gna_ref,
    gno_ref,
    table,
    hot,
    sg,
    zsum,
    back,
    gacc,
):
    proc_scale, node_scale = scales
    edges, width = mel_ref.buffer.shape
    rows = h0_ref.buffer.shape[0]
    reach = table.shape[0]
    first = reach - 256
    step = 256
    steps = edges // step
    table[pl.ds(0, rows), :] = pb_ref.get()[...]
    table[pl.ds(rows, rows), :] = po_ref.get()[...]
    table[pl.ds(2 * rows, rows), :] = pa_ref.get()[...]
    table[pl.ds(3 * rows, reach - 3 * rows), :] = jnp.zeros((reach - 3 * rows, width), BF)
    table[pl.ds(first, rows), :] = pd_ref.get()[...]
    zsum[...] = jnp.zeros_like(zsum)
    for ref in (msrc_ref, mtgt_ref, we_ref, mel_ref):
        ref.get()

    def ahead(i, carry):
        at = pl.multiple_of(i * step, step)
        src = columns(msrc_ref.get()[pl.ds(i, 1), :])
        tgt = columns(mtgt_ref.get()[pl.ds(i, 1), :] + first)
        src = jnp.concatenate([src] * (reach // LANE), axis=1)
        tgt = jnp.concatenate([tgt] * (reach // LANE), axis=1)
        lane = lax.broadcasted_iota(I32, (step, reach), 1).astype(F32)
        chosen = jnp.where((src == lane) | (tgt == lane), 1.0, 0.0).astype(BF)
        hot[pl.ds(at, step), :] = chosen
        pre = dot(mel_ref.get()[pl.ds(at, step), :], we_ref.get()[...]) + dot(chosen, table[...])
        act, grad = silu_pair(pre)
        sg[pl.ds(at, step), :] = grad.astype(BF)
        zsum[...] += dot_lt(chosen[:, first:], act.astype(BF))
        return carry

    lax.fori_loop(0, steps, ahead, 0)
    zeta = zsum[pl.ds(0, rows), :].astype(BF)
    h0 = h0_ref.get()[...]
    cot = cot_ref.get()[...]
    agg = dot(zeta, wpo_ref.get()[...]).astype(BF)
    pre_node = dot(h0, wns_ref.get()[...]) + dot(agg, wna_ref.get()[...])
    act, grad = silu_pair(pre_node)
    unit = act.astype(BF)
    out_ref.buffer[...] = (h0.astype(F32) + dot(unit, wno_ref.get()[...])).astype(BF)
    out_ref.send()
    gno_ref.buffer[...] = (dot_lt(unit, cot) * node_scale).astype(BF)
    gno_ref.send()
    d_node = (dot_rt(cot, wno_ref.get()[...]) * grad).astype(BF)
    gns_ref.buffer[...] = (dot_lt(h0, d_node) * node_scale).astype(BF)
    gns_ref.send()
    gna_ref.buffer[...] = (dot_lt(agg, d_node) * node_scale).astype(BF)
    gna_ref.send()
    d_agg = dot_rt(d_node, wna_ref.get()[...]).astype(BF)
    gpo_ref.buffer[...] = (dot_lt(zeta, d_agg) * proc_scale).astype(BF)
    gpo_ref.send()
    d_zeta = dot_rt(d_agg, wpo_ref.get()[...]).astype(BF)
    mg_ref.buffer[...] = cot.astype(F32) + dot_rt(d_node, wns_ref.get()[...])
    back[...] = jnp.zeros_like(back)
    gacc[...] = jnp.zeros_like(gacc)
    table[pl.ds(first, rows), :] = d_zeta

    def behind(i, carry):
        at = pl.multiple_of(i * step, step)
        chosen = hot[pl.ds(at, step), :]
        d_edge = dot(chosen[:, first:], table[pl.ds(first, 256), :])
        d_proc = (d_edge * sg[pl.ds(at, step), :].astype(F32)).astype(BF)
        back[...] += dot_lt(chosen, d_proc)
        gacc[...] += dot_lt(mel_ref.get()[pl.ds(at, step), :], d_proc)
        return carry

    lax.fori_loop(0, steps, behind, 0)
    gpe_ref.buffer[...] = (gacc[...] * proc_scale).astype(BF)
    gpe_ref.send()
    sb_ref.buffer[...] = back[pl.ds(0, rows), :].astype(BF)
    so_ref.buffer[...] = back[pl.ds(rows, rows), :].astype(BF)
    sa_ref.buffer[...] = back[pl.ds(2 * rows, rows), :].astype(BF)
    sa_ref.send()
    sb_ref.send()
    so_ref.send()
    dst_sum = back[pl.ds(first, rows), :].astype(BF)
    mg_ref.buffer[...] += dot_rt(dst_sum, wdst_ref.get()[...])
    gpd_ref.buffer[...] = (dot_lt(h0, dst_sum) * proc_scale).astype(BF)


def split_halves(core, held, layout, kept_ref, sent_ref):
    first, groups, half = layout
    width = kept_ref.shape[1]
    even = core == 0
    step = 16

    def piece(row):
        ref = held[row // width] if row < 10 * width else None
        return jnp.zeros((step, width), BF) if ref is None else ref[pl.ds(row % width, step), :]

    for group in range(groups):
        for part in range(0, half, step):
            row = (first + group) * 2 * half + part
            at = pl.ds(group * half + part, step)
            left, right = piece(row), piece(row + half)
            kept_ref[at, :] = jnp.where(even, left, right)
            sent_ref[at, :] = jnp.where(even, right, left)


def mesh_backward(
    scales, layout, core_ref, so_ref, sb_ref, sa_ref, wsrc_ref, mg_ref, wout_ref, pick_ref, h0_ref,
    a0_ref, gpe_ref, gpd_ref, gpo_ref, gns_ref, gna_ref, gno_ref,
    out_ref, ret_ref, kept_ref, sent_ref, padded, geo, gps,
):
    proc_scale, enc_scale = scales
    rows = h0_ref.buffer.shape[0]
    total = sum(ref.get()[...].astype(F32) for ref in (so_ref, sb_ref, sa_ref)).astype(BF)
    grad = mg_ref.get()[...] + dot_rt(total, wsrc_ref.get()[...])
    out_ref.buffer[...] = grad
    out_ref.send()
    d_mesh = grad.astype(BF)
    padded[pl.ds(rows, 256 - rows), :] = jnp.zeros((256 - rows, padded.shape[1]), BF)
    padded[pl.ds(0, rows), :] = dot_rt(d_mesh, wout_ref.get()[...]).astype(BF)
    step = 256
    for at in range(0, ret_ref.buffer.shape[0], step):
        ret_ref.buffer[pl.ds(at, step), :] = dot(pick_ref.get()[pl.ds(at, step), :], padded[...]).astype(BF)
    ret_ref.send()
    gps[...] = (dot_lt(h0_ref.get()[...], total) * proc_scale).astype(BF)
    geo[...] = (dot_lt(a0_ref.get()[...], d_mesh) * enc_scale).astype(BF)
    held = [None, None, geo, gpe_ref.get(), gps, gpd_ref.get()] + [
        ref.get() for ref in (gpo_ref, gns_ref, gna_ref, gno_ref)
    ]
    split_halves(core_ref[0], held, layout, kept_ref.buffer, sent_ref.buffer)


def enc_backward(
    enc_scale, layout, core_ref, slot_ref, src_ref, ret_ref, sg_ref, edge_ref, grid_ref, wg_ref,
    out_ref, kept_ref, sent_ref, gee, geg,
):
    chosen = same(columns(slot_ref.get()[...]), ret_ref.buffer.shape[0])
    d_enc = (dot(chosen, ret_ref.get()[...]) * sg_ref.get()[...].astype(F32)).astype(BF)
    gee[...] = (dot_lt(edge_ref.get()[...], d_enc) * enc_scale).astype(BF)
    grid_sum = dot(same_t(src_ref.get()[...], grid_ref.buffer.shape[0]), d_enc).astype(BF)
    geg[...] = (dot_lt(grid_ref.get()[...], grid_sum) * enc_scale).astype(BF)
    out_ref.buffer[...] = dot_rt(grid_sum, wg_ref.get()[...])
    out_ref.send()
    split_halves(core_ref[0], [gee, geg] + [None] * 8, layout, kept_ref.buffer, sent_ref.buffer)


def add_halves(chunk, turn_ref, kept_ref, came_ref, out_ref):
    narrow, length, width = out_ref.buffer.shape
    blocks = turn_ref.buffer.shape[0]
    step = blocks // narrow
    skip = length - kept_ref.buffer.shape[0] // narrow
    if skip:
        for y in range(narrow):
            out_ref.buffer[y, pl.ds(0, skip), :] = jnp.zeros((skip, width), BF)
    for at in range(0, kept_ref.buffer.shape[0], blocks):
        total = kept_ref.get()[pl.ds(at, blocks), :].astype(F32) + came_ref.get()[pl.ds(at, blocks), :].astype(F32)
        total = total.astype(BF)
        if step > chunk:
            total = dot(turn_ref.get()[...], total).astype(BF)
        for y in range(narrow):
            out_ref.buffer[y, pl.ds(skip + at // narrow, step), :] = total[y * step : (y + 1) * step]


def turned(narrow, chunk, groups):
    rows = np.arange(groups * narrow * chunk).reshape(groups, narrow, chunk)
    rows = rows.transpose(1, 0, 2).reshape(-1)
    return jnp.asarray(rows[:, None] == np.arange(rows.size)[None, :], BF)


class Inward:
    def __init__(self, source, buffer, sem):
        self.copy = pltpu.make_async_copy(source, buffer, sem)
        self.copy.start()
        self.buffer = buffer
        self.waited = False

    def get(self):
        if not self.waited:
            self.copy.wait()
            self.waited = True
        return self.buffer


class Outward:
    def __init__(self, buffer, target, sem):
        self.copy = pltpu.make_async_copy(buffer, target, sem)
        self.buffer = buffer
        self.started = False

    def send(self):
        self.copy.start()
        self.started = True

    def finish(self):
        if not self.started:
            self.send()
        self.copy.wait()


def call(body, ins, outs, scratch=(), scalar=None):
    count, made, extra = len(ins), len(outs), int(scalar is not None)

    def kernel(*refs):
        lead, refs = refs[:extra], refs[extra:]
        source, target, refs = refs[:count], refs[count : count + made], refs[count + made :]
        here, there, refs = refs[:count], refs[count : count + made], refs[count + made :]
        in_sem, out_sem = refs[:2]
        got = [Inward(source[i], here[i], in_sem.at[i]) for i in range(count)]
        put = [Outward(there[i], target[i], out_sem.at[i]) for i in range(made)]
        body(*lead, *got, *put, *refs[2:])
        for one in got:
            one.get()
        for one in put:
            one.finish()

    hbm = pl.BlockSpec(memory_space=pl.ANY)
    return pl.pallas_call(
        kernel,
        in_specs=[pl.BlockSpec(memory_space=pltpu.SMEM)] * extra + [hbm] * count,
        out_specs=[hbm] * made,
        out_shape=[jax.ShapeDtypeStruct(shape, kind) for shape, kind in outs],
        scratch_shapes=[pltpu.VMEM(one.shape, one.dtype) for one in ins]
        + [pltpu.VMEM(shape, kind) for shape, kind in outs]
        + [pltpu.SemaphoreType.DMA((count,)), pltpu.SemaphoreType.DMA((made,))]
        + [pltpu.VMEM(shape, kind) for shape, kind in scratch],
        compiler_params=pltpu.CompilerParams(vmem_limit_bytes=60 << 20),
    )(*([scalar] * extra), *ins)


def on_device(
    grid_latent,
    enc_edge_latent,
    enc_source,
    enc_target_device,
    enc_target_row,
    mesh_static,
    mesh_edge_latent,
    mesh_source,
    mesh_target,
    w_enc_edge,
    w_enc_grid,
    w_enc_out,
    w_proc_edge,
    w_proc_src,
    w_proc_dst,
    w_proc_out,
    w_node_self,
    w_node_agg,
    w_node_out,
    cotangent,
):
    wide = lax.axis_size("wide")
    narrow = lax.axis_size("narrow")
    devices = wide * narrow
    edges, width = enc_edge_latent.shape
    grid_rows = grid_latent.shape[0]
    rows = mesh_static.shape[0]
    mesh_edges = mesh_source.shape[0]
    capacity = 2 * edges // devices
    slots = devices * capacity
    enc_scale = float(edges * devices) ** (-0.5)
    proc_scale = float(mesh_edges * devices) ** (-0.5)
    node_scale = float(rows * devices) ** (-0.5)
    core = lax.axis_index("wide") % 2

    source = enc_source.reshape(1, edges)
    payload, enc_sg, slot = call(
        functools.partial(enc_forward, capacity),
        [
            enc_target_device.reshape(1, edges),
            enc_target_row.reshape(1, edges),
            source,
            grid_latent,
            enc_edge_latent,
            w_enc_edge,
            w_enc_grid,
        ],
        [((slots, width + LANE), BF), ((edges, width), BF), ((1, edges), I32)],
    )
    received = lax.all_to_all(
        payload.reshape(devices, capacity, width + LANE),
        ("wide", "narrow"),
        split_axis=0,
        concat_axis=0,
        tiled=True,
    ).reshape(slots, width + LANE)
    h0, a0, p_src, p_dst, pick = call(
        mesh_forward,
        [received, w_enc_out, mesh_static, w_proc_src, w_proc_dst],
        [((rows, width), BF)] * 4 + [((slots, 256), BF)],
    )
    up = [(i, (i + 1) % wide) for i in range(wide)]
    down = [(j, i) for i, j in up]
    p_before = lax.ppermute(p_src, "wide", up)
    p_after = lax.ppermute(p_src, "wide", down)
    square = ((width, width), BF)
    block = ((rows, width), BF)
    reach = -(-3 * rows // LANE) * LANE + 256
    mesh_out, s_before, s_own, s_after, partial_grad, gpe, gpd, gpo, gns, gna, gno = call(
        functools.partial(processor, (proc_scale, node_scale)),
        [
            mesh_source.reshape(-1, 256),
            mesh_target.reshape(-1, 256),
            p_before,
            p_src,
            p_after,
            p_dst,
            w_proc_edge,
            mesh_edge_latent,
            w_proc_out,
            h0,
            w_node_self,
            w_node_agg,
            w_node_out,
            cotangent,
            w_proc_dst,
        ],
        [block] * 4 + [((rows, width), F32)] + [square] * 6,
        [
            ((reach, width), BF),
            ((mesh_edges, reach), BF),
            ((mesh_edges, width), BF),
            ((256, width), F32),
            ((reach, width), F32),
            ((width, width), F32),
        ],
    )
    from_after = lax.ppermute(s_before, "wide", down)
    from_before = lax.ppermute(s_after, "wide", up)
    chips = wide // 2
    chunk = 10 * width // devices
    half = narrow * chunk
    late = 2 * width
    block = 4 if chunk % 16 else 1
    span = 2 * half * block
    late_layout = (0, -(-late // span) * block, half)
    early_layout = (late // span * block, chips - late // span * block, half)
    turn = turned(narrow, chunk, block)
    late_block = ((late_layout[1] * half, width), BF)
    early_block = ((early_layout[1] * half, width), BF)
    where = core.reshape(1)
    swap = [(i, i ^ 1) for i in range(wide)]
    mesh_grad, returning, kept, sent = call(
        functools.partial(mesh_backward, (proc_scale, enc_scale), early_layout),
        [s_own, from_after, from_before, w_proc_src, partial_grad, w_enc_out, pick, h0, a0]
        + [gpe, gpd, gpo, gns, gna, gno],
        [((rows, width), F32), ((slots, width), BF), early_block, early_block],
        [((256, width), BF), square, square],
        scalar=where,
    )
    came = lax.ppermute(sent, "wide", swap)
    far = 4 if chips > 4 else 2
    near = chips // far
    line = [[i + j * 2 * near for j in range(far)] for i in range(2 * near)]
    plane = [[i * 2 * near + 2 * j + c for j in range(near)] for i in range(far) for c in range(2)]
    turning = functools.partial(add_halves, chunk)
    (early,) = call(turning, [turn, kept, came], [((narrow, chips * chunk, width), BF)])
    early = lax.psum_scatter(early, "narrow", scatter_dimension=0, tiled=True)
    early = lax.psum_scatter(
        early.reshape(far, near * chunk, width),
        "wide",
        scatter_dimension=0,
        tiled=True,
        axis_index_groups=line,
    ).reshape(near * chunk, width)
    returned = lax.all_to_all(
        returning.reshape(devices, capacity, width),
        ("wide", "narrow"),
        split_axis=0,
        concat_axis=0,
        tiled=True,
    ).reshape(slots, width)
    grid_grad, kept, sent = call(
        functools.partial(enc_backward, enc_scale, late_layout),
        [slot, source, returned, enc_sg, enc_edge_latent, grid_latent, w_enc_grid],
        [((grid_rows, width), F32), late_block, late_block],
        [square, square],
        scalar=where,
    )
    came = lax.ppermute(sent, "wide", swap)
    spread = late_layout[1] * chunk
    (last,) = call(turning, [turn, kept, came], [((narrow, spread, width), BF)])
    last = lax.all_to_all(last, "narrow", split_axis=0, concat_axis=0, tiled=True)
    last = jnp.sum(last.astype(F32), axis=0).astype(BF)
    parts = [
        lax.ppermute(last, "wide", [(j * 2 * near + i, i) for i in range(2 * near)])
        for j in range(1, far)
    ]
    at_first = lax.axis_index("wide") < 2 * near
    last = jnp.where(at_first, last.astype(F32), 0.0) + sum(p.astype(F32) for p in parts)
    both = early.astype(F32) + last[: near * chunk]
    both = lax.all_to_all(
        both.astype(BF).reshape(near, chunk, width),
        "wide",
        split_axis=0,
        concat_axis=0,
        tiled=True,
        axis_index_groups=plane,
    )
    summed = jnp.sum(both.astype(F32), axis=0).reshape(-1)
    return (mesh_out, grid_grad, summed, mesh_grad)


def solution(mesh):
    in_specs = (
        P(("wide", "narrow"), None),
        P(("wide", "narrow"), None),
        P(("wide", "narrow")),
        P(("wide", "narrow"), None),
        P(("wide", "narrow")),
        P(("wide", "narrow"), None),
        P(("wide", "narrow"), None),
        P(("wide", "narrow")),
        P(("wide", "narrow")),
        P(),
        P(),
        P(),
        P(),
        P(),
        P(),
        P(),
        P(),
        P(),
        P(),
        P(("wide", "narrow"), None),
    )
    out_specs = (
        P(("wide", "narrow"), None),
        P(("wide", "narrow"), None),
        P(("wide", "narrow")),
        P(("wide", "narrow"), None),
    )
    return jax.shard_map(
        on_device, mesh=mesh, in_specs=in_specs, out_specs=out_specs, check_vma=False
    )
```

```python
import functools

import jax
import jax.numpy as jnp
import numpy as np
from jax import lax
from jax.experimental import pallas as pl
from jax.experimental.pallas import tpu as pltpu
from jax.sharding import PartitionSpec as P

BF = jnp.bfloat16
F32 = jnp.float32
I32 = jnp.int32
LANE = 128


def dot(left, right):
    return jnp.dot(left, right, preferred_element_type=F32)


def dot_rt(left, right):
    return lax.dot_general(left, right, (((1,), (1,)), ((), ())), preferred_element_type=F32)


def dot_lt(left, right):
    return lax.dot_general(left, right, (((0,), (0,)), ((), ())), preferred_element_type=F32)


def silu_pair(value):
    sig = jax.nn.sigmoid(value)
    act = value * sig
    return act, sig + act * (1.0 - sig)


def columns(row):
    return jnp.broadcast_to(row.astype(F32), (LANE, row.shape[1])).T


def same(cols, width, shift=0):
    wide = jnp.concatenate([cols] * (-(-width // LANE)), axis=1)
    lane = lax.broadcasted_iota(I32, wide.shape, 1) + shift
    return jnp.where(wide == lane.astype(F32), 1.0, 0.0).astype(BF)


def same_t(row, height, shift=0):
    sub = lax.broadcasted_iota(I32, (height, row.shape[1]), 0) + shift
    return jnp.where(sub == row, 1.0, 0.0).astype(BF)


def enc_forward(
    capacity, tdev_ref, trow_ref, src_ref, grid_ref, edge_ref, we_ref, wg_ref, out_ref, sg_ref, slot_ref
):
    edges, width = edge_ref.buffer.shape
    slots = out_ref.buffer.shape[0]
    tdev = tdev_ref.get()[...]
    member = same_t(tdev, slots // capacity)
    before = lax.broadcasted_iota(I32, (edges, edges), 0) < lax.broadcasted_iota(
        I32, (edges, edges), 1
    )
    ahead = dot(member, jnp.where(before, 1.0, 0.0).astype(BF))
    rank = jnp.sum(member.astype(F32) * ahead, axis=0, keepdims=True)
    slot = tdev * capacity + rank.astype(I32)
    slot_ref.buffer[...] = slot
    slot_ref.send()
    tag = columns(trow_ref.get()[...] + 1).astype(BF)
    grid = grid_ref.get()[...]
    gathered = dot(same(columns(src_ref.get()[...]), grid.shape[0]), grid).astype(BF)
    pre = dot(edge_ref.get()[...], we_ref.get()[...]) + dot(gathered, wg_ref.get()[...])
    act, grad = silu_pair(pre)
    sg_ref.buffer[...] = grad.astype(BF)
    sg_ref.send()
    payload = jnp.concatenate([act.astype(BF), tag], axis=1)
    step = 256
    for at in range(0, slots, step):
        place = same_t(slot, step, at)
        out_ref.buffer[pl.ds(at, step), :] = dot(place, payload).astype(BF)


def mesh_forward(recv_ref, wout_ref, static_ref, wsrc_ref, h0_ref, a0_ref, psrc_ref):
    rows, width = static_ref.buffer.shape
    recv = recv_ref.get()
    pick = same(recv[:, width:].astype(F32), 256, 1)
    a0 = dot_lt(pick, recv[:, :width])[:rows].astype(BF)
    a0_ref.buffer[...] = a0
    a0_ref.send()
    h0 = (static_ref.get()[...].astype(F32) + dot(a0, wout_ref.get()[...])).astype(BF)
    h0_ref.buffer[...] = h0
    h0_ref.send()
    psrc_ref.buffer[...] = dot(h0, wsrc_ref.get()[...]).astype(BF)


def processor(
    proc_scale,
    msrc_ref,
    mtgt_ref,
    pb_ref,
    po_ref,
    pa_ref,
    h0_ref,
    wdst_ref,
    we_ref,
    mel_ref,
    wpo_ref,
    wns_ref,
    wna_ref,
    wno_ref,
    cot_ref,
    sb_ref,
    so_ref,
    sa_ref,
    dst_ref,
    unit_ref,
    dnode_ref,
    dagg_ref,
    agg_ref,
    zeta_ref,
    gpe_ref,
    table,
    hot,
    sg,
    zsum,
    back,
    gacc,
):
    edges, width = mel_ref.buffer.shape
    rows = h0_ref.buffer.shape[0]
    reach = table.shape[0]
    first = reach - 256
    step = 256
    steps = edges // step
    h0 = h0_ref.get()[...]
    table[pl.ds(3 * rows, reach - 3 * rows), :] = jnp.zeros((reach - 3 * rows, width), BF)
    table[pl.ds(first, rows), :] = dot(h0, wdst_ref.get()[...]).astype(BF)
    table[pl.ds(0, rows), :] = pb_ref.get()[...]
    table[pl.ds(rows, rows), :] = po_ref.get()[...]
    table[pl.ds(2 * rows, rows), :] = pa_ref.get()[...]
    zsum[...] = jnp.zeros_like(zsum)
    for ref in (msrc_ref, mtgt_ref, we_ref, mel_ref):
        ref.get()

    def ahead(i, carry):
        at = pl.multiple_of(i * step, step)
        src = columns(msrc_ref.buffer[pl.ds(i, 1), :])
        tgt = columns(mtgt_ref.buffer[pl.ds(i, 1), :] + first)
        src = jnp.concatenate([src] * (reach // LANE), axis=1)
        tgt = jnp.concatenate([tgt] * (reach // LANE), axis=1)
        lane = lax.broadcasted_iota(I32, (step, reach), 1).astype(F32)
        chosen = jnp.where((src == lane) | (tgt == lane), 1.0, 0.0).astype(BF)
        hot[pl.ds(at, step), :] = chosen
        pre = dot(mel_ref.buffer[pl.ds(at, step), :], we_ref.buffer[...])
        act, grad = silu_pair(pre + dot(chosen, table[...]))
        sg[pl.ds(at, step), :] = grad.astype(BF)
        zsum[...] += dot_lt(chosen[:, first:], act.astype(BF))
        return carry

    lax.fori_loop(0, steps, ahead, 0)
    zeta = zsum[pl.ds(0, rows), :].astype(BF)
    cot = cot_ref.get()[...]
    agg = dot(zeta, wpo_ref.get()[...]).astype(BF)
    pre_node = dot(h0, wns_ref.get()[...]) + dot(agg, wna_ref.get()[...])
    act, grad = silu_pair(pre_node)
    d_node = (dot_rt(cot, wno_ref.get()[...]) * grad).astype(BF)
    d_agg = dot_rt(d_node, wna_ref.get()[...]).astype(BF)
    table[pl.ds(first, rows), :] = dot_rt(d_agg, wpo_ref.get()[...]).astype(BF)
    for ref, value in (
        (unit_ref, act.astype(BF)),
        (dnode_ref, d_node),
        (dagg_ref, d_agg),
        (agg_ref, agg),
        (zeta_ref, zeta),
    ):
        ref.buffer[...] = value
        ref.send()
    back[...] = jnp.zeros_like(back)
    gacc[...] = jnp.zeros_like(gacc)

    def behind(i, carry):
        at = pl.multiple_of(i * step, step)
        chosen = hot[pl.ds(at, step), :]
        d_edge = dot(chosen[:, first:], table[pl.ds(first, 256), :])
        d_proc = (d_edge * sg[pl.ds(at, step), :].astype(F32)).astype(BF)
        back[...] += dot_lt(chosen, d_proc)
        gacc[...] += dot_lt(mel_ref.buffer[pl.ds(at, step), :], d_proc)
        return carry

    lax.fori_loop(0, steps, behind, 0)
    for ref, at in ((sa_ref, 2 * rows), (sb_ref, 0), (so_ref, rows), (dst_ref, first)):
        ref.buffer[...] = back[pl.ds(at, rows), :].astype(BF)
        ref.send()
    gpe_ref.buffer[...] = (gacc[...] * proc_scale).astype(BF)


def node_gradients(
    scales, h0_ref, unit_ref, wno_ref, cot_ref, dnode_ref, wns_ref, dagg_ref, agg_ref, zeta_ref,
    dst_ref, wdst_ref, turn_ref, out_ref, mg_ref, early_ref, gpd, gpo, gns, gna, gno,
):
    proc_scale, node_scale = scales
    h0 = h0_ref.get()[...]
    unit = unit_ref.get()[...]
    out_ref.buffer[...] = (h0.astype(F32) + dot(unit, wno_ref.get()[...])).astype(BF)
    out_ref.send()
    cot = cot_ref.get()[...]
    d_node = dnode_ref.get()[...]
    dst_sum = dst_ref.get()[...]
    mg_ref.buffer[...] = (
        cot.astype(F32) + dot_rt(d_node, wns_ref.get()[...]) + dot_rt(dst_sum, wdst_ref.get()[...])
    )
    mg_ref.send()
    gno[...] = (dot_lt(unit, cot) * node_scale).astype(BF)
    gns[...] = (dot_lt(h0, d_node) * node_scale).astype(BF)
    gna[...] = (dot_lt(agg_ref.get()[...], d_node) * node_scale).astype(BF)
    gpo[...] = (dot_lt(zeta_ref.get()[...], dagg_ref.get()[...]) * proc_scale).astype(BF)
    gpd[...] = (dot_lt(h0, dst_sum) * proc_scale).astype(BF)
    held = [None] * 5 + [gpd, gpo, gns, gna, gno]
    width = h0.shape[1]
    turn_rows(held, turn_ref.get()[...], 5 * width, 10 * width, early_ref.buffer)


def rows_of(held, start, count):
    width = next(ref for ref in held if ref is not None).shape[1]
    pieces = []
    while count:
        size = min(count, width - start % width)
        ref = held[start // width] if start < 10 * width else None
        pieces.append(
            jnp.zeros((size, width), BF) if ref is None else ref[pl.ds(start % width, size), :]
        )
        start, count = start + size, count - size
    return pieces[0] if len(pieces) == 1 else jnp.concatenate(pieces, axis=0)


def turn_rows(held, turn, start, stop, out):
    narrow = out.shape[0]
    block = turn.shape[0]
    slab = block // narrow
    for at in range(start, stop, block):
        value = dot(turn, rows_of(held, at, block)).astype(BF)
        for y in range(narrow):
            out[y, pl.ds((at - start) // narrow, slab), :] = value[y * slab : (y + 1) * slab]


def mesh_backward(
    scales, start, so_ref, sb_ref, sa_ref, wsrc_ref, mg_ref, wout_ref, tag_ref, h0_ref, a0_ref,
    gpe_ref, turn_ref, out_ref, ret_ref, early_ref, padded, geo, gps,
):
    proc_scale, enc_scale = scales
    rows, width = h0_ref.buffer.shape
    total = sum(ref.get()[...].astype(F32) for ref in (so_ref, sb_ref, sa_ref)).astype(BF)
    grad = mg_ref.get()[...] + dot_rt(total, wsrc_ref.get()[...])
    out_ref.buffer[...] = grad
    out_ref.send()
    d_mesh = grad.astype(BF)
    padded[pl.ds(rows, 256 - rows), :] = jnp.zeros((256 - rows, padded.shape[1]), BF)
    padded[pl.ds(0, rows), :] = dot_rt(d_mesh, wout_ref.get()[...]).astype(BF)
    tag = tag_ref.get()
    step = 256
    for at in range(0, ret_ref.buffer.shape[0], step):
        pick = same(tag[pl.ds(at, step), :].astype(F32), 256, 1)
        ret_ref.buffer[pl.ds(at, step), :] = dot(pick, padded[...]).astype(BF)
    ret_ref.send()
    gps[...] = (dot_lt(h0_ref.get()[...], total) * proc_scale).astype(BF)
    geo[...] = (dot_lt(a0_ref.get()[...], d_mesh) * enc_scale).astype(BF)
    held = [None, None, geo, gpe_ref.get(), gps] + [None] * 5
    turn_rows(held, turn_ref.get()[...], start, 5 * width, early_ref.buffer)


def enc_backward(
    enc_scale, half, core_ref, slot_ref, src_ref, ret_ref, sg_ref, edge_ref, grid_ref, turn_ref,
    wg_ref,
    out_ref, kept_ref, sent_ref, gee, geg,
):
    chosen = same(columns(slot_ref.get()[...]), ret_ref.buffer.shape[0])
    d_enc = (dot(chosen, ret_ref.get()[...]) * sg_ref.get()[...].astype(F32)).astype(BF)
    grid_sum = dot(same_t(src_ref.get()[...], grid_ref.buffer.shape[0]), d_enc).astype(BF)
    out_ref.buffer[...] = dot_rt(grid_sum, wg_ref.get()[...])
    out_ref.send()
    gee[...] = (dot_lt(edge_ref.get()[...], d_enc) * enc_scale).astype(BF)
    geg[...] = (dot_lt(grid_ref.get()[...], grid_sum) * enc_scale).astype(BF)
    held = [gee, geg] + [None] * 8
    even = core_ref[0] == 0
    turn = turn_ref.get()[...]
    narrow, length, _ = kept_ref.buffer.shape
    block = turn.shape[0]
    slab = block // narrow
    for at in range(0, length, slab):
        both = []
        for c in range(2):
            lead = range(2 * at * narrow, 2 * (at + slab) * narrow, 2 * half)
            rows = [rows_of(held, row + c * half, half) for row in lead]
            both.append(dot(turn, jnp.concatenate(rows, axis=0)).astype(BF))
        own, other = jnp.where(even, both[0], both[1]), jnp.where(even, both[1], both[0])
        for y in range(narrow):
            kept_ref.buffer[y, pl.ds(at, slab), :] = own[y * slab : (y + 1) * slab]
            sent_ref.buffer[y, pl.ds(at, slab), :] = other[y * slab : (y + 1) * slab]


def turned(narrow, chunk, groups):
    rows = np.arange(groups * narrow * chunk).reshape(groups, narrow, chunk)
    rows = rows.transpose(1, 0, 2).reshape(-1)
    return jnp.asarray(rows[:, None] == np.arange(rows.size)[None, :], BF)


class Inward:
    def __init__(self, source, buffer, sem):
        self.copy = pltpu.make_async_copy(source, buffer, sem)
        self.copy.start()
        self.buffer = buffer
        self.waited = False

    def get(self):
        if not self.waited:
            self.copy.wait()
            self.waited = True
        return self.buffer


class Outward:
    def __init__(self, buffer, target, sem):
        self.copy = pltpu.make_async_copy(buffer, target, sem)
        self.buffer = buffer
        self.started = False

    def send(self):
        self.copy.start()
        self.started = True

    def finish(self):
        if not self.started:
            self.send()
        self.copy.wait()


def call(body, ins, outs, scratch=(), scalar=None, cut=None, place=None, alias=None, flops=0):
    cut, place = cut or {}, place or {}
    extra, more = int(scalar is not None), int(alias is not None)
    count, made = len(ins), len(outs)
    held_in = [(one.shape[0], cut[i][1]) if i in cut else one.shape for i, one in enumerate(ins)]
    held_out = [
        (shape[0], place[i][1], shape[2]) if i in place else shape
        for i, (shape, _) in enumerate(outs)
    ]

    def kernel(*refs):
        lead, refs = refs[:extra], refs[extra:]
        source, refs = refs[:count], refs[count + more :]
        target, refs = refs[:made], refs[made:]
        here, there, refs = refs[:count], refs[count : count + made], refs[count + made :]
        in_sem, out_sem = refs[:2]
        got, put = [], []
        for i in range(count):
            part = source[i].at[:, pl.ds(*cut[i])] if i in cut else source[i]
            got.append(Inward(part, here[i], in_sem.at[i]))
        for i in range(made):
            part = target[i].at[:, pl.ds(*place[i]), :] if i in place else target[i]
            put.append(Outward(there[i], part, out_sem.at[i]))
        body(*lead, *got, *put, *refs[2:])
        for one in got:
            one.get()
        for one in put:
            one.finish()

    hbm = pl.BlockSpec(memory_space=pl.ANY)
    moved = sum(one.size * one.dtype.itemsize for one in ins)
    return pl.pallas_call(
        kernel,
        in_specs=[pl.BlockSpec(memory_space=pltpu.SMEM)] * extra + [hbm] * (count + more),
        out_specs=[hbm] * made,
        out_shape=[jax.ShapeDtypeStruct(shape, kind) for shape, kind in outs],
        scratch_shapes=[pltpu.VMEM(held_in[i], ins[i].dtype) for i in range(count)]
        + [pltpu.VMEM(held_out[i], outs[i][1]) for i in range(made)]
        + [pltpu.SemaphoreType.DMA((count,)), pltpu.SemaphoreType.DMA((made,))]
        + [pltpu.VMEM(shape, kind) for shape, kind in scratch],
        input_output_aliases={extra + count: next(iter(place))} if more else {},
        compiler_params=pltpu.CompilerParams(vmem_limit_bytes=60 << 20),
        cost_estimate=pl.CostEstimate(flops=flops, bytes_accessed=moved, transcendentals=0),
    )(*([scalar] * extra), *ins, *([alias] * more))


def on_device(
    grid_latent,
    enc_edge_latent,
    enc_source,
    enc_target_device,
    enc_target_row,
    mesh_static,
    mesh_edge_latent,
    mesh_source,
    mesh_target,
    w_enc_edge,
    w_enc_grid,
    w_enc_out,
    w_proc_edge,
    w_proc_src,
    w_proc_dst,
    w_proc_out,
    w_node_self,
    w_node_agg,
    w_node_out,
    cotangent,
):
    wide = lax.axis_size("wide")
    narrow = lax.axis_size("narrow")
    devices = wide * narrow
    edges, width = enc_edge_latent.shape
    grid_rows = grid_latent.shape[0]
    rows = mesh_static.shape[0]
    mesh_edges = mesh_source.shape[0]
    capacity = 2 * edges // devices
    slots = devices * capacity
    enc_scale = float(edges * devices) ** (-0.5)
    proc_scale = float(mesh_edges * devices) ** (-0.5)
    node_scale = float(rows * devices) ** (-0.5)
    core = lax.axis_index("wide") % 2

    source = enc_source.reshape(1, edges)
    payload, enc_sg, slot = call(
        functools.partial(enc_forward, capacity),
        [
            enc_target_device.reshape(1, edges),
            enc_target_row.reshape(1, edges),
            source,
            grid_latent,
            enc_edge_latent,
            w_enc_edge,
            w_enc_grid,
        ],
        [((slots, width + LANE), BF), ((edges, width), BF), ((1, edges), I32)],
    )
    received = lax.all_to_all(
        payload.reshape(devices, capacity, width + LANE),
        ("wide", "narrow"),
        split_axis=0,
        concat_axis=0,
        tiled=True,
    ).reshape(slots, width + LANE)
    h0, a0, p_src = call(
        mesh_forward,
        [received, w_enc_out, mesh_static, w_proc_src],
        [((rows, width), BF)] * 3,
    )
    up = [(i, (i + 1) % wide) for i in range(wide)]
    down = [(j, i) for i, j in up]
    p_before = lax.ppermute(p_src, "wide", up)
    p_after = lax.ppermute(p_src, "wide", down)
    square = ((width, width), BF)
    block = ((rows, width), BF)
    reach = -(-3 * rows // LANE) * LANE + 256
    s_before, s_own, s_after, dst_sum, unit, d_node, d_agg, agg, zeta, gpe = call(
        functools.partial(processor, proc_scale),
        [
            mesh_source.reshape(-1, 256),
            mesh_target.reshape(-1, 256),
            p_before,
            p_src,
            p_after,
            h0,
            w_proc_dst,
            w_proc_edge,
            mesh_edge_latent,
            w_proc_out,
            w_node_self,
            w_node_agg,
            w_node_out,
            cotangent,
        ],
        [block] * 9 + [square],
        [
            ((reach, width), BF),
            ((mesh_edges, reach), BF),
            ((mesh_edges, width), BF),
            ((256, width), F32),
            ((reach, width), F32),
            ((width, width), F32),
        ],
        flops=12 * mesh_edges * width * width,
    )
    from_after = lax.ppermute(s_before, "wide", down)
    from_before = lax.ppermute(s_after, "wide", up)

    chips = wide // 2
    chunk = 10 * width // devices
    half = narrow * chunk
    far = 4 if chips > 4 else 2
    near = chips // far
    small = chunk % 16 != 0
    turn = turned(narrow, chunk, 4 if small else 2)
    late_turn = turned(narrow, chunk, 4 if small else 1)
    late = 2 * width
    start = late // turn.shape[0] * turn.shape[0]
    length = (10 * width - start) // narrow
    split = (5 * width - start) // narrow
    early_shape = ((narrow, length, width), BF)
    mesh_out, partial_grad, early = call(
        functools.partial(node_gradients, (proc_scale, node_scale)),
        [h0, unit, w_node_out, cotangent, d_node, w_node_self, d_agg, agg, zeta]
        + [dst_sum, w_proc_dst, turn],
        [block, ((rows, width), F32), early_shape],
        [square] * 5,
        place={2: (split, length - split)},
        flops=24 * rows * width * width,
    )
    mesh_grad, returning, early = call(
        functools.partial(mesh_backward, (proc_scale, enc_scale), start),
        [s_own, from_after, from_before, w_proc_src, partial_grad, w_enc_out, received, h0, a0]
        + [gpe, turn],
        [((rows, width), F32), ((slots, width), BF), early_shape],
        [((256, width), BF), square, square],
        cut={6: (width, LANE)},
        place={2: (0, split)},
        alias=early,
        flops=12 * rows * width * width,
    )
    line = [[i + j * 2 * near for j in range(far)] for i in range(2 * near)]
    plane = [[i * 2 * near + j for j in range(2 * near)] for i in range(far)]
    early = lax.psum_scatter(early, "narrow", scatter_dimension=0, tiled=True)
    early = jnp.pad(early.reshape(length, width), ((start // narrow, 0), (0, 0)))
    early = lax.psum_scatter(
        early.reshape(far, near * 2 * chunk, width),
        "wide",
        scatter_dimension=0,
        tiled=True,
        axis_index_groups=line,
    )
    returned = lax.all_to_all(
        returning.reshape(devices, capacity, width),
        ("wide", "narrow"),
        split_axis=0,
        concat_axis=0,
        tiled=True,
    ).reshape(slots, width)
    spread = -(-late // (2 * late_turn.shape[0])) * late_turn.shape[0] // narrow
    late_shape = ((narrow, spread, width), BF)
    grid_grad, kept, sent = call(
        functools.partial(enc_backward, enc_scale, half),
        [slot, source, returned, enc_sg, enc_edge_latent, grid_latent, late_turn, w_enc_grid],
        [((grid_rows, width), F32), late_shape, late_shape],
        [square, square],
        scalar=core.reshape(1),
        flops=8 * edges * width * width,
    )
    came = lax.ppermute(sent, "wide", [(i, i ^ 1) for i in range(wide)])
    last = (kept.astype(F32) + came.astype(F32)).astype(BF)
    last = lax.all_to_all(last, "narrow", split_axis=0, concat_axis=0, tiled=True)
    last = jnp.sum(last.astype(F32), axis=0).astype(BF)
    parts = [
        lax.ppermute(last, "wide", [(j * 2 * near + i, i) for i in range(2 * near)])
        for j in range(1, far)
    ]
    at_first = lax.axis_index("wide") < 2 * near
    last = jnp.where(at_first, last.astype(F32), 0.0) + sum(p.astype(F32) for p in parts)
    last = last[: near * chunk].reshape(near, 1, chunk, width)
    own = (jnp.arange(2) == core)[None, :, None, None]
    both = early.reshape(near, 2, chunk, width).astype(F32) + jnp.where(own, last, 0.0)
    both = lax.all_to_all(
        both.astype(BF).reshape(2 * near, chunk, width),
        "wide",
        split_axis=0,
        concat_axis=0,
        tiled=True,
        axis_index_groups=plane,
    )
    summed = jnp.sum(both.astype(F32), axis=0).reshape(-1)
    return (mesh_out, grid_grad, summed, mesh_grad)


def solution(mesh):
    in_specs = (
        P(("wide", "narrow"), None),
        P(("wide", "narrow"), None),
        P(("wide", "narrow")),
        P(("wide", "narrow"), None),
        P(("wide", "narrow")),
        P(("wide", "narrow"), None),
        P(("wide", "narrow"), None),
        P(("wide", "narrow")),
        P(("wide", "narrow")),
        P(),
        P(),
        P(),
        P(),
        P(),
        P(),
        P(),
        P(),
        P(),
        P(),
        P(("wide", "narrow"), None),
    )
    out_specs = (
        P(("wide", "narrow"), None),
        P(("wide", "narrow"), None),
        P(("wide", "narrow")),
        P(("wide", "narrow"), None),
    )
    return jax.shard_map(
        on_device, mesh=mesh, in_specs=in_specs, out_specs=out_specs, check_vma=False
    )
```

```python
import functools

import jax
import jax.numpy as jnp
import numpy as np
from jax import lax
from jax.experimental import pallas as pl
from jax.experimental.pallas import tpu as pltpu
from jax.sharding import PartitionSpec as P

BF = jnp.bfloat16
F32 = jnp.float32
I32 = jnp.int32
LANE = 128


def dot(left, right):
    return jnp.dot(left, right, preferred_element_type=F32)


def dot_rt(left, right):
    return lax.dot_general(left, right, (((1,), (1,)), ((), ())), preferred_element_type=F32)


def dot_lt(left, right):
    return lax.dot_general(left, right, (((0,), (0,)), ((), ())), preferred_element_type=F32)


def silu_pair(value):
    sig = jax.nn.sigmoid(value)
    act = value * sig
    return act, sig + act * (1.0 - sig)


def columns(row):
    return jnp.broadcast_to(row.astype(F32), (LANE, row.shape[1])).T


def same(cols, width, shift=0):
    wide = jnp.concatenate([cols] * (-(-width // LANE)), axis=1)
    lane = lax.broadcasted_iota(I32, wide.shape, 1) + shift
    return jnp.where(wide == lane.astype(F32), 1.0, 0.0).astype(BF)


def same_t(row, height, shift=0):
    sub = lax.broadcasted_iota(I32, (height, row.shape[1]), 0) + shift
    return jnp.where(sub == row, 1.0, 0.0).astype(BF)


def enc_forward(
    capacity, tdev_ref, trow_ref, src_ref, grid_ref, edge_ref, we_ref, wg_ref, out_ref, sg_ref, slot_ref
):
    edges, width = edge_ref.buffer.shape
    slots = out_ref.buffer.shape[0]
    tdev = tdev_ref.get()[...]
    member = same_t(tdev, slots // capacity)
    before = lax.broadcasted_iota(I32, (edges, edges), 0) < lax.broadcasted_iota(
        I32, (edges, edges), 1
    )
    ahead = dot(member, jnp.where(before, 1.0, 0.0).astype(BF))
    rank = jnp.sum(member.astype(F32) * ahead, axis=0, keepdims=True)
    slot = tdev * capacity + rank.astype(I32)
    slot_ref.buffer[...] = slot
    slot_ref.send()
    tag = columns(trow_ref.get()[...] + 1).astype(BF)
    grid = grid_ref.get()[...]
    gathered = dot(same(columns(src_ref.get()[...]), grid.shape[0]), grid).astype(BF)
    pre = dot(edge_ref.get()[...], we_ref.get()[...]) + dot(gathered, wg_ref.get()[...])
    act, grad = silu_pair(pre)
    sg_ref.buffer[...] = grad.astype(BF)
    sg_ref.send()
    payload = jnp.concatenate([act.astype(BF), tag], axis=1)
    step = 256
    for at in range(0, slots, step):
        place = same_t(slot, step, at)
        out_ref.buffer[pl.ds(at, step), :] = dot(place, payload).astype(BF)


def mesh_forward(recv_ref, wout_ref, static_ref, wsrc_ref, h0_ref, a0_ref, psrc_ref):
    rows, width = static_ref.buffer.shape
    recv = recv_ref.get()
    pick = same(recv[:, width:].astype(F32), 256, 1)
    a0 = dot_lt(pick, recv[:, :width])[:rows].astype(BF)
    a0_ref.buffer[...] = a0
    a0_ref.send()
    h0 = (static_ref.get()[...].astype(F32) + dot(a0, wout_ref.get()[...])).astype(BF)
    h0_ref.buffer[...] = h0
    h0_ref.send()
    psrc_ref.buffer[...] = dot(h0, wsrc_ref.get()[...]).astype(BF)


def processor(
    proc_scale,
    msrc_ref,
    mtgt_ref,
    pb_ref,
    po_ref,
    pa_ref,
    h0_ref,
    wdst_ref,
    we_ref,
    mel_ref,
    wpo_ref,
    wns_ref,
    wna_ref,
    wno_ref,
    cot_ref,
    sb_ref,
    so_ref,
    sa_ref,
    dst_ref,
    unit_ref,
    dnode_ref,
    dagg_ref,
    agg_ref,
    zeta_ref,
    gpe_ref,
    table,
    hot,
    sg,
    zsum,
    back,
    gacc,
):
    edges, width = mel_ref.buffer.shape
    rows = h0_ref.buffer.shape[0]
    reach = table.shape[0]
    first = reach - 256
    step = 256
    steps = edges // step
    h0 = h0_ref.get()[...]
    table[pl.ds(3 * rows, reach - 3 * rows), :] = jnp.zeros((reach - 3 * rows, width), BF)
    table[pl.ds(first, rows), :] = dot(h0, wdst_ref.get()[...]).astype(BF)
    table[pl.ds(0, rows), :] = pb_ref.get()[...]
    table[pl.ds(rows, rows), :] = po_ref.get()[...]
    table[pl.ds(2 * rows, rows), :] = pa_ref.get()[...]
    zsum[...] = jnp.zeros_like(zsum)
    for ref in (msrc_ref, mtgt_ref, we_ref, mel_ref):
        ref.get()

    def ahead(i, carry):
        at = pl.multiple_of(i * step, step)
        src = columns(msrc_ref.buffer[pl.ds(i, 1), :])
        tgt = columns(mtgt_ref.buffer[pl.ds(i, 1), :] + first)
        src = jnp.concatenate([src] * (reach // LANE), axis=1)
        tgt = jnp.concatenate([tgt] * (reach // LANE), axis=1)
        lane = lax.broadcasted_iota(I32, (step, reach), 1).astype(F32)
        chosen = jnp.where((src == lane) | (tgt == lane), 1.0, 0.0).astype(BF)
        hot[pl.ds(at, step), :] = chosen
        pre = dot(mel_ref.buffer[pl.ds(at, step), :], we_ref.buffer[...])
        act, grad = silu_pair(pre + dot(chosen, table[...]))
        sg[pl.ds(at, step), :] = grad.astype(BF)
        zsum[...] += dot_lt(chosen[:, first:], act.astype(BF))
        return carry

    lax.fori_loop(0, steps, ahead, 0)
    zeta = zsum[pl.ds(0, rows), :].astype(BF)
    cot = cot_ref.get()[...]
    agg = dot(zeta, wpo_ref.get()[...]).astype(BF)
    pre_node = dot(h0, wns_ref.get()[...]) + dot(agg, wna_ref.get()[...])
    act, grad = silu_pair(pre_node)
    d_node = (dot_rt(cot, wno_ref.get()[...]) * grad).astype(BF)
    d_agg = dot_rt(d_node, wna_ref.get()[...]).astype(BF)
    table[pl.ds(first, rows), :] = dot_rt(d_agg, wpo_ref.get()[...]).astype(BF)
    for ref, value in (
        (unit_ref, act.astype(BF)),
        (dnode_ref, d_node),
        (dagg_ref, d_agg),
        (agg_ref, agg),
        (zeta_ref, zeta),
    ):
        ref.buffer[...] = value
        ref.send()
    back[...] = jnp.zeros_like(back)
    gacc[...] = jnp.zeros_like(gacc)

    def behind(i, carry):
        at = pl.multiple_of(i * step, step)
        chosen = hot[pl.ds(at, step), :]
        d_edge = dot(chosen[:, first:], table[pl.ds(first, 256), :])
        d_proc = (d_edge * sg[pl.ds(at, step), :].astype(F32)).astype(BF)
        back[...] += dot_lt(chosen, d_proc)
        gacc[...] += dot_lt(mel_ref.buffer[pl.ds(at, step), :], d_proc)
        return carry

    lax.fori_loop(0, steps, behind, 0)
    for ref, at in ((sa_ref, 2 * rows), (sb_ref, 0), (so_ref, rows), (dst_ref, first)):
        ref.buffer[...] = back[pl.ds(at, rows), :].astype(BF)
        ref.send()
    gpe_ref.buffer[...] = (gacc[...] * proc_scale).astype(BF)


def rows_of(held, start, count):
    width = next(ref for ref in held if ref is not None).shape[1]
    pieces = []
    while count:
        size = min(count, width - start % width)
        ref = held[start // width] if start < 10 * width else None
        pieces.append(
            jnp.zeros((size, width), BF) if ref is None else ref[pl.ds(start % width, size), :]
        )
        start, count = start + size, count - size
    return pieces[0] if len(pieces) == 1 else jnp.concatenate(pieces, axis=0)


def split_turned(held, turn, core, start, half, kept, sent):
    even = core == 0
    narrow, length, _ = kept.shape
    slab = turn.shape[0] // narrow
    for at in range(0, length, slab):
        both = []
        for c in range(2):
            lead = range(start + 2 * at * narrow, start + 2 * (at + slab) * narrow, 2 * half)
            rows = [rows_of(held, row + c * half, half) for row in lead]
            rows = rows[0] if len(rows) == 1 else jnp.concatenate(rows, axis=0)
            both.append(dot(turn, rows).astype(BF))
        own, other = jnp.where(even, both[0], both[1]), jnp.where(even, both[1], both[0])
        for y in range(narrow):
            kept[y, pl.ds(at, slab), :] = own[y * slab : (y + 1) * slab]
            sent[y, pl.ds(at, slab), :] = other[y * slab : (y + 1) * slab]


def mesh_backward(
    so_ref, sb_ref, sa_ref, wsrc_ref, dnode_ref, wns_ref, dst_ref, wdst_ref, cot_ref, wout_ref,
    tag_ref, out_ref, ret_ref, total_ref, dmesh_ref, padded,
):
    rows = so_ref.buffer.shape[0]
    total = sum(ref.get()[...].astype(F32) for ref in (so_ref, sb_ref, sa_ref)).astype(BF)
    total_ref.buffer[...] = total
    total_ref.send()
    grad = cot_ref.get()[...].astype(F32) + dot_rt(dnode_ref.get()[...], wns_ref.get()[...])
    grad += dot_rt(dst_ref.get()[...], wdst_ref.get()[...])
    grad += dot_rt(total, wsrc_ref.get()[...])
    out_ref.buffer[...] = grad
    out_ref.send()
    d_mesh = grad.astype(BF)
    dmesh_ref.buffer[...] = d_mesh
    dmesh_ref.send()
    padded[pl.ds(rows, 256 - rows), :] = jnp.zeros((256 - rows, padded.shape[1]), BF)
    padded[pl.ds(0, rows), :] = dot_rt(d_mesh, wout_ref.get()[...]).astype(BF)
    tag = tag_ref.get()
    step = 256
    for at in range(0, ret_ref.buffer.shape[0], step):
        pick = same(tag[pl.ds(at, step), :].astype(F32), 256, 1)
        ret_ref.buffer[pl.ds(at, step), :] = dot(pick, padded[...]).astype(BF)


def mesh_gradients(
    scales, start, half, core_ref, h0_ref, unit_ref, wno_ref, cot_ref, dnode_ref, dagg_ref, agg_ref,
    zeta_ref, dst_ref, total_ref, a0_ref, dmesh_ref, gpe_ref, turn_ref,
    out_ref, kept_ref, sent_ref, geo, gps, gpd, gpo, gns, gna, gno,
):
    enc_scale, proc_scale, node_scale = scales
    h0 = h0_ref.get()[...]
    unit = unit_ref.get()[...]
    out_ref.buffer[...] = (h0.astype(F32) + dot(unit, wno_ref.get()[...])).astype(BF)
    out_ref.send()
    d_node = dnode_ref.get()[...]
    gno[...] = (dot_lt(unit, cot_ref.get()[...]) * node_scale).astype(BF)
    gns[...] = (dot_lt(h0, d_node) * node_scale).astype(BF)
    gna[...] = (dot_lt(agg_ref.get()[...], d_node) * node_scale).astype(BF)
    gpo[...] = (dot_lt(zeta_ref.get()[...], dagg_ref.get()[...]) * proc_scale).astype(BF)
    gpd[...] = (dot_lt(h0, dst_ref.get()[...]) * proc_scale).astype(BF)
    gps[...] = (dot_lt(h0, total_ref.get()[...]) * proc_scale).astype(BF)
    geo[...] = (dot_lt(a0_ref.get()[...], dmesh_ref.get()[...]) * enc_scale).astype(BF)
    held = [None, None, geo, gpe_ref.get(), gps, gpd, gpo, gns, gna, gno]
    turn = turn_ref.get()[...]
    split_turned(held, turn, core_ref[0], start, half, kept_ref.buffer, sent_ref.buffer)


def enc_backward(
    enc_scale, half, core_ref, slot_ref, src_ref, ret_ref, sg_ref, edge_ref, grid_ref, wg_ref,
    turn_ref, out_ref, kept_ref, sent_ref, gee, geg,
):
    chosen = same(columns(slot_ref.get()[...]), ret_ref.buffer.shape[0])
    d_enc = (dot(chosen, ret_ref.get()[...]) * sg_ref.get()[...].astype(F32)).astype(BF)
    grid_sum = dot(same_t(src_ref.get()[...], grid_ref.buffer.shape[0]), d_enc).astype(BF)
    out_ref.buffer[...] = dot_rt(grid_sum, wg_ref.get()[...])
    out_ref.send()
    gee[...] = (dot_lt(edge_ref.get()[...], d_enc) * enc_scale).astype(BF)
    geg[...] = (dot_lt(grid_ref.get()[...], grid_sum) * enc_scale).astype(BF)
    held = [gee, geg] + [None] * 8
    turn = turn_ref.get()[...]
    split_turned(held, turn, core_ref[0], 0, half, kept_ref.buffer, sent_ref.buffer)


def turned(narrow, chunk, groups):
    rows = np.arange(groups * narrow * chunk).reshape(groups, narrow, chunk)
    rows = rows.transpose(1, 0, 2).reshape(-1)
    return jnp.asarray(rows[:, None] == np.arange(rows.size)[None, :], BF)


class Inward:
    def __init__(self, source, buffer, sem):
        self.copy = pltpu.make_async_copy(source, buffer, sem)
        self.copy.start()
        self.buffer = buffer
        self.waited = False

    def get(self):
        if not self.waited:
            self.copy.wait()
            self.waited = True
        return self.buffer


class Outward:
    def __init__(self, buffer, target, sem):
        self.copy = pltpu.make_async_copy(buffer, target, sem)
        self.buffer = buffer
        self.started = False

    def send(self):
        self.copy.start()
        self.started = True

    def finish(self):
        if not self.started:
            self.send()
        self.copy.wait()


def call(body, ins, outs, scratch=(), scalar=None, cut=None, flops=0):
    cut = cut or {}
    extra = int(scalar is not None)
    count, made = len(ins), len(outs)
    held = [(one.shape[0], cut[i][1]) if i in cut else one.shape for i, one in enumerate(ins)]

    def kernel(*refs):
        lead, refs = refs[:extra], refs[extra:]
        source, target, refs = refs[:count], refs[count : count + made], refs[count + made :]
        here, there, refs = refs[:count], refs[count : count + made], refs[count + made :]
        in_sem, out_sem = refs[:2]
        got = []
        for i in range(count):
            part = source[i].at[:, pl.ds(*cut[i])] if i in cut else source[i]
            got.append(Inward(part, here[i], in_sem.at[i]))
        put = [Outward(there[i], target[i], out_sem.at[i]) for i in range(made)]
        body(*lead, *got, *put, *refs[2:])
        for one in got:
            one.get()
        for one in put:
            one.finish()

    hbm = pl.BlockSpec(memory_space=pl.ANY)
    moved = sum(one.size * one.dtype.itemsize for one in ins)
    return pl.pallas_call(
        kernel,
        in_specs=[pl.BlockSpec(memory_space=pltpu.SMEM)] * extra + [hbm] * count,
        out_specs=[hbm] * made,
        out_shape=[jax.ShapeDtypeStruct(shape, kind) for shape, kind in outs],
        scratch_shapes=[pltpu.VMEM(held[i], ins[i].dtype) for i in range(count)]
        + [pltpu.VMEM(shape, kind) for shape, kind in outs]
        + [pltpu.SemaphoreType.DMA((count,)), pltpu.SemaphoreType.DMA((made,))]
        + [pltpu.VMEM(shape, kind) for shape, kind in scratch],
        compiler_params=pltpu.CompilerParams(vmem_limit_bytes=60 << 20),
        cost_estimate=pl.CostEstimate(flops=flops, bytes_accessed=moved, transcendentals=0),
    )(*([scalar] * extra), *ins)


def on_device(
    grid_latent,
    enc_edge_latent,
    enc_source,
    enc_target_device,
    enc_target_row,
    mesh_static,
    mesh_edge_latent,
    mesh_source,
    mesh_target,
    w_enc_edge,
    w_enc_grid,
    w_enc_out,
    w_proc_edge,
    w_proc_src,
    w_proc_dst,
    w_proc_out,
    w_node_self,
    w_node_agg,
    w_node_out,
    cotangent,
):
    wide = lax.axis_size("wide")
    narrow = lax.axis_size("narrow")
    devices = wide * narrow
    edges, width = enc_edge_latent.shape
    grid_rows = grid_latent.shape[0]
    rows = mesh_static.shape[0]
    mesh_edges = mesh_source.shape[0]
    capacity = 2 * edges // devices
    slots = devices * capacity
    enc_scale = float(edges * devices) ** (-0.5)
    proc_scale = float(mesh_edges * devices) ** (-0.5)
    node_scale = float(rows * devices) ** (-0.5)
    core = lax.axis_index("wide") % 2

    source = enc_source.reshape(1, edges)
    payload, enc_sg, slot = call(
        functools.partial(enc_forward, capacity),
        [
            enc_target_device.reshape(1, edges),
            enc_target_row.reshape(1, edges),
            source,
            grid_latent,
            enc_edge_latent,
            w_enc_edge,
            w_enc_grid,
        ],
        [((slots, width + LANE), BF), ((edges, width), BF), ((1, edges), I32)],
    )
    received = lax.all_to_all(
        payload.reshape(devices, capacity, width + LANE),
        ("wide", "narrow"),
        split_axis=0,
        concat_axis=0,
        tiled=True,
    ).reshape(slots, width + LANE)
    h0, a0, p_src = call(
        mesh_forward,
        [received, w_enc_out, mesh_static, w_proc_src],
        [((rows, width), BF)] * 3,
    )
    up = [(i, (i + 1) % wide) for i in range(wide)]
    down = [(j, i) for i, j in up]
    p_before = lax.ppermute(p_src, "wide", up)
    p_after = lax.ppermute(p_src, "wide", down)
    square = ((width, width), BF)
    block = ((rows, width), BF)
    reach = -(-3 * rows // LANE) * LANE + 256
    s_before, s_own, s_after, dst_sum, unit, d_node, d_agg, agg, zeta, gpe = call(
        functools.partial(processor, proc_scale),
        [
            mesh_source.reshape(-1, 256),
            mesh_target.reshape(-1, 256),
            p_before,
            p_src,
            p_after,
            h0,
            w_proc_dst,
            w_proc_edge,
            mesh_edge_latent,
            w_proc_out,
            w_node_self,
            w_node_agg,
            w_node_out,
            cotangent,
        ],
        [block] * 9 + [square],
        [
            ((reach, width), BF),
            ((mesh_edges, reach), BF),
            ((mesh_edges, width), BF),
            ((256, width), F32),
            ((reach, width), F32),
            ((width, width), F32),
        ],
        flops=12 * mesh_edges * width * width,
    )
    from_after = lax.ppermute(s_before, "wide", down)
    from_before = lax.ppermute(s_after, "wide", up)

    mesh_grad, returning, total, d_mesh = call(
        mesh_backward,
        [s_own, from_after, from_before, w_proc_src, d_node, w_node_self, dst_sum, w_proc_dst]
        + [cotangent, w_enc_out, received],
        [((rows, width), F32), ((slots, width), BF), block, block],
        [((256, width), BF)],
        cut={10: (width, LANE)},
        flops=12 * rows * width * width,
    )

    chips = wide // 2
    chunk = 10 * width // devices
    half = narrow * chunk
    far = 4 if chips > 4 else 2
    near = chips // far
    turn = turned(narrow, chunk, 4 if chunk % 16 else 1)
    late = 2 * width
    start = late // (2 * turn.shape[0]) * 2 * turn.shape[0]
    scales = (enc_scale, proc_scale, node_scale)
    early_shape = ((narrow, (10 * width - start) // (2 * narrow), width), BF)
    swap = [(i, i ^ 1) for i in range(wide)]
    mesh_out, kept, sent = call(
        functools.partial(mesh_gradients, scales, start, half),
        [h0, unit, w_node_out, cotangent, d_node, d_agg, agg, zeta, dst_sum, total, a0, d_mesh]
        + [gpe, turn],
        [block, early_shape, early_shape],
        [square] * 7,
        scalar=core.reshape(1),
        flops=32 * rows * width * width,
    )
    came = lax.ppermute(sent, "wide", swap)
    early = (kept.astype(F32) + came.astype(F32)).astype(BF)
    early = lax.psum_scatter(early, "narrow", scatter_dimension=0, tiled=True)
    returned = lax.all_to_all(
        returning.reshape(devices, capacity, width),
        ("wide", "narrow"),
        split_axis=0,
        concat_axis=0,
        tiled=True,
    ).reshape(slots, width)
    spread = -(-late // (2 * turn.shape[0])) * turn.shape[0] // narrow
    late_shape = ((narrow, spread, width), BF)
    grid_grad, kept, sent = call(
        functools.partial(enc_backward, enc_scale, half),
        [slot, source, returned, enc_sg, enc_edge_latent, grid_latent, w_enc_grid, turn],
        [((grid_rows, width), F32), late_shape, late_shape],
        [square, square],
        scalar=core.reshape(1),
        flops=8 * edges * width * width,
    )
    came = lax.ppermute(sent, "wide", swap)
    last = (kept.astype(F32) + came.astype(F32)).astype(BF)
    last = lax.all_to_all(last, "narrow", split_axis=0, concat_axis=0, tiled=True)
    last = jnp.sum(last.astype(F32), axis=0)[: near * chunk]
    early = jnp.pad(early[0], ((start // (2 * narrow), 0), (0, 0)))
    early = early.reshape(far, near * chunk, width)
    x = lax.axis_index("wide") // (2 * near)

    def toward(j):
        to = lax.rem(x + j, far)
        part = lax.dynamic_index_in_dim(early, to, 0, keepdims=False).astype(F32)
        return (part + jnp.where(to == 0, last, 0.0)).astype(BF)

    both = toward(0).astype(F32)
    for j in range(1, far):
        ring = [(i, (i + j * 2 * near) % wide) for i in range(wide)]
        both += lax.ppermute(toward(j), "wide", ring).astype(F32)
    both = lax.all_to_all(
        both.astype(BF).reshape(near, chunk, width),
        "wide",
        split_axis=0,
        concat_axis=0,
        tiled=True,
        axis_index_groups=[
            [i * 2 * near + 2 * j + c for j in range(near)] for i in range(far) for c in range(2)
        ],
    )
    summed = jnp.sum(both.astype(F32), axis=0).reshape(-1)
    return (mesh_out, grid_grad, summed, mesh_grad)


def solution(mesh):
    in_specs = (
        P(("wide", "narrow"), None),
        P(("wide", "narrow"), None),
        P(("wide", "narrow")),
        P(("wide", "narrow"), None),
        P(("wide", "narrow")),
        P(("wide", "narrow"), None),
        P(("wide", "narrow"), None),
        P(("wide", "narrow")),
        P(("wide", "narrow")),
        P(),
        P(),
        P(),
        P(),
        P(),
        P(),
        P(),
        P(),
        P(),
        P(),
        P(("wide", "narrow"), None),
    )
    out_specs = (
        P(("wide", "narrow"), None),
        P(("wide", "narrow"), None),
        P(("wide", "narrow")),
        P(("wide", "narrow"), None),
    )
    return jax.shard_map(
        on_device, mesh=mesh, in_specs=in_specs, out_specs=out_specs, check_vma=False
    )
```

```python
import functools

import jax
import jax.numpy as jnp
import numpy as np
from jax import lax
from jax.experimental import pallas as pl
from jax.experimental.pallas import tpu as pltpu
from jax.sharding import PartitionSpec as P

BF = jnp.bfloat16
F32 = jnp.float32
I32 = jnp.int32
LANE = 128


def dot(left, right):
    return jnp.dot(left, right, preferred_element_type=F32)


def dot_rt(left, right):
    return lax.dot_general(left, right, (((1,), (1,)), ((), ())), preferred_element_type=F32)


def dot_lt(left, right):
    return lax.dot_general(left, right, (((0,), (0,)), ((), ())), preferred_element_type=F32)


def silu_pair(value):
    sig = jax.nn.sigmoid(value)
    act = value * sig
    return act, sig + act * (1.0 - sig)


def columns(row):
    return jnp.broadcast_to(row.astype(F32), (LANE, row.shape[1])).T


def same(cols, width, shift=0):
    wide = jnp.concatenate([cols] * (-(-width // LANE)), axis=1)
    lane = lax.broadcasted_iota(I32, wide.shape, 1) + shift
    return jnp.where(wide == lane.astype(F32), 1.0, 0.0).astype(BF)


def same_t(row, height, shift=0):
    sub = lax.broadcasted_iota(I32, (height, row.shape[1]), 0) + shift
    return jnp.where(sub == row, 1.0, 0.0).astype(BF)


def enc_forward(
    capacity, tdev_ref, trow_ref, src_ref, grid_ref, edge_ref, we_ref, wg_ref, out_ref, sg_ref, slot_ref
):
    edges, width = edge_ref.buffer.shape
    slots = out_ref.buffer.shape[0]
    tdev = tdev_ref.get()[...]
    member = same_t(tdev, slots // capacity)
    before = lax.broadcasted_iota(I32, (edges, edges), 0) < lax.broadcasted_iota(
        I32, (edges, edges), 1
    )
    ahead = dot(member, jnp.where(before, 1.0, 0.0).astype(BF))
    rank = jnp.sum(member.astype(F32) * ahead, axis=0, keepdims=True)
    slot = tdev * capacity + rank.astype(I32)
    slot_ref.buffer[...] = slot
    slot_ref.send()
    tag = columns(trow_ref.get()[...] + 1).astype(BF)
    grid = grid_ref.get()[...]
    gathered = dot(same(columns(src_ref.get()[...]), grid.shape[0]), grid).astype(BF)
    pre = dot(edge_ref.get()[...], we_ref.get()[...]) + dot(gathered, wg_ref.get()[...])
    act, grad = silu_pair(pre)
    sg_ref.buffer[...] = grad.astype(BF)
    sg_ref.send()
    payload = jnp.concatenate([act.astype(BF), tag], axis=1)
    step = 256
    for at in range(0, slots, step):
        place = same_t(slot, step, at)
        out_ref.buffer[pl.ds(at, step), :] = dot(place, payload).astype(BF)


def mesh_forward(recv_ref, wout_ref, static_ref, wsrc_ref, h0_ref, a0_ref, psrc_ref):
    rows, width = static_ref.buffer.shape
    recv = recv_ref.get()
    pick = same(recv[:, width:].astype(F32), 256, 1)
    a0 = dot_lt(pick, recv[:, :width])[:rows].astype(BF)
    a0_ref.buffer[...] = a0
    a0_ref.send()
    h0 = (static_ref.get()[...].astype(F32) + dot(a0, wout_ref.get()[...])).astype(BF)
    h0_ref.buffer[...] = h0
    h0_ref.send()
    psrc_ref.buffer[...] = dot(h0, wsrc_ref.get()[...]).astype(BF)


def processor(
    proc_scale,
    msrc_ref,
    mtgt_ref,
    pb_ref,
    po_ref,
    pa_ref,
    h0_ref,
    wdst_ref,
    we_ref,
    mel_ref,
    wpo_ref,
    wns_ref,
    wna_ref,
    wno_ref,
    cot_ref,
    sb_ref,
    so_ref,
    sa_ref,
    dst_ref,
    unit_ref,
    dnode_ref,
    dagg_ref,
    agg_ref,
    zeta_ref,
    gpe_ref,
    table,
    hot,
    sg,
    zsum,
    back,
    gacc,
):
    edges, width = mel_ref.buffer.shape
    rows = h0_ref.buffer.shape[0]
    reach = table.shape[0]
    first = reach - 256
    step = 256
    steps = edges // step
    h0 = h0_ref.get()[...]
    table[pl.ds(3 * rows, reach - 3 * rows), :] = jnp.zeros((reach - 3 * rows, width), BF)
    table[pl.ds(first, rows), :] = dot(h0, wdst_ref.get()[...]).astype(BF)
    table[pl.ds(0, rows), :] = pb_ref.get()[...]
    table[pl.ds(rows, rows), :] = po_ref.get()[...]
    table[pl.ds(2 * rows, rows), :] = pa_ref.get()[...]
    zsum[...] = jnp.zeros_like(zsum)
    for ref in (msrc_ref, mtgt_ref, we_ref, mel_ref):
        ref.get()

    def ahead(i, carry):
        at = pl.multiple_of(i * step, step)
        src = columns(msrc_ref.buffer[pl.ds(i, 1), :])
        tgt = columns(mtgt_ref.buffer[pl.ds(i, 1), :] + first)
        src = jnp.concatenate([src] * (reach // LANE), axis=1)
        tgt = jnp.concatenate([tgt] * (reach // LANE), axis=1)
        lane = lax.broadcasted_iota(I32, (step, reach), 1).astype(F32)
        chosen = jnp.where((src == lane) | (tgt == lane), 1.0, 0.0).astype(BF)
        hot[pl.ds(at, step), :] = chosen
        pre = dot(mel_ref.buffer[pl.ds(at, step), :], we_ref.buffer[...])
        act, grad = silu_pair(pre + dot(chosen, table[...]))
        sg[pl.ds(at, step), :] = grad.astype(BF)
        zsum[...] += dot_lt(chosen[:, first:], act.astype(BF))
        return carry

    lax.fori_loop(0, steps, ahead, 0)
    zeta = zsum[pl.ds(0, rows), :].astype(BF)
    cot = cot_ref.get()[...]
    agg = dot(zeta, wpo_ref.get()[...]).astype(BF)
    pre_node = dot(h0, wns_ref.get()[...]) + dot(agg, wna_ref.get()[...])
    act, grad = silu_pair(pre_node)
    d_node = (dot_rt(cot, wno_ref.get()[...]) * grad).astype(BF)
    d_agg = dot_rt(d_node, wna_ref.get()[...]).astype(BF)
    table[pl.ds(first, rows), :] = dot_rt(d_agg, wpo_ref.get()[...]).astype(BF)
    for ref, value in (
        (unit_ref, act.astype(BF)),
        (dnode_ref, d_node),
        (dagg_ref, d_agg),
        (agg_ref, agg),
        (zeta_ref, zeta),
    ):
        ref.buffer[...] = value
        ref.send()
    back[...] = jnp.zeros_like(back)
    gacc[...] = jnp.zeros_like(gacc)

    def behind(i, carry):
        at = pl.multiple_of(i * step, step)
        chosen = hot[pl.ds(at, step), :]
        d_edge = dot(chosen[:, first:], table[pl.ds(first, 256), :])
        d_proc = (d_edge * sg[pl.ds(at, step), :].astype(F32)).astype(BF)
        back[...] += dot_lt(chosen, d_proc)
        gacc[...] += dot_lt(mel_ref.buffer[pl.ds(at, step), :], d_proc)
        return carry

    lax.fori_loop(0, steps, behind, 0)
    for ref, at in ((sa_ref, 2 * rows), (sb_ref, 0), (so_ref, rows), (dst_ref, first)):
        ref.buffer[...] = back[pl.ds(at, rows), :].astype(BF)
        ref.send()
    gpe_ref.buffer[...] = (gacc[...] * proc_scale).astype(BF)


def rows_of(held, start, count):
    width = next(ref for ref in held if ref is not None).shape[1]
    pieces = []
    while count:
        size = min(count, width - start % width)
        ref = held[start // width] if start < 10 * width else None
        pieces.append(
            jnp.zeros((size, width), BF) if ref is None else ref[pl.ds(start % width, size), :]
        )
        start, count = start + size, count - size
    return pieces[0] if len(pieces) == 1 else jnp.concatenate(pieces, axis=0)


def split_turned(held, turn, core, start, half, kept, sent):
    even = core == 0
    narrow, length, _ = kept.shape
    slab = turn.shape[0] // narrow
    for at in range(0, length, slab):
        both = []
        for c in range(2):
            lead = range(start + 2 * at * narrow, start + 2 * (at + slab) * narrow, 2 * half)
            rows = [rows_of(held, row + c * half, half) for row in lead]
            rows = rows[0] if len(rows) == 1 else jnp.concatenate(rows, axis=0)
            both.append(dot(turn, rows).astype(BF))
        own, other = jnp.where(even, both[0], both[1]), jnp.where(even, both[1], both[0])
        for y in range(narrow):
            kept[y, pl.ds(at, slab), :] = own[y * slab : (y + 1) * slab]
            sent[y, pl.ds(at, slab), :] = other[y * slab : (y + 1) * slab]


def turn_cores(held, turn, start, half, out):
    narrow = out.buffer.shape[0]
    slab = turn.shape[0] // narrow
    span = 2 * turn.shape[0]
    width = out.buffer.shape[3]
    first = start // span * span
    skip = (start - first) // (2 * narrow)
    leads = [*range(first + span, 10 * width, span), first]
    for k, lead in enumerate(leads):
        low = skip if lead == first else 0
        for c in range(2):
            rows = [rows_of(held, row + c * half, half) for row in range(lead, lead + span, 2 * half)]
            rows = rows[0] if len(rows) == 1 else jnp.concatenate(rows, axis=0)
            value = dot(turn, rows)
            for y in range(narrow):
                piece = value[y * slab + low : (y + 1) * slab]
                out.buffer[y, c, pl.ds(k * slab, slab - low), :] = piece.astype(BF)
    fill = out.buffer.shape[2] - len(leads) * slab + skip
    if fill:
        at = pl.ds(len(leads) * slab - skip, fill)
        out.buffer[:, :, at, :] = jnp.zeros((narrow, 2, fill, width), BF)


def mesh_backward(
    scales, start, half, so_ref, sb_ref, sa_ref, wsrc_ref, dnode_ref, wns_ref, dst_ref, wdst_ref,
    cot_ref, wout_ref, tag_ref, h0_ref, a0_ref, agg_ref, dagg_ref, zeta_ref, unit_ref, wno_ref,
    gpe_ref, turn_ref, out_ref, grad_ref, ret_ref, early_ref,
    padded, geo, gps, gpd, gpo, gns, gna, gno,
):
    enc_scale, proc_scale, node_scale = scales
    rows = so_ref.buffer.shape[0]
    total = sum(ref.get()[...].astype(F32) for ref in (so_ref, sb_ref, sa_ref)).astype(BF)
    d_node = dnode_ref.get()[...]
    dst_sum = dst_ref.get()[...]
    cot = cot_ref.get()[...]
    grad = cot.astype(F32) + dot_rt(d_node, wns_ref.get()[...])
    grad += dot_rt(dst_sum, wdst_ref.get()[...])
    grad += dot_rt(total, wsrc_ref.get()[...])
    grad_ref.buffer[...] = grad
    grad_ref.send()
    d_mesh = grad.astype(BF)
    padded[pl.ds(rows, 256 - rows), :] = jnp.zeros((256 - rows, padded.shape[1]), BF)
    padded[pl.ds(0, rows), :] = dot_rt(d_mesh, wout_ref.get()[...]).astype(BF)
    tag = tag_ref.get()
    step = 256
    for at in range(0, ret_ref.buffer.shape[0], step):
        pick = same(tag[pl.ds(at, step), :].astype(F32), 256, 1)
        ret_ref.buffer[pl.ds(at, step), :] = dot(pick, padded[...]).astype(BF)
    ret_ref.send()
    h0 = h0_ref.get()[...]
    gps[...] = (dot_lt(h0, total) * proc_scale).astype(BF)
    geo[...] = (dot_lt(a0_ref.get()[...], d_mesh) * enc_scale).astype(BF)
    gns[...] = (dot_lt(h0, d_node) * node_scale).astype(BF)
    gna[...] = (dot_lt(agg_ref.get()[...], d_node) * node_scale).astype(BF)
    gpd[...] = (dot_lt(h0, dst_sum) * proc_scale).astype(BF)
    gpo[...] = (dot_lt(zeta_ref.get()[...], dagg_ref.get()[...]) * proc_scale).astype(BF)
    unit = unit_ref.get()[...]
    gno[...] = (dot_lt(unit, cot) * node_scale).astype(BF)
    out_ref.buffer[...] = (h0.astype(F32) + dot(unit, wno_ref.get()[...])).astype(BF)
    out_ref.send()
    held = [None, None, geo, gpe_ref.get(), gps, gpd, gpo, gns, gna, gno]
    turn_cores(held, turn_ref.get()[...], start, half, early_ref)


def enc_backward(
    enc_scale, half, core_ref, slot_ref, src_ref, ret_ref, sg_ref, edge_ref, grid_ref, wg_ref,
    turn_ref, out_ref, kept_ref, sent_ref, gee, geg,
):
    chosen = same(columns(slot_ref.get()[...]), ret_ref.buffer.shape[0])
    d_enc = (dot(chosen, ret_ref.get()[...]) * sg_ref.get()[...].astype(F32)).astype(BF)
    grid_sum = dot(same_t(src_ref.get()[...], grid_ref.buffer.shape[0]), d_enc).astype(BF)
    out_ref.buffer[...] = dot_rt(grid_sum, wg_ref.get()[...])
    out_ref.send()
    gee[...] = (dot_lt(edge_ref.get()[...], d_enc) * enc_scale).astype(BF)
    geg[...] = (dot_lt(grid_ref.get()[...], grid_sum) * enc_scale).astype(BF)
    held = [gee, geg] + [None] * 8
    turn = turn_ref.get()[...]
    split_turned(held, turn, core_ref[0], 0, half, kept_ref.buffer, sent_ref.buffer)


def turned(narrow, chunk, groups):
    rows = np.arange(groups * narrow * chunk).reshape(groups, narrow, chunk)
    rows = rows.transpose(1, 0, 2).reshape(-1)
    return jnp.asarray(rows[:, None] == np.arange(rows.size)[None, :], BF)


class Inward:
    def __init__(self, source, buffer, sem):
        self.copy = pltpu.make_async_copy(source, buffer, sem)
        self.copy.start()
        self.buffer = buffer
        self.waited = False

    def get(self):
        if not self.waited:
            self.copy.wait()
            self.waited = True
        return self.buffer


class Outward:
    def __init__(self, buffer, target, sem):
        self.copy = pltpu.make_async_copy(buffer, target, sem)
        self.buffer = buffer
        self.started = False

    def send(self):
        self.copy.start()
        self.started = True

    def finish(self):
        if not self.started:
            self.send()
        self.copy.wait()


def call(body, ins, outs, scratch=(), scalar=None, cut=None, flops=0):
    cut = cut or {}
    extra = int(scalar is not None)
    count, made = len(ins), len(outs)
    held = [(one.shape[0], cut[i][1]) if i in cut else one.shape for i, one in enumerate(ins)]

    def kernel(*refs):
        lead, refs = refs[:extra], refs[extra:]
        source, target, refs = refs[:count], refs[count : count + made], refs[count + made :]
        here, there, refs = refs[:count], refs[count : count + made], refs[count + made :]
        in_sem, out_sem = refs[:2]
        got = []
        for i in range(count):
            part = source[i].at[:, pl.ds(*cut[i])] if i in cut else source[i]
            got.append(Inward(part, here[i], in_sem.at[i]))
        put = [Outward(there[i], target[i], out_sem.at[i]) for i in range(made)]
        body(*lead, *got, *put, *refs[2:])
        for one in got:
            one.get()
        for one in put:
            one.finish()

    hbm = pl.BlockSpec(memory_space=pl.ANY)
    moved = sum(one.size * one.dtype.itemsize for one in ins)
    return pl.pallas_call(
        kernel,
        in_specs=[pl.BlockSpec(memory_space=pltpu.SMEM)] * extra + [hbm] * count,
        out_specs=[hbm] * made,
        out_shape=[jax.ShapeDtypeStruct(shape, kind) for shape, kind in outs],
        scratch_shapes=[pltpu.VMEM(held[i], ins[i].dtype) for i in range(count)]
        + [pltpu.VMEM(shape, kind) for shape, kind in outs]
        + [pltpu.SemaphoreType.DMA((count,)), pltpu.SemaphoreType.DMA((made,))]
        + [pltpu.VMEM(shape, kind) for shape, kind in scratch],
        compiler_params=pltpu.CompilerParams(vmem_limit_bytes=60 << 20),
        cost_estimate=pl.CostEstimate(flops=flops, bytes_accessed=moved, transcendentals=0),
    )(*([scalar] * extra), *ins)


def on_device(
    grid_latent,
    enc_edge_latent,
    enc_source,
    enc_target_device,
    enc_target_row,
    mesh_static,
    mesh_edge_latent,
    mesh_source,
    mesh_target,
    w_enc_edge,
    w_enc_grid,
    w_enc_out,
    w_proc_edge,
    w_proc_src,
    w_proc_dst,
    w_proc_out,
    w_node_self,
    w_node_agg,
    w_node_out,
    cotangent,
):
    wide = lax.axis_size("wide")
    narrow = lax.axis_size("narrow")
    devices = wide * narrow
    edges, width = enc_edge_latent.shape
    grid_rows = grid_latent.shape[0]
    rows = mesh_static.shape[0]
    mesh_edges = mesh_source.shape[0]
    capacity = 2 * edges // devices
    slots = devices * capacity
    enc_scale = float(edges * devices) ** (-0.5)
    proc_scale = float(mesh_edges * devices) ** (-0.5)
    node_scale = float(rows * devices) ** (-0.5)
    core = lax.axis_index("wide") % 2

    source = enc_source.reshape(1, edges)
    payload, enc_sg, slot = call(
        functools.partial(enc_forward, capacity),
        [
            enc_target_device.reshape(1, edges),
            enc_target_row.reshape(1, edges),
            source,
            grid_latent,
            enc_edge_latent,
            w_enc_edge,
            w_enc_grid,
        ],
        [((slots, width + LANE), BF), ((edges, width), BF), ((1, edges), I32)],
    )
    received = lax.all_to_all(
        payload.reshape(devices, capacity, width + LANE),
        ("wide", "narrow"),
        split_axis=0,
        concat_axis=0,
        tiled=True,
    ).reshape(slots, width + LANE)
    h0, a0, p_src = call(
        mesh_forward,
        [received, w_enc_out, mesh_static, w_proc_src],
        [((rows, width), BF)] * 3,
    )
    up = [(i, (i + 1) % wide) for i in range(wide)]
    down = [(j, i) for i, j in up]
    p_before = lax.ppermute(p_src, "wide", up)
    p_after = lax.ppermute(p_src, "wide", down)
    square = ((width, width), BF)
    block = ((rows, width), BF)
    reach = -(-3 * rows // LANE) * LANE + 256
    s_before, s_own, s_after, dst_sum, unit, d_node, d_agg, agg, zeta, gpe = call(
        functools.partial(processor, proc_scale),
        [
            mesh_source.reshape(-1, 256),
            mesh_target.reshape(-1, 256),
            p_before,
            p_src,
            p_after,
            h0,
            w_proc_dst,
            w_proc_edge,
            mesh_edge_latent,
            w_proc_out,
            w_node_self,
            w_node_agg,
            w_node_out,
            cotangent,
        ],
        [block] * 9 + [square],
        [
            ((reach, width), BF),
            ((mesh_edges, reach), BF),
            ((mesh_edges, width), BF),
            ((256, width), F32),
            ((reach, width), F32),
            ((width, width), F32),
        ],
        flops=12 * mesh_edges * width * width,
    )
    from_after = lax.ppermute(s_before, "wide", down)
    from_before = lax.ppermute(s_after, "wide", up)

    chips = wide // 2
    chunk = 10 * width // devices
    half = narrow * chunk
    far = 4 if chips > 4 else 2
    near = chips // far
    turn = turned(narrow, chunk, 4 if chunk % 16 else 1)
    late = 2 * width
    start = late // (2 * half) * 2 * half
    scales = (enc_scale, proc_scale, node_scale)
    count = (10 * width - start) // (2 * narrow)
    early_shape = ((narrow, 2, -(-count // 16) * 16, width), BF)
    swap = [(i, i ^ 1) for i in range(wide)]
    mesh_out, mesh_grad, returning, early = call(
        functools.partial(mesh_backward, scales, start, half),
        [s_own, from_after, from_before, w_proc_src, d_node, w_node_self, dst_sum, w_proc_dst]
        + [cotangent, w_enc_out, received, h0, a0, agg, d_agg, zeta, unit, w_node_out, gpe, turn],
        [block, ((rows, width), F32), ((slots, width), BF), early_shape],
        [((256, width), BF)] + [square] * 7,
        cut={10: (width, LANE)},
        flops=44 * rows * width * width,
    )
    early = lax.psum_scatter(early, "narrow", scatter_dimension=0, tiled=True)[0]
    returned = lax.all_to_all(
        returning.reshape(devices, capacity, width),
        ("wide", "narrow"),
        split_axis=0,
        concat_axis=0,
        tiled=True,
    ).reshape(slots, width)
    spread = -(-late // (2 * turn.shape[0])) * turn.shape[0] // narrow
    late_shape = ((narrow, spread, width), BF)
    grid_grad, kept, sent = call(
        functools.partial(enc_backward, enc_scale, half),
        [slot, source, returned, enc_sg, enc_edge_latent, grid_latent, w_enc_grid, turn],
        [((grid_rows, width), F32), late_shape, late_shape],
        [square, square],
        scalar=core.reshape(1),
        flops=8 * edges * width * width,
    )
    came = lax.ppermute(sent, "wide", swap)
    last = (kept.astype(F32) + came.astype(F32)).astype(BF)
    early, last = lax.optimization_barrier((early, last))
    sent = lax.dynamic_index_in_dim(early, 1 - core, 0, keepdims=False)
    came = lax.ppermute(sent, "wide", swap)
    last = lax.all_to_all(last, "narrow", split_axis=0, concat_axis=0, tiled=True)
    last = jnp.sum(last.astype(F32), axis=0)[: near * chunk]
    early = lax.dynamic_index_in_dim(early, core, 0, keepdims=False).astype(F32)
    early = (early + came.astype(F32))[:count]
    rest = (10 * width - near * far * 2 * half // far) // (2 * narrow)
    last += jnp.pad(early[rest:], ((near * chunk - (count - rest), 0), (0, 0)))
    both = jnp.concatenate([last, early[:rest]], axis=0).astype(BF)
    both = both.reshape(far, near * chunk, width)
    x = lax.axis_index("wide") // (2 * near)

    def toward(j):
        return lax.dynamic_index_in_dim(both, lax.rem(x + j, far), 0, keepdims=False)

    total = toward(0).astype(F32)
    for j in range(1, far):
        ring = [(i, (i + j * 2 * near) % wide) for i in range(wide)]
        total += lax.ppermute(toward(j), "wide", ring).astype(F32)
    both = total
    both = lax.all_to_all(
        both.astype(BF).reshape(near, chunk, width),
        "wide",
        split_axis=0,
        concat_axis=0,
        tiled=True,
        axis_index_groups=[
            [i * 2 * near + 2 * j + c for j in range(near)] for i in range(far) for c in range(2)
        ],
    )
    summed = jnp.sum(both.astype(F32), axis=0).reshape(-1)
    return (mesh_out, grid_grad, summed, mesh_grad)


def solution(mesh):
    in_specs = (
        P(("wide", "narrow"), None),
        P(("wide", "narrow"), None),
        P(("wide", "narrow")),
        P(("wide", "narrow"), None),
        P(("wide", "narrow")),
        P(("wide", "narrow"), None),
        P(("wide", "narrow"), None),
        P(("wide", "narrow")),
        P(("wide", "narrow")),
        P(),
        P(),
        P(),
        P(),
        P(),
        P(),
        P(),
        P(),
        P(),
        P(),
        P(("wide", "narrow"), None),
    )
    out_specs = (
        P(("wide", "narrow"), None),
        P(("wide", "narrow"), None),
        P(("wide", "narrow")),
        P(("wide", "narrow"), None),
    )
    return jax.shard_map(
        on_device, mesh=mesh, in_specs=in_specs, out_specs=out_specs, check_vma=False
    )
```

```python
import functools

import jax
import jax.numpy as jnp
import numpy as np
from jax import lax
from jax.experimental import pallas as pl
from jax.experimental.pallas import tpu as pltpu
from jax.sharding import PartitionSpec as P

BF = jnp.bfloat16
F32 = jnp.float32
I32 = jnp.int32
LANE = 128
STEP = 640


def dot(left, right):
    return jnp.dot(left, right, preferred_element_type=F32)


def dot_rt(left, right):
    return lax.dot_general(left, right, (((1,), (1,)), ((), ())), preferred_element_type=F32)


def dot_lt(left, right):
    return lax.dot_general(left, right, (((0,), (0,)), ((), ())), preferred_element_type=F32)


def silu_pair(value):
    sig = jax.nn.sigmoid(value)
    act = value * sig
    return act, sig + act * (1.0 - sig)


def columns(row):
    return jnp.broadcast_to(row.astype(F32), (LANE, row.shape[1])).T


def same(cols, width, shift=0):
    wide = jnp.concatenate([cols] * (-(-width // LANE)), axis=1)
    lane = lax.broadcasted_iota(I32, wide.shape, 1) + shift
    return jnp.where(wide == lane.astype(F32), 1.0, 0.0).astype(BF)


def same_t(row, height, shift=0):
    sub = lax.broadcasted_iota(I32, (height, row.shape[1]), 0) + shift
    return jnp.where(sub == row, 1.0, 0.0).astype(BF)


def enc_forward(
    capacity, tdev_ref, trow_ref, src_ref, grid_ref, edge_ref, we_ref, wg_ref, out_ref, sg_ref, slot_ref
):
    edges, width = edge_ref.buffer.shape
    slots = out_ref.buffer.shape[0] * capacity
    tdev = tdev_ref.get()[...]
    member = same_t(tdev, slots // capacity)
    before = lax.broadcasted_iota(I32, (edges, edges), 0) < lax.broadcasted_iota(
        I32, (edges, edges), 1
    )
    ahead = dot(member, jnp.where(before, 1.0, 0.0).astype(BF))
    rank = jnp.sum(member.astype(F32) * ahead, axis=0, keepdims=True)
    slot = tdev * capacity + rank.astype(I32)
    slot_ref.buffer[...] = slot
    slot_ref.send()
    tag = columns(trow_ref.get()[...] + 1).astype(BF)
    grid = grid_ref.get()[...]
    gathered = dot(same(columns(src_ref.get()[...]), grid.shape[0]), grid).astype(BF)
    pre = dot(edge_ref.get()[...], we_ref.get()[...]) + dot(gathered, wg_ref.get()[...])
    act, grad = silu_pair(pre)
    sg_ref.buffer[...] = grad.astype(BF)
    sg_ref.send()
    payload = jnp.concatenate([act.astype(BF), tag], axis=1)
    step = 256
    for at in range(0, slots, step):
        place = same_t(slot, step, at)
        value = dot(place, payload).reshape(step // capacity, capacity, payload.shape[1])
        out_ref.buffer[pl.ds(at // capacity, step // capacity)] = value.astype(BF)


def mesh_forward(recv_ref, wout_ref, static_ref, wsrc_ref, h0_ref, a0_ref, psrc_ref):
    rows, width = static_ref.buffer.shape
    recv = recv_ref.get()[...].astype(F32).reshape(-1, recv_ref.buffer.shape[2])
    pick = same(recv[:, width:], 256, 1)
    a0 = dot_lt(pick, recv[:, :width].astype(BF))[:rows].astype(BF)
    a0_ref.buffer[...] = a0
    a0_ref.send()
    h0 = (static_ref.get()[...].astype(F32) + dot(a0, wout_ref.get()[...])).astype(BF)
    h0_ref.buffer[...] = h0
    h0_ref.send()
    psrc_ref.buffer[...] = dot(h0, wsrc_ref.get()[...]).astype(BF)


def processor(
    proc_scale,
    core_ref,
    msrc_ref,
    mtgt_ref,
    mate_ref,
    po_ref,
    other_ref,
    h0_ref,
    wdst_ref,
    we_ref,
    mel_ref,
    wpo_ref,
    wns_ref,
    wna_ref,
    wno_ref,
    cot_ref,
    smate_ref,
    so_ref,
    sother_ref,
    dst_ref,
    unit_ref,
    dnode_ref,
    dagg_ref,
    agg_ref,
    zeta_ref,
    gpe_ref,
    table,
    hot,
    sg,
    zsum,
    back,
    gacc,
):
    edges, width = mel_ref.buffer.shape
    rows = h0_ref.buffer.shape[0]
    reach = table.shape[0]
    first = reach - 256
    steps, step = msrc_ref.buffer.shape
    h0 = h0_ref.get()[...]
    table[pl.ds(3 * rows, reach - 3 * rows), :] = jnp.zeros((reach - 3 * rows, width), BF)
    table[pl.ds(first, rows), :] = dot(h0, wdst_ref.get()[...]).astype(BF)
    even = core_ref[0] == 0
    mate, other = mate_ref.get()[...], other_ref.get()[...]
    table[pl.ds(0, rows), :] = jnp.where(even, other, mate)
    table[pl.ds(rows, rows), :] = po_ref.get()[...]
    table[pl.ds(2 * rows, rows), :] = jnp.where(even, mate, other)
    zsum[...] = jnp.zeros_like(zsum)
    for ref in (msrc_ref, mtgt_ref, we_ref, mel_ref):
        ref.get()

    def ahead(i, carry):
        at = pl.multiple_of(i * step, step)
        src = columns(msrc_ref.buffer[pl.ds(i, 1), :])
        tgt = columns(mtgt_ref.buffer[pl.ds(i, 1), :] + first)
        src = jnp.concatenate([src] * (reach // LANE), axis=1)
        tgt = jnp.concatenate([tgt] * (reach // LANE), axis=1)
        lane = lax.broadcasted_iota(I32, (step, reach), 1).astype(F32)
        chosen = jnp.where((src == lane) | (tgt == lane), 1.0, 0.0).astype(BF)
        hot[pl.ds(at, step), :] = chosen
        pre = dot(mel_ref.buffer[pl.ds(at, step), :], we_ref.buffer[...])
        act, grad = silu_pair(pre + dot(chosen, table[...]))
        sg[pl.ds(at, step), :] = grad.astype(BF)
        zsum[...] += dot_lt(chosen[:, first:], act.astype(BF))
        return carry

    lax.fori_loop(0, steps, ahead, 0)
    zeta = zsum[pl.ds(0, rows), :].astype(BF)
    cot = cot_ref.get()[...]
    agg = dot(zeta, wpo_ref.get()[...]).astype(BF)
    pre_node = dot(h0, wns_ref.get()[...]) + dot(agg, wna_ref.get()[...])
    act, grad = silu_pair(pre_node)
    d_node = (dot_rt(cot, wno_ref.get()[...]) * grad).astype(BF)
    d_agg = dot_rt(d_node, wna_ref.get()[...]).astype(BF)
    table[pl.ds(first, rows), :] = dot_rt(d_agg, wpo_ref.get()[...]).astype(BF)
    for ref, value in (
        (unit_ref, act.astype(BF)),
        (dnode_ref, d_node),
        (dagg_ref, d_agg),
        (agg_ref, agg),
        (zeta_ref, zeta),
    ):
        ref.buffer[...] = value
        ref.send()
    back[...] = jnp.zeros_like(back)
    gacc[...] = jnp.zeros_like(gacc)

    def behind(i, carry):
        at = pl.multiple_of(i * step, step)
        chosen = hot[pl.ds(at, step), :]
        d_edge = dot(chosen[:, first:], table[pl.ds(first, 256), :])
        d_proc = (d_edge * sg[pl.ds(at, step), :].astype(F32)).astype(BF)
        back[...] += dot_lt(chosen, d_proc)
        gacc[...] += dot_lt(mel_ref.buffer[pl.ds(at, step), :], d_proc)
        return carry

    lax.fori_loop(0, steps, behind, 0)
    lower = back[pl.ds(0, rows), :].astype(BF)
    upper = back[pl.ds(2 * rows, rows), :].astype(BF)
    for ref, value in (
        (sother_ref, jnp.where(even, lower, upper)),
        (smate_ref, jnp.where(even, upper, lower)),
        (so_ref, back[pl.ds(rows, rows), :].astype(BF)),
        (dst_ref, back[pl.ds(first, rows), :].astype(BF)),
    ):
        ref.buffer[...] = value
        ref.send()
    gpe_ref.buffer[...] = (gacc[...] * proc_scale).astype(BF)


def rows_of(held, start, count):
    width = next(ref for ref in held if ref is not None).shape[1]
    pieces = []
    while count:
        size = min(count, width - start % width)
        ref = held[start // width] if start < 10 * width else None
        pieces.append(
            jnp.zeros((size, width), BF) if ref is None else ref[pl.ds(start % width, size), :]
        )
        start, count = start + size, count - size
    return pieces[0] if len(pieces) == 1 else jnp.concatenate(pieces, axis=0)


def split_turned(held, turn, core, start, half, kept, sent):
    even = core == 0
    narrow, length, _ = kept.shape
    slab = turn.shape[0] // narrow
    for at in range(0, length, slab):
        both = []
        for c in range(2):
            lead = range(start + 2 * at * narrow, start + 2 * (at + slab) * narrow, 2 * half)
            rows = [rows_of(held, row + c * half, half) for row in lead]
            rows = rows[0] if len(rows) == 1 else jnp.concatenate(rows, axis=0)
            both.append(dot(turn, rows).astype(BF))
        own, other = jnp.where(even, both[0], both[1]), jnp.where(even, both[1], both[0])
        for y in range(narrow):
            kept[y, pl.ds(at, slab), :] = own[y * slab : (y + 1) * slab]
            sent[y, pl.ds(at, slab), :] = other[y * slab : (y + 1) * slab]


def turn_cores(held, turn, start, half, out):
    narrow = out.buffer.shape[0]
    slab = turn.shape[0] // narrow
    span = 2 * turn.shape[0]
    width = out.buffer.shape[3]
    first = start // span * span
    skip = (start - first) // (2 * narrow)
    leads = [*range(first + span, 10 * width, span), first]
    for k, lead in enumerate(leads):
        low = skip if lead == first else 0
        for c in range(2):
            rows = [rows_of(held, row + c * half, half) for row in range(lead, lead + span, 2 * half)]
            rows = rows[0] if len(rows) == 1 else jnp.concatenate(rows, axis=0)
            value = dot(turn, rows)
            for y in range(narrow):
                piece = value[y * slab + low : (y + 1) * slab]
                out.buffer[y, c, pl.ds(k * slab, slab - low), :] = piece.astype(BF)
    fill = out.buffer.shape[2] - len(leads) * slab + skip
    if fill:
        at = pl.ds(len(leads) * slab - skip, fill)
        out.buffer[:, :, at, :] = jnp.zeros((narrow, 2, fill, width), BF)


def mesh_backward(
    scales, start, half, so_ref, sb_ref, sa_ref, wsrc_ref, dnode_ref, wns_ref, dst_ref, wdst_ref,
    cot_ref, wout_ref, tag_ref, h0_ref, a0_ref, agg_ref, dagg_ref, zeta_ref, unit_ref, wno_ref,
    gpe_ref, turn_ref, out_ref, grad_ref, ret_ref, early_ref,
    padded, geo, gps, gpd, gpo, gns, gna, gno,
):
    enc_scale, proc_scale, node_scale = scales
    rows = so_ref.buffer.shape[0]
    total = sum(ref.get()[...].astype(F32) for ref in (so_ref, sb_ref, sa_ref)).astype(BF)
    d_node = dnode_ref.get()[...]
    dst_sum = dst_ref.get()[...]
    cot = cot_ref.get()[...]
    grad = cot.astype(F32) + dot_rt(d_node, wns_ref.get()[...])
    grad += dot_rt(dst_sum, wdst_ref.get()[...])
    grad += dot_rt(total, wsrc_ref.get()[...])
    grad_ref.buffer[...] = grad
    grad_ref.send()
    d_mesh = grad.astype(BF)
    padded[pl.ds(rows, 256 - rows), :] = jnp.zeros((256 - rows, padded.shape[1]), BF)
    padded[pl.ds(0, rows), :] = dot_rt(d_mesh, wout_ref.get()[...]).astype(BF)
    tag = tag_ref.get()
    devices, capacity, width = ret_ref.buffer.shape
    step = 256 // capacity
    for at in range(0, devices, step):
        pick = same(tag[pl.ds(at, step)].astype(F32).reshape(-1, LANE), 256, 1)
        value = dot(pick, padded[...]).reshape(step, capacity, width)
        ret_ref.buffer[pl.ds(at, step)] = value.astype(BF)
    ret_ref.send()
    h0 = h0_ref.get()[...]
    gps[...] = (dot_lt(h0, total) * proc_scale).astype(BF)
    geo[...] = (dot_lt(a0_ref.get()[...], d_mesh) * enc_scale).astype(BF)
    gns[...] = (dot_lt(h0, d_node) * node_scale).astype(BF)
    gna[...] = (dot_lt(agg_ref.get()[...], d_node) * node_scale).astype(BF)
    gpd[...] = (dot_lt(h0, dst_sum) * proc_scale).astype(BF)
    gpo[...] = (dot_lt(zeta_ref.get()[...], dagg_ref.get()[...]) * proc_scale).astype(BF)
    unit = unit_ref.get()[...]
    gno[...] = (dot_lt(unit, cot) * node_scale).astype(BF)
    out_ref.buffer[...] = (h0.astype(F32) + dot(unit, wno_ref.get()[...])).astype(BF)
    out_ref.send()
    held = [None, None, geo, gpe_ref.get(), gps, gpd, gpo, gns, gna, gno]
    turn_cores(held, turn_ref.get()[...], start, half, early_ref)


def enc_backward(
    enc_scale, half, core_ref, slot_ref, src_ref, ret_ref, sg_ref, edge_ref, grid_ref, wg_ref,
    turn_ref, out_ref, kept_ref, sent_ref, gee, geg,
):
    returned = ret_ref.get()[...].astype(F32).reshape(-1, ret_ref.buffer.shape[2]).astype(BF)
    chosen = same(columns(slot_ref.get()[...]), returned.shape[0])
    d_enc = (dot(chosen, returned) * sg_ref.get()[...].astype(F32)).astype(BF)
    grid_sum = dot(same_t(src_ref.get()[...], grid_ref.buffer.shape[0]), d_enc).astype(BF)
    out_ref.buffer[...] = dot_rt(grid_sum, wg_ref.get()[...])
    out_ref.send()
    gee[...] = (dot_lt(edge_ref.get()[...], d_enc) * enc_scale).astype(BF)
    geg[...] = (dot_lt(grid_ref.get()[...], grid_sum) * enc_scale).astype(BF)
    held = [gee, geg] + [None] * 8
    turn = turn_ref.get()[...]
    split_turned(held, turn, core_ref[0], 0, half, kept_ref.buffer, sent_ref.buffer)


def turned(narrow, chunk, groups):
    rows = np.arange(groups * narrow * chunk).reshape(groups, narrow, chunk)
    rows = rows.transpose(1, 0, 2).reshape(-1)
    return jnp.asarray(rows[:, None] == np.arange(rows.size)[None, :], BF)


class Inward:
    def __init__(self, source, buffer, sem):
        self.copy = pltpu.make_async_copy(source, buffer, sem)
        self.copy.start()
        self.buffer = buffer
        self.waited = False

    def get(self):
        if not self.waited:
            self.copy.wait()
            self.waited = True
        return self.buffer


class Outward:
    def __init__(self, buffer, target, sem):
        self.copy = pltpu.make_async_copy(buffer, target, sem)
        self.buffer = buffer
        self.started = False

    def send(self):
        self.copy.start()
        self.started = True

    def finish(self):
        if not self.started:
            self.send()
        self.copy.wait()


def call(body, ins, outs, scratch=(), scalar=None, cut=None, flops=0):
    cut = cut or {}
    extra = int(scalar is not None)
    count, made = len(ins), len(outs)
    held = [(*one.shape[:-1], cut[i][1]) if i in cut else one.shape for i, one in enumerate(ins)]

    def kernel(*refs):
        lead, refs = refs[:extra], refs[extra:]
        source, target, refs = refs[:count], refs[count : count + made], refs[count + made :]
        here, there, refs = refs[:count], refs[count : count + made], refs[count + made :]
        in_sem, out_sem = refs[:2]
        got = []
        for i in range(count):
            part = source[i].at[:, :, pl.ds(*cut[i])] if i in cut else source[i]
            got.append(Inward(part, here[i], in_sem.at[i]))
        put = [Outward(there[i], target[i], out_sem.at[i]) for i in range(made)]
        body(*lead, *got, *put, *refs[2:])
        for one in got:
            one.get()
        for one in put:
            one.finish()

    hbm = pl.BlockSpec(memory_space=pl.ANY)
    moved = sum(one.size * one.dtype.itemsize for one in ins)
    return pl.pallas_call(
        kernel,
        in_specs=[pl.BlockSpec(memory_space=pltpu.SMEM)] * extra + [hbm] * count,
        out_specs=[hbm] * made,
        out_shape=[jax.ShapeDtypeStruct(shape, kind) for shape, kind in outs],
        scratch_shapes=[pltpu.VMEM(held[i], ins[i].dtype) for i in range(count)]
        + [pltpu.VMEM(shape, kind) for shape, kind in outs]
        + [pltpu.SemaphoreType.DMA((count,)), pltpu.SemaphoreType.DMA((made,))]
        + [pltpu.VMEM(shape, kind) for shape, kind in scratch],
        compiler_params=pltpu.CompilerParams(vmem_limit_bytes=60 << 20),
        cost_estimate=pl.CostEstimate(flops=flops, bytes_accessed=moved, transcendentals=0),
    )(*([scalar] * extra), *ins)


def on_device(
    grid_latent,
    enc_edge_latent,
    enc_source,
    enc_target_device,
    enc_target_row,
    mesh_static,
    mesh_edge_latent,
    mesh_source,
    mesh_target,
    w_enc_edge,
    w_enc_grid,
    w_enc_out,
    w_proc_edge,
    w_proc_src,
    w_proc_dst,
    w_proc_out,
    w_node_self,
    w_node_agg,
    w_node_out,
    cotangent,
):
    wide = lax.axis_size("wide")
    narrow = lax.axis_size("narrow")
    devices = wide * narrow
    edges, width = enc_edge_latent.shape
    grid_rows = grid_latent.shape[0]
    rows = mesh_static.shape[0]
    mesh_edges = mesh_source.shape[0]
    capacity = 2 * edges // devices
    slots = devices * capacity
    enc_scale = float(edges * devices) ** (-0.5)
    proc_scale = float(mesh_edges * devices) ** (-0.5)
    node_scale = float(rows * devices) ** (-0.5)
    core = lax.axis_index("wide") % 2

    source = enc_source.reshape(1, edges)
    payload, enc_sg, slot = call(
        functools.partial(enc_forward, capacity),
        [
            enc_target_device.reshape(1, edges),
            enc_target_row.reshape(1, edges),
            source,
            grid_latent,
            enc_edge_latent,
            w_enc_edge,
            w_enc_grid,
        ],
        [((devices, capacity, width + LANE), BF), ((edges, width), BF), ((1, edges), I32)],
    )
    received = lax.all_to_all(
        payload, ("wide", "narrow"), split_axis=0, concat_axis=0, tiled=True
    )
    h0, a0, p_src = call(
        mesh_forward,
        [received, w_enc_out, mesh_static, w_proc_src],
        [((rows, width), BF)] * 3,
    )
    swap = [(i, i ^ 1) for i in range(wide)]
    cross = [(i, (i + (1 if i % 2 else -1)) % wide) for i in range(wide)]
    p_other = lax.ppermute(p_src, "wide", cross)
    p_mate = lax.ppermute(p_src, "wide", swap)
    where = core.reshape(1)
    square = ((width, width), BF)
    block = ((rows, width), BF)
    reach = -(-3 * rows // LANE) * LANE + 256
    s_mate, s_own, s_other, dst_sum, unit, d_node, d_agg, agg, zeta, gpe = call(
        functools.partial(processor, proc_scale),
        [
            mesh_source.reshape(-1, STEP),
            mesh_target.reshape(-1, STEP),
            p_mate,
            p_src,
            p_other,
            h0,
            w_proc_dst,
            w_proc_edge,
            mesh_edge_latent,
            w_proc_out,
            w_node_self,
            w_node_agg,
            w_node_out,
            cotangent,
        ],
        [block] * 9 + [square],
        [
            ((reach, width), BF),
            ((mesh_edges, reach), BF),
            ((mesh_edges, width), BF),
            ((256, width), F32),
            ((reach, width), F32),
            ((width, width), F32),
        ],
        scalar=where,
        flops=12 * mesh_edges * width * width,
    )
    from_other = lax.ppermute(s_other, "wide", cross)
    from_mate = lax.ppermute(s_mate, "wide", swap)

    chips = wide // 2
    chunk = 10 * width // devices
    half = narrow * chunk
    far = 4 if chips > 4 else 2
    near = chips // far
    turn = turned(narrow, chunk, 4 if chunk % 16 else 1)
    late = 2 * width
    start = late // (2 * half) * 2 * half
    scales = (enc_scale, proc_scale, node_scale)
    count = (10 * width - start) // (2 * narrow)
    early_shape = ((narrow, 2, -(-count // 16) * 16, width), BF)
    mesh_out, mesh_grad, returning, early = call(
        functools.partial(mesh_backward, scales, start, half),
        [s_own, from_mate, from_other, w_proc_src, d_node, w_node_self, dst_sum, w_proc_dst]
        + [cotangent, w_enc_out, received, h0, a0, agg, d_agg, zeta, unit, w_node_out, gpe, turn],
        [block, ((rows, width), F32), ((devices, capacity, width), BF), early_shape],
        [((256, width), BF)] + [square] * 7,
        cut={10: (width, LANE)},
        flops=44 * rows * width * width,
    )
    early = lax.psum_scatter(early, "narrow", scatter_dimension=0, tiled=True)[0]
    returned = lax.all_to_all(
        returning, ("wide", "narrow"), split_axis=0, concat_axis=0, tiled=True
    )
    spread = -(-late // (2 * turn.shape[0])) * turn.shape[0] // narrow
    late_shape = ((narrow, spread, width), BF)
    grid_grad, kept, sent = call(
        functools.partial(enc_backward, enc_scale, half),
        [slot, source, returned, enc_sg, enc_edge_latent, grid_latent, w_enc_grid, turn],
        [((grid_rows, width), F32), late_shape, late_shape],
        [square, square],
        scalar=where,
        flops=8 * edges * width * width,
    )
    came = lax.ppermute(sent, "wide", swap)
    last = (kept.astype(F32) + came.astype(F32)).astype(BF)
    last = lax.all_to_all(last, "narrow", split_axis=0, concat_axis=0, tiled=True)
    last = jnp.sum(last.astype(F32), axis=0)[: near * chunk]
    early, last = lax.optimization_barrier((early, last))
    sent = lax.dynamic_index_in_dim(early, 1 - core, 0, keepdims=False)
    came = lax.ppermute(sent, "wide", swap)
    early = lax.dynamic_index_in_dim(early, core, 0, keepdims=False).astype(F32)
    early = (early + came.astype(F32))[:count]
    rest = (10 * width - near * far * 2 * half // far) // (2 * narrow)
    last += jnp.pad(early[rest:], ((near * chunk - (count - rest), 0), (0, 0)))
    both = jnp.concatenate([last, early[:rest]], axis=0).astype(BF)
    both = both.reshape(far, near * chunk, width)
    x = lax.axis_index("wide") // (2 * near)

    def toward(j):
        return lax.dynamic_index_in_dim(both, lax.rem(x + j, far), 0, keepdims=False)

    total = toward(0).astype(F32)
    for j in range(1, far):
        ring = [(i, (i + j * 2 * near) % wide) for i in range(wide)]
        total += lax.ppermute(toward(j), "wide", ring).astype(F32)
    both = total
    both = lax.all_to_all(
        both.astype(BF).reshape(near, chunk, width),
        "wide",
        split_axis=0,
        concat_axis=0,
        tiled=True,
        axis_index_groups=[
            [i * 2 * near + 2 * j + c for j in range(near)] for i in range(far) for c in range(2)
        ],
    )
    summed = jnp.sum(both.astype(F32), axis=0).reshape(-1)
    return (mesh_out, grid_grad, summed, mesh_grad)


def solution(mesh):
    in_specs = (
        P(("wide", "narrow"), None),
        P(("wide", "narrow"), None),
        P(("wide", "narrow")),
        P(("wide", "narrow"), None),
        P(("wide", "narrow")),
        P(("wide", "narrow"), None),
        P(("wide", "narrow"), None),
        P(("wide", "narrow")),
        P(("wide", "narrow")),
        P(),
        P(),
        P(),
        P(),
        P(),
        P(),
        P(),
        P(),
        P(),
        P(),
        P(("wide", "narrow"), None),
    )
    out_specs = (
        P(("wide", "narrow"), None),
        P(("wide", "narrow"), None),
        P(("wide", "narrow")),
        P(("wide", "narrow"), None),
    )
    return jax.shard_map(
        on_device, mesh=mesh, in_specs=in_specs, out_specs=out_specs, check_vma=False
    )
```

```python
import functools

import jax
import jax.numpy as jnp
import numpy as np
from jax import lax
from jax.experimental import pallas as pl
from jax.experimental.pallas import tpu as pltpu
from jax.sharding import PartitionSpec as P

BF = jnp.bfloat16
F32 = jnp.float32
I32 = jnp.int32
LANE = 128
STEP = 640


def dot(left, right):
    return jnp.dot(left, right, preferred_element_type=F32)


def dot_rt(left, right):
    return lax.dot_general(left, right, (((1,), (1,)), ((), ())), preferred_element_type=F32)


def dot_lt(left, right):
    return lax.dot_general(left, right, (((0,), (0,)), ((), ())), preferred_element_type=F32)


def silu_pair(value):
    sig = jax.nn.sigmoid(value)
    act = value * sig
    return act, sig + act * (1.0 - sig)


def columns(row):
    return jnp.broadcast_to(row.astype(F32), (LANE, row.shape[1])).T


def same(cols, width, shift=0):
    wide = jnp.concatenate([cols] * (-(-width // LANE)), axis=1)
    lane = lax.broadcasted_iota(I32, wide.shape, 1) + shift
    return jnp.where(wide == lane.astype(F32), 1.0, 0.0).astype(BF)


def same_t(row, height, shift=0):
    sub = lax.broadcasted_iota(I32, (height, row.shape[1]), 0) + shift
    return jnp.where(sub == row, 1.0, 0.0).astype(BF)


def enc_forward(
    capacity, tdev_ref, trow_ref, src_ref, grid_ref, edge_ref, we_ref, wg_ref, out_ref, sg_ref, slot_ref
):
    edges, width = edge_ref.buffer.shape
    slots = out_ref.buffer.shape[0] * capacity
    tdev = tdev_ref.get()[...]
    member = same_t(tdev, slots // capacity)
    before = lax.broadcasted_iota(I32, (edges, edges), 0) < lax.broadcasted_iota(
        I32, (edges, edges), 1
    )
    ahead = dot(member, jnp.where(before, 1.0, 0.0).astype(BF))
    rank = jnp.sum(member.astype(F32) * ahead, axis=0, keepdims=True)
    slot = tdev * capacity + rank.astype(I32)
    slot_ref.buffer[...] = slot
    slot_ref.send()
    tag = columns(trow_ref.get()[...] + 1).astype(BF)
    grid = grid_ref.get()[...]
    gathered = dot(same(columns(src_ref.get()[...]), grid.shape[0]), grid).astype(BF)
    pre = dot(edge_ref.get()[...], we_ref.get()[...]) + dot(gathered, wg_ref.get()[...])
    act, grad = silu_pair(pre)
    sg_ref.buffer[...] = grad.astype(BF)
    sg_ref.send()
    payload = jnp.concatenate([act.astype(BF), tag], axis=1)
    step = 256
    for at in range(0, slots, step):
        place = same_t(slot, step, at)
        value = dot(place, payload).reshape(step // capacity, capacity, payload.shape[1])
        out_ref.buffer[pl.ds(at // capacity, step // capacity)] = value.astype(BF)


def mesh_forward(recv_ref, wout_ref, static_ref, wsrc_ref, h0_ref, a0_ref, psrc_ref):
    rows, width = static_ref.buffer.shape
    recv = recv_ref.get()[...].astype(F32).reshape(-1, recv_ref.buffer.shape[2])
    pick = same(recv[:, width:], 256, 1)
    a0 = dot_lt(pick, recv[:, :width].astype(BF))[:rows].astype(BF)
    a0_ref.buffer[...] = a0
    a0_ref.send()
    h0 = (static_ref.get()[...].astype(F32) + dot(a0, wout_ref.get()[...])).astype(BF)
    h0_ref.buffer[...] = h0
    h0_ref.send()
    psrc_ref.buffer[...] = dot(h0, wsrc_ref.get()[...]).astype(BF)


def processor(
    proc_scale,
    core_ref,
    msrc_ref,
    mtgt_ref,
    mate_ref,
    po_ref,
    other_ref,
    h0_ref,
    wdst_ref,
    we_ref,
    mel_ref,
    wpo_ref,
    wns_ref,
    wna_ref,
    wno_ref,
    cot_ref,
    smate_ref,
    so_ref,
    sother_ref,
    dst_ref,
    unit_ref,
    dnode_ref,
    dagg_ref,
    agg_ref,
    zeta_ref,
    gpe_ref,
    table,
    hot,
    sg,
    zsum,
    back,
    gacc,
):
    edges, width = mel_ref.buffer.shape
    rows = h0_ref.buffer.shape[0]
    reach = table.shape[0]
    first = reach - 256
    steps, step = msrc_ref.buffer.shape
    h0 = h0_ref.get()[...]
    table[pl.ds(3 * rows, reach - 3 * rows), :] = jnp.zeros((reach - 3 * rows, width), BF)
    table[pl.ds(first, rows), :] = dot(h0, wdst_ref.get()[...]).astype(BF)
    even = core_ref[0] == 0
    mate, other = mate_ref.get()[...], other_ref.get()[...]
    table[pl.ds(0, rows), :] = jnp.where(even, other, mate)
    table[pl.ds(rows, rows), :] = po_ref.get()[...]
    table[pl.ds(2 * rows, rows), :] = jnp.where(even, mate, other)
    zsum[...] = jnp.zeros_like(zsum)
    for ref in (msrc_ref, mtgt_ref, we_ref, mel_ref):
        ref.get()

    def ahead(i, carry):
        at = i * step
        src = columns(msrc_ref.buffer[pl.ds(i, 1), :])
        tgt = columns(mtgt_ref.buffer[pl.ds(i, 1), :] + first)
        src = jnp.concatenate([src] * (reach // LANE), axis=1)
        tgt = jnp.concatenate([tgt] * (reach // LANE), axis=1)
        lane = lax.broadcasted_iota(I32, (step, reach), 1).astype(F32)
        chosen = jnp.where((src == lane) | (tgt == lane), 1.0, 0.0).astype(BF)
        hot[pl.ds(at, step), :] = chosen
        pre = dot(mel_ref.buffer[pl.ds(at, step), :], we_ref.buffer[...])
        act, grad = silu_pair(pre + dot(chosen, table[...]))
        sg[pl.ds(at, step), :] = grad.astype(BF)
        zsum[...] += dot_lt(chosen[:, first:], act.astype(BF))
        return carry

    for i in range(steps):
        ahead(i, 0)
    zeta = zsum[pl.ds(0, rows), :].astype(BF)
    cot = cot_ref.get()[...]
    agg = dot(zeta, wpo_ref.get()[...]).astype(BF)
    pre_node = dot(h0, wns_ref.get()[...]) + dot(agg, wna_ref.get()[...])
    act, grad = silu_pair(pre_node)
    d_node = (dot_rt(cot, wno_ref.get()[...]) * grad).astype(BF)
    d_agg = dot_rt(d_node, wna_ref.get()[...]).astype(BF)
    table[pl.ds(first, rows), :] = dot_rt(d_agg, wpo_ref.get()[...]).astype(BF)
    for ref, value in (
        (unit_ref, act.astype(BF)),
        (dnode_ref, d_node),
        (dagg_ref, d_agg),
        (agg_ref, agg),
        (zeta_ref, zeta),
    ):
        ref.buffer[...] = value
        ref.send()
    back[...] = jnp.zeros_like(back)
    gacc[...] = jnp.zeros_like(gacc)

    def behind(i, carry):
        at = i * step
        chosen = hot[pl.ds(at, step), :]
        d_edge = dot(chosen[:, first:], table[pl.ds(first, 256), :])
        d_proc = (d_edge * sg[pl.ds(at, step), :].astype(F32)).astype(BF)
        back[...] += dot_lt(chosen, d_proc)
        gacc[...] += dot_lt(mel_ref.buffer[pl.ds(at, step), :], d_proc)
        return carry

    for i in range(steps):
        behind(i, 0)
    lower = back[pl.ds(0, rows), :].astype(BF)
    upper = back[pl.ds(2 * rows, rows), :].astype(BF)
    for ref, value in (
        (sother_ref, jnp.where(even, lower, upper)),
        (smate_ref, jnp.where(even, upper, lower)),
        (so_ref, back[pl.ds(rows, rows), :].astype(BF)),
        (dst_ref, back[pl.ds(first, rows), :].astype(BF)),
    ):
        ref.buffer[...] = value
        ref.send()
    gpe_ref.buffer[...] = (gacc[...] * proc_scale).astype(BF)


def rows_of(held, start, count):
    width = next(ref for ref in held if ref is not None).shape[1]
    pieces = []
    while count:
        size = min(count, width - start % width)
        ref = held[start // width] if start < 10 * width else None
        pieces.append(
            jnp.zeros((size, width), BF) if ref is None else ref[pl.ds(start % width, size), :]
        )
        start, count = start + size, count - size
    return pieces[0] if len(pieces) == 1 else jnp.concatenate(pieces, axis=0)


def split_turned(held, turn, core, start, half, kept, sent):
    even = core == 0
    narrow, length, _ = kept.shape
    slab = turn.shape[0] // narrow
    for at in range(0, length, slab):
        both = []
        for c in range(2):
            lead = range(start + 2 * at * narrow, start + 2 * (at + slab) * narrow, 2 * half)
            rows = [rows_of(held, row + c * half, half) for row in lead]
            rows = rows[0] if len(rows) == 1 else jnp.concatenate(rows, axis=0)
            both.append(dot(turn, rows).astype(BF))
        own, other = jnp.where(even, both[0], both[1]), jnp.where(even, both[1], both[0])
        for y in range(narrow):
            kept[y, pl.ds(at, slab), :] = own[y * slab : (y + 1) * slab]
            sent[y, pl.ds(at, slab), :] = other[y * slab : (y + 1) * slab]


def turn_cores(held, turn, start, half, out):
    narrow = out.buffer.shape[0]
    slab = turn.shape[0] // narrow
    span = 2 * turn.shape[0]
    width = out.buffer.shape[3]
    first = start // span * span
    skip = (start - first) // (2 * narrow)
    leads = [*range(first + span, 10 * width, span), first]
    length = out.buffer.shape[2]
    for k, lead in enumerate(leads):
        low = skip if lead == first else 0
        for c in range(2):
            rows = [rows_of(held, row + c * half, half) for row in range(lead, lead + span, 2 * half)]
            rows = rows[0] if len(rows) == 1 else jnp.concatenate(rows, axis=0)
            value = dot(turn, rows)
            for y in range(narrow):
                piece = value[y * slab + low : (y + 1) * slab]
                out.buffer[y, c, pl.ds(k * slab, slab - low), :] = piece.astype(BF)
        if lead != first:
            out.send_rows(pl.ds(k * slab, slab))
    last = (len(leads) - 1) * slab
    fill = length - last - slab + skip
    if fill:
        at = pl.ds(length - fill, fill)
        out.buffer[:, :, at, :] = jnp.zeros((narrow, 2, fill, width), BF)
    out.send_rows(pl.ds(last, length - last))


def mesh_backward(
    so_ref, sb_ref, sa_ref, wsrc_ref, dnode_ref, wns_ref, dst_ref, wdst_ref, cot_ref, wout_ref,
    tag_ref, grad_ref, ret_ref, total_ref, dmesh_ref, padded,
):
    rows = so_ref.buffer.shape[0]
    total = sum(ref.get()[...].astype(F32) for ref in (so_ref, sb_ref, sa_ref)).astype(BF)
    total_ref.buffer[...] = total
    total_ref.send()
    grad = dot_rt(total, wsrc_ref.get()[...]) + dot_rt(dnode_ref.get()[...], wns_ref.get()[...])
    grad += dot_rt(dst_ref.get()[...], wdst_ref.get()[...])
    grad += cot_ref.get()[...].astype(F32)
    grad_ref.buffer[...] = grad
    grad_ref.send()
    d_mesh = grad.astype(BF)
    dmesh_ref.buffer[...] = d_mesh
    dmesh_ref.send()
    padded[pl.ds(rows, 256 - rows), :] = jnp.zeros((256 - rows, padded.shape[1]), BF)
    padded[pl.ds(0, rows), :] = dot_rt(d_mesh, wout_ref.get()[...]).astype(BF)
    tag = tag_ref.get()
    devices, capacity, width = ret_ref.buffer.shape
    step = 256 // capacity
    for at in range(0, devices, step):
        pick = same(tag[pl.ds(at, step)].astype(F32).reshape(-1, LANE), 256, 1)
        value = dot(pick, padded[...]).reshape(step, capacity, width)
        ret_ref.buffer[pl.ds(at, step)] = value.astype(BF)


def mesh_gradients(
    scales, start, half, h0_ref, total_ref, a0_ref, dmesh_ref, dnode_ref, agg_ref, dst_ref,
    zeta_ref, dagg_ref, unit_ref, cot_ref, wno_ref, gpe_ref, turn_ref, out_ref, early_ref,
    geo, gps, gpd, gpo, gns, gna, gno,
):
    enc_scale, proc_scale, node_scale = scales
    h0 = h0_ref.get()[...]
    d_node = dnode_ref.get()[...]
    gps[...] = (dot_lt(h0, total_ref.get()[...]) * proc_scale).astype(BF)
    geo[...] = (dot_lt(a0_ref.get()[...], dmesh_ref.get()[...]) * enc_scale).astype(BF)
    gns[...] = (dot_lt(h0, d_node) * node_scale).astype(BF)
    gna[...] = (dot_lt(agg_ref.get()[...], d_node) * node_scale).astype(BF)
    gpd[...] = (dot_lt(h0, dst_ref.get()[...]) * proc_scale).astype(BF)
    gpo[...] = (dot_lt(zeta_ref.get()[...], dagg_ref.get()[...]) * proc_scale).astype(BF)
    unit = unit_ref.get()[...]
    gno[...] = (dot_lt(unit, cot_ref.get()[...]) * node_scale).astype(BF)
    out_ref.buffer[...] = (h0.astype(F32) + dot(unit, wno_ref.get()[...])).astype(BF)
    out_ref.send()
    held = [None, None, geo, gpe_ref.get(), gps, gpd, gpo, gns, gna, gno]
    turn_cores(held, turn_ref.get()[...], start, half, early_ref)


def enc_backward(
    enc_scale, half, core_ref, slot_ref, src_ref, ret_ref, sg_ref, edge_ref, grid_ref, wg_ref,
    turn_ref, out_ref, kept_ref, sent_ref, gee, geg,
):
    returned = ret_ref.get()[...].astype(F32).reshape(-1, ret_ref.buffer.shape[2]).astype(BF)
    chosen = same(columns(slot_ref.get()[...]), returned.shape[0])
    d_enc = (dot(chosen, returned) * sg_ref.get()[...].astype(F32)).astype(BF)
    grid_sum = dot(same_t(src_ref.get()[...], grid_ref.buffer.shape[0]), d_enc).astype(BF)
    out_ref.buffer[...] = dot_rt(grid_sum, wg_ref.get()[...])
    out_ref.send()
    gee[...] = (dot_lt(edge_ref.get()[...], d_enc) * enc_scale).astype(BF)
    geg[...] = (dot_lt(grid_ref.get()[...], grid_sum) * enc_scale).astype(BF)
    held = [gee, geg] + [None] * 8
    turn = turn_ref.get()[...]
    split_turned(held, turn, core_ref[0], 0, half, kept_ref.buffer, sent_ref.buffer)


def turned(narrow, chunk, groups):
    rows = np.arange(groups * narrow * chunk).reshape(groups, narrow, chunk)
    rows = rows.transpose(1, 0, 2).reshape(-1)
    return jnp.asarray(rows[:, None] == np.arange(rows.size)[None, :], BF)


class Inward:
    def __init__(self, source, buffer, sem):
        self.copy = pltpu.make_async_copy(source, buffer, sem)
        self.copy.start()
        self.buffer = buffer
        self.waited = False

    def get(self):
        if not self.waited:
            self.copy.wait()
            self.waited = True
        return self.buffer


class Outward:
    def __init__(self, buffer, target, sem, spare):
        self.buffer, self.target, self.sem, self.spare = buffer, target, sem, spare
        self.parts = []

    def send_rows(self, at):
        part = pltpu.make_async_copy(
            self.buffer.at[:, :, at], self.target.at[:, :, at], self.spare.at[len(self.parts)]
        )
        part.start()
        self.parts.append(part)

    def send(self):
        self.parts.append(pltpu.make_async_copy(self.buffer, self.target, self.sem))
        self.parts[0].start()

    def finish(self):
        if not self.parts:
            self.send()
        for part in self.parts:
            part.wait()


def call(body, ins, outs, scratch=(), scalar=None, cut=None, flops=0):
    cut = cut or {}
    extra = int(scalar is not None)
    count, made = len(ins), len(outs)
    held = [(*one.shape[:-1], cut[i][1]) if i in cut else one.shape for i, one in enumerate(ins)]

    def kernel(*refs):
        lead, refs = refs[:extra], refs[extra:]
        source, target, refs = refs[:count], refs[count : count + made], refs[count + made :]
        here, there, refs = refs[:count], refs[count : count + made], refs[count + made :]
        in_sem, out_sem = refs[:2]
        got = []
        for i in range(count):
            part = source[i].at[:, :, pl.ds(*cut[i])] if i in cut else source[i]
            got.append(Inward(part, here[i], in_sem.at[i]))
        put = [Outward(there[i], target[i], out_sem.at[i], refs[2]) for i in range(made)]
        body(*lead, *got, *put, *refs[3:])
        for one in got:
            one.get()
        for one in put:
            one.finish()

    hbm = pl.BlockSpec(memory_space=pl.ANY)
    moved = sum(one.size * one.dtype.itemsize for one in ins)
    return pl.pallas_call(
        kernel,
        in_specs=[pl.BlockSpec(memory_space=pltpu.SMEM)] * extra + [hbm] * count,
        out_specs=[hbm] * made,
        out_shape=[jax.ShapeDtypeStruct(shape, kind) for shape, kind in outs],
        scratch_shapes=[pltpu.VMEM(held[i], ins[i].dtype) for i in range(count)]
        + [pltpu.VMEM(shape, kind) for shape, kind in outs]
        + [pltpu.SemaphoreType.DMA((n,)) for n in (count, made, 8)]
        + [pltpu.VMEM(shape, kind) for shape, kind in scratch],
        compiler_params=pltpu.CompilerParams(vmem_limit_bytes=60 << 20),
        cost_estimate=pl.CostEstimate(flops=flops, bytes_accessed=moved, transcendentals=0),
    )(*([scalar] * extra), *ins)


def on_device(
    grid_latent,
    enc_edge_latent,
    enc_source,
    enc_target_device,
    enc_target_row,
    mesh_static,
    mesh_edge_latent,
    mesh_source,
    mesh_target,
    w_enc_edge,
    w_enc_grid,
    w_enc_out,
    w_proc_edge,
    w_proc_src,
    w_proc_dst,
    w_proc_out,
    w_node_self,
    w_node_agg,
    w_node_out,
    cotangent,
):
    wide = lax.axis_size("wide")
    narrow = lax.axis_size("narrow")
    devices = wide * narrow
    edges, width = enc_edge_latent.shape
    grid_rows = grid_latent.shape[0]
    rows = mesh_static.shape[0]
    mesh_edges = mesh_source.shape[0]
    capacity = 2 * edges // devices
    slots = devices * capacity
    enc_scale = float(edges * devices) ** (-0.5)
    proc_scale = float(mesh_edges * devices) ** (-0.5)
    node_scale = float(rows * devices) ** (-0.5)
    core = lax.axis_index("wide") % 2

    source = enc_source.reshape(1, edges)
    payload, enc_sg, slot = call(
        functools.partial(enc_forward, capacity),
        [
            enc_target_device.reshape(1, edges),
            enc_target_row.reshape(1, edges),
            source,
            grid_latent,
            enc_edge_latent,
            w_enc_edge,
            w_enc_grid,
        ],
        [((devices, capacity, width + LANE), BF), ((edges, width), BF), ((1, edges), I32)],
    )
    received = lax.all_to_all(
        payload, ("wide", "narrow"), split_axis=0, concat_axis=0, tiled=True
    )
    h0, a0, p_src = call(
        mesh_forward,
        [received, w_enc_out, mesh_static, w_proc_src],
        [((rows, width), BF)] * 3,
    )
    swap = [(i, i ^ 1) for i in range(wide)]
    cross = [(i, (i + (1 if i % 2 else -1)) % wide) for i in range(wide)]
    p_other = lax.ppermute(p_src, "wide", cross)
    p_mate = lax.ppermute(p_src, "wide", swap)
    where = core.reshape(1)
    square = ((width, width), BF)
    block = ((rows, width), BF)
    reach = -(-3 * rows // LANE) * LANE + 256
    s_mate, s_own, s_other, dst_sum, unit, d_node, d_agg, agg, zeta, gpe = call(
        functools.partial(processor, proc_scale),
        [
            mesh_source.reshape(-1, STEP),
            mesh_target.reshape(-1, STEP),
            p_mate,
            p_src,
            p_other,
            h0,
            w_proc_dst,
            w_proc_edge,
            mesh_edge_latent,
            w_proc_out,
            w_node_self,
            w_node_agg,
            w_node_out,
            cotangent,
        ],
        [block] * 9 + [square],
        [
            ((reach, width), BF),
            ((mesh_edges, reach), BF),
            ((mesh_edges, width), BF),
            ((256, width), F32),
            ((reach, width), F32),
            ((width, width), F32),
        ],
        scalar=where,
        flops=12 * mesh_edges * width * width,
    )
    from_other = lax.ppermute(s_other, "wide", cross)
    from_mate = lax.ppermute(s_mate, "wide", swap)

    chips = wide // 2
    chunk = 10 * width // devices
    half = narrow * chunk
    far = 4 if chips > 4 else 2
    near = chips // far
    turn = turned(narrow, chunk, 4 if chunk % 16 else 1)
    late = 2 * width
    start = late // (2 * half) * 2 * half
    scales = (enc_scale, proc_scale, node_scale)
    count = (10 * width - start) // (2 * narrow)
    early_shape = ((narrow, 2, -(-count // 16) * 16, width), BF)
    mesh_grad, returning, total, d_mesh = call(
        mesh_backward,
        [s_own, from_mate, from_other, w_proc_src, d_node, w_node_self, dst_sum, w_proc_dst]
        + [cotangent, w_enc_out, received],
        [((rows, width), F32), ((devices, capacity, width), BF), block, block],
        [((256, width), BF)],
        cut={10: (width, LANE)},
        flops=12 * rows * width * width,
    )
    mesh_out, early = call(
        functools.partial(mesh_gradients, scales, start, half),
        [h0, total, a0, d_mesh, d_node, agg, dst_sum, zeta, d_agg, unit, cotangent, w_node_out]
        + [gpe, turn],
        [block, early_shape],
        [square] * 7,
        flops=32 * rows * width * width,
    )
    early = lax.psum_scatter(early, "narrow", scatter_dimension=0, tiled=True)[0]
    returned = lax.all_to_all(
        returning, ("wide", "narrow"), split_axis=0, concat_axis=0, tiled=True
    )
    spread = -(-late // (2 * turn.shape[0])) * turn.shape[0] // narrow
    late_shape = ((narrow, spread, width), BF)
    grid_grad, kept, sent = call(
        functools.partial(enc_backward, enc_scale, half),
        [slot, source, returned, enc_sg, enc_edge_latent, grid_latent, w_enc_grid, turn],
        [((grid_rows, width), F32), late_shape, late_shape],
        [square, square],
        scalar=where,
        flops=1200 * edges * width * width,
    )
    came = lax.ppermute(sent, "wide", swap)
    last = (kept.astype(F32) + came.astype(F32)).astype(BF)
    last = lax.all_to_all(last, "narrow", split_axis=0, concat_axis=0, tiled=True)
    last = jnp.sum(last.astype(F32), axis=0)[: near * chunk]
    early, last = lax.optimization_barrier((early, last))
    sent = lax.dynamic_index_in_dim(early, 1 - core, 0, keepdims=False)
    came = lax.ppermute(sent, "wide", swap)
    early = lax.dynamic_index_in_dim(early, core, 0, keepdims=False).astype(F32)
    early = (early + came.astype(F32))[:count]
    rest = (10 * width - near * far * 2 * half // far) // (2 * narrow)
    last += jnp.pad(early[rest:], ((near * chunk - (count - rest), 0), (0, 0)))
    both = jnp.concatenate([last, early[:rest]], axis=0).astype(BF)
    both = both.reshape(far, near * chunk, width)
    x = lax.axis_index("wide") // (2 * near)

    def toward(j):
        return lax.dynamic_index_in_dim(both, lax.rem(x + j, far), 0, keepdims=False)

    total = toward(0).astype(F32)
    for j in range(1, far):
        ring = [(i, (i + j * 2 * near) % wide) for i in range(wide)]
        total += lax.ppermute(toward(j), "wide", ring).astype(F32)
    both = total
    both = lax.all_to_all(
        both.astype(BF).reshape(near, chunk, width),
        "wide",
        split_axis=0,
        concat_axis=0,
        tiled=True,
        axis_index_groups=[
            [i * 2 * near + 2 * j + c for j in range(near)] for i in range(far) for c in range(2)
        ],
    )
    summed = jnp.sum(both.astype(F32), axis=0).reshape(-1)
    return (mesh_out, grid_grad, summed, mesh_grad)


def solution(mesh):
    in_specs = (
        P(("wide", "narrow"), None),
        P(("wide", "narrow"), None),
        P(("wide", "narrow")),
        P(("wide", "narrow"), None),
        P(("wide", "narrow")),
        P(("wide", "narrow"), None),
        P(("wide", "narrow"), None),
        P(("wide", "narrow")),
        P(("wide", "narrow")),
        P(),
        P(),
        P(),
        P(),
        P(),
        P(),
        P(),
        P(),
        P(),
        P(),
        P(("wide", "narrow"), None),
    )
    out_specs = (
        P(("wide", "narrow"), None),
        P(("wide", "narrow"), None),
        P(("wide", "narrow")),
        P(("wide", "narrow"), None),
    )
    return jax.shard_map(
        on_device, mesh=mesh, in_specs=in_specs, out_specs=out_specs, check_vma=False
    )
```

```python
import functools

import jax
import jax.numpy as jnp
import numpy as np
from jax import lax
from jax.experimental import pallas as pl
from jax.experimental.pallas import tpu as pltpu
from jax.sharding import PartitionSpec as P

BF = jnp.bfloat16
F32 = jnp.float32
I32 = jnp.int32
LANE = 128
STEP = 640


def dot(left, right):
    return jnp.dot(left, right, preferred_element_type=F32)


def dot_rt(left, right):
    return lax.dot_general(left, right, (((1,), (1,)), ((), ())), preferred_element_type=F32)


def dot_lt(left, right):
    return lax.dot_general(left, right, (((0,), (0,)), ((), ())), preferred_element_type=F32)


def silu_pair(value):
    sig = jax.nn.sigmoid(value)
    act = value * sig
    return act, sig + act * (1.0 - sig)


def columns(row):
    return jnp.broadcast_to(row.astype(F32), (LANE, row.shape[1])).T


def same(cols, width, shift=0):
    wide = jnp.concatenate([cols] * (-(-width // LANE)), axis=1)
    lane = lax.broadcasted_iota(I32, wide.shape, 1) + shift
    return jnp.where(wide == lane.astype(F32), 1.0, 0.0).astype(BF)


def same_t(row, height, shift=0):
    sub = lax.broadcasted_iota(I32, (height, row.shape[1]), 0) + shift
    return jnp.where(sub == row, 1.0, 0.0).astype(BF)


def enc_forward(
    capacity, tdev_ref, trow_ref, src_ref, grid_ref, edge_ref, we_ref, wg_ref, out_ref, sg_ref, slot_ref
):
    edges, width = edge_ref.buffer.shape
    slots = out_ref.buffer.shape[0] * capacity
    tdev = tdev_ref.get()[...]
    member = same_t(tdev, slots // capacity)
    before = lax.broadcasted_iota(I32, (edges, edges), 0) < lax.broadcasted_iota(
        I32, (edges, edges), 1
    )
    ahead = dot(member, jnp.where(before, 1.0, 0.0).astype(BF))
    rank = jnp.sum(member.astype(F32) * ahead, axis=0, keepdims=True)
    slot = tdev * capacity + rank.astype(I32)
    slot_ref.buffer[...] = slot
    slot_ref.send()
    tag = columns(trow_ref.get()[...] + 1).astype(BF)
    grid = grid_ref.get()[...]
    gathered = dot(same(columns(src_ref.get()[...]), grid.shape[0]), grid).astype(BF)
    pre = dot(edge_ref.get()[...], we_ref.get()[...]) + dot(gathered, wg_ref.get()[...])
    act, grad = silu_pair(pre)
    sg_ref.buffer[...] = grad.astype(BF)
    sg_ref.send()
    payload = jnp.concatenate([act.astype(BF), tag], axis=1)
    step = 256
    for at in range(0, slots, step):
        place = same_t(slot, step, at)
        value = dot(place, payload).reshape(step // capacity, capacity, payload.shape[1])
        out_ref.buffer[pl.ds(at // capacity, step // capacity)] = value.astype(BF)


def mesh_forward(recv_ref, wout_ref, static_ref, wsrc_ref, h0_ref, a0_ref, psrc_ref):
    rows, width = static_ref.buffer.shape
    recv = recv_ref.get()[...].astype(F32).reshape(-1, recv_ref.buffer.shape[2])
    pick = same(recv[:, width:], 256, 1)
    a0 = dot_lt(pick, recv[:, :width].astype(BF))[:rows].astype(BF)
    a0_ref.buffer[...] = a0
    a0_ref.send()
    h0 = (static_ref.get()[...].astype(F32) + dot(a0, wout_ref.get()[...])).astype(BF)
    h0_ref.buffer[...] = h0
    h0_ref.send()
    psrc_ref.buffer[...] = dot(h0, wsrc_ref.get()[...]).astype(BF)


def processor(
    proc_scale,
    core_ref,
    msrc_ref,
    mtgt_ref,
    mate_ref,
    po_ref,
    other_ref,
    h0_ref,
    wdst_ref,
    we_ref,
    mel_ref,
    wpo_ref,
    wns_ref,
    wna_ref,
    wno_ref,
    cot_ref,
    smate_ref,
    so_ref,
    sother_ref,
    dst_ref,
    unit_ref,
    dnode_ref,
    dagg_ref,
    agg_ref,
    zeta_ref,
    gpe_ref,
    table,
    hot,
    sg,
    zsum,
    back,
    gacc,
):
    edges, width = mel_ref.buffer.shape
    rows = h0_ref.buffer.shape[0]
    reach = table.shape[0]
    first = reach - 256
    steps, step = msrc_ref.buffer.shape
    h0 = h0_ref.get()[...]
    table[pl.ds(3 * rows, reach - 3 * rows), :] = jnp.zeros((reach - 3 * rows, width), BF)
    table[pl.ds(first, rows), :] = dot(h0, wdst_ref.get()[...]).astype(BF)
    even = core_ref[0] == 0
    mate, other = mate_ref.get()[...], other_ref.get()[...]
    table[pl.ds(0, rows), :] = jnp.where(even, other, mate)
    table[pl.ds(rows, rows), :] = po_ref.get()[...]
    table[pl.ds(2 * rows, rows), :] = jnp.where(even, mate, other)
    zsum[...] = jnp.zeros_like(zsum)
    for ref in (msrc_ref, mtgt_ref, we_ref, mel_ref):
        ref.get()

    def ahead(i, carry):
        at = i * step
        src = columns(msrc_ref.buffer[pl.ds(i, 1), :])
        tgt = columns(mtgt_ref.buffer[pl.ds(i, 1), :] + first)
        src = jnp.concatenate([src] * (reach // LANE), axis=1)
        tgt = jnp.concatenate([tgt] * (reach // LANE), axis=1)
        lane = lax.broadcasted_iota(I32, (step, reach), 1).astype(F32)
        chosen = jnp.where((src == lane) | (tgt == lane), 1.0, 0.0).astype(BF)
        hot[pl.ds(at, step), :] = chosen
        pre = dot(mel_ref.buffer[pl.ds(at, step), :], we_ref.buffer[...])
        act, grad = silu_pair(pre + dot(chosen, table[...]))
        sg[pl.ds(at, step), :] = grad.astype(BF)
        zsum[...] += dot_lt(chosen[:, first:], act.astype(BF))
        return carry

    for i in range(steps):
        ahead(i, 0)
    zeta = zsum[pl.ds(0, rows), :].astype(BF)
    cot = cot_ref.get()[...]
    agg = dot(zeta, wpo_ref.get()[...]).astype(BF)
    pre_node = dot(h0, wns_ref.get()[...]) + dot(agg, wna_ref.get()[...])
    act, grad = silu_pair(pre_node)
    d_node = (dot_rt(cot, wno_ref.get()[...]) * grad).astype(BF)
    d_agg = dot_rt(d_node, wna_ref.get()[...]).astype(BF)
    table[pl.ds(first, rows), :] = dot_rt(d_agg, wpo_ref.get()[...]).astype(BF)
    for ref, value in (
        (unit_ref, act.astype(BF)),
        (dnode_ref, d_node),
        (dagg_ref, d_agg),
        (agg_ref, agg),
        (zeta_ref, zeta),
    ):
        ref.buffer[...] = value
        ref.send()
    back[...] = jnp.zeros_like(back)
    gacc[...] = jnp.zeros_like(gacc)

    def behind(i, carry):
        at = i * step
        chosen = hot[pl.ds(at, step), :]
        d_edge = dot(chosen[:, first:], table[pl.ds(first, 256), :])
        d_proc = (d_edge * sg[pl.ds(at, step), :].astype(F32)).astype(BF)
        back[...] += dot_lt(chosen, d_proc)
        gacc[...] += dot_lt(mel_ref.buffer[pl.ds(at, step), :], d_proc)
        return carry

    for i in range(steps):
        behind(i, 0)
    lower = back[pl.ds(0, rows), :].astype(BF)
    upper = back[pl.ds(2 * rows, rows), :].astype(BF)
    for ref, value in (
        (sother_ref, jnp.where(even, lower, upper)),
        (smate_ref, jnp.where(even, upper, lower)),
        (so_ref, back[pl.ds(rows, rows), :].astype(BF)),
        (dst_ref, back[pl.ds(first, rows), :].astype(BF)),
    ):
        ref.buffer[...] = value
        ref.send()
    gpe_ref.buffer[...] = (gacc[...] * proc_scale).astype(BF)


def rows_of(held, start, count):
    width = next(ref for ref in held if ref is not None).shape[1]
    pieces = []
    while count:
        size = min(count, width - start % width)
        ref = held[start // width] if start < 10 * width else None
        pieces.append(
            jnp.zeros((size, width), BF) if ref is None else ref[pl.ds(start % width, size), :]
        )
        start, count = start + size, count - size
    return pieces[0] if len(pieces) == 1 else jnp.concatenate(pieces, axis=0)


def split_turned(held, turn, core, start, half, kept, sent):
    even = core == 0
    narrow, length, _ = kept.buffer.shape
    share = narrow // len(sent)
    slab = turn.shape[0] // narrow
    for at in range(0, length, slab):
        both = []
        for c in range(2):
            lead = range(start + 2 * at * narrow, start + 2 * (at + slab) * narrow, 2 * half)
            rows = [rows_of(held, row + c * half, half) for row in lead]
            rows = rows[0] if len(rows) == 1 else jnp.concatenate(rows, axis=0)
            both.append(dot(turn, rows).astype(BF))
        own, other = jnp.where(even, both[0], both[1]), jnp.where(even, both[1], both[0])
        for y in range(narrow):
            kept.buffer[y, pl.ds(at, slab), :] = own[y * slab : (y + 1) * slab]
            sent[y // share].buffer[y % share, pl.ds(at, slab), :] = other[y * slab : (y + 1) * slab]
        for one in (kept, *sent):
            one.send_rows(pl.ds(at, slab))


def mesh_backward(
    so_ref, sb_ref, sa_ref, wsrc_ref, dnode_ref, wns_ref, dst_ref, wdst_ref, cot_ref, wout_ref,
    tag_ref, grad_ref, ret_ref, total_ref, dmesh_ref, padded,
):
    rows = so_ref.buffer.shape[0]
    total = sum(ref.get()[...].astype(F32) for ref in (so_ref, sb_ref, sa_ref)).astype(BF)
    total_ref.buffer[...] = total
    total_ref.send()
    grad = dot_rt(total, wsrc_ref.get()[...]) + dot_rt(dnode_ref.get()[...], wns_ref.get()[...])
    grad += dot_rt(dst_ref.get()[...], wdst_ref.get()[...])
    grad += cot_ref.get()[...].astype(F32)
    grad_ref.buffer[...] = grad
    grad_ref.send()
    d_mesh = grad.astype(BF)
    dmesh_ref.buffer[...] = d_mesh
    dmesh_ref.send()
    padded[pl.ds(rows, 256 - rows), :] = jnp.zeros((256 - rows, padded.shape[1]), BF)
    padded[pl.ds(0, rows), :] = dot_rt(d_mesh, wout_ref.get()[...]).astype(BF)
    tag = tag_ref.get()
    devices, capacity, width = ret_ref.buffer.shape
    step = 256 // capacity
    for at in range(0, devices, step):
        pick = same(tag[pl.ds(at, step)].astype(F32).reshape(-1, LANE), 256, 1)
        value = dot(pick, padded[...]).reshape(step, capacity, width)
        ret_ref.buffer[pl.ds(at, step)] = value.astype(BF)


def mesh_gradients(
    scales, start, half, core_ref, h0_ref, total_ref, a0_ref, dmesh_ref, dnode_ref, agg_ref, dst_ref,
    zeta_ref, dagg_ref, unit_ref, cot_ref, wno_ref, gpe_ref, turn_ref, out_ref, kept_ref, *refs,
):
    sent, (geo, gps, gpd, gpo, gns, gna, gno) = refs[:-7], refs[-7:]
    enc_scale, proc_scale, node_scale = scales
    h0 = h0_ref.get()[...]
    d_node = dnode_ref.get()[...]
    gps[...] = (dot_lt(h0, total_ref.get()[...]) * proc_scale).astype(BF)
    geo[...] = (dot_lt(a0_ref.get()[...], dmesh_ref.get()[...]) * enc_scale).astype(BF)
    gns[...] = (dot_lt(h0, d_node) * node_scale).astype(BF)
    gna[...] = (dot_lt(agg_ref.get()[...], d_node) * node_scale).astype(BF)
    gpd[...] = (dot_lt(h0, dst_ref.get()[...]) * proc_scale).astype(BF)
    gpo[...] = (dot_lt(zeta_ref.get()[...], dagg_ref.get()[...]) * proc_scale).astype(BF)
    unit = unit_ref.get()[...]
    gno[...] = (dot_lt(unit, cot_ref.get()[...]) * node_scale).astype(BF)
    out_ref.buffer[...] = (h0.astype(F32) + dot(unit, wno_ref.get()[...])).astype(BF)
    out_ref.send()
    held = [None, None, geo, gpe_ref.get(), gps, gpd, gpo, gns, gna, gno]
    split_turned(held, turn_ref.get()[...], core_ref[0], start, half, kept_ref, sent)


def enc_backward(
    enc_scale, half, core_ref, slot_ref, src_ref, ret_ref, sg_ref, edge_ref, grid_ref, wg_ref,
    turn_ref, out_ref, kept_ref, sent_ref, gee, geg,
):
    returned = ret_ref.get()[...].astype(F32).reshape(-1, ret_ref.buffer.shape[2]).astype(BF)
    chosen = same(columns(slot_ref.get()[...]), returned.shape[0])
    d_enc = (dot(chosen, returned) * sg_ref.get()[...].astype(F32)).astype(BF)
    grid_sum = dot(same_t(src_ref.get()[...], grid_ref.buffer.shape[0]), d_enc).astype(BF)
    out_ref.buffer[...] = dot_rt(grid_sum, wg_ref.get()[...])
    out_ref.send()
    gee[...] = (dot_lt(edge_ref.get()[...], d_enc) * enc_scale).astype(BF)
    geg[...] = (dot_lt(grid_ref.get()[...], grid_sum) * enc_scale).astype(BF)
    held = [gee, geg] + [None] * 8
    turn = turn_ref.get()[...]
    split_turned(held, turn, core_ref[0], 0, half, kept_ref, [sent_ref])


def turned(narrow, chunk, groups):
    rows = np.arange(groups * narrow * chunk).reshape(groups, narrow, chunk)
    rows = rows.transpose(1, 0, 2).reshape(-1)
    return jnp.asarray(rows[:, None] == np.arange(rows.size)[None, :], BF)


class Inward:
    def __init__(self, source, buffer, sem):
        self.copy = pltpu.make_async_copy(source, buffer, sem)
        self.copy.start()
        self.buffer = buffer
        self.waited = False

    def get(self):
        if not self.waited:
            self.copy.wait()
            self.waited = True
        return self.buffer


class Outward:
    def __init__(self, buffer, target, sem, spare, first):
        self.buffer, self.target, self.sem, self.spare = buffer, target, sem, spare
        self.parts, self.first = [], first

    def send_rows(self, at):
        part = pltpu.make_async_copy(
            self.buffer.at[:, at], self.target.at[:, at], self.spare.at[self.first + len(self.parts)]
        )
        part.start()
        self.parts.append(part)

    def send(self):
        self.parts.append(pltpu.make_async_copy(self.buffer, self.target, self.sem))
        self.parts[0].start()

    def finish(self):
        if not self.parts:
            self.send()
        for part in self.parts:
            part.wait()


def call(body, ins, outs, scratch=(), scalar=None, cut=None, flops=0):
    cut = cut or {}
    extra = int(scalar is not None)
    count, made = len(ins), len(outs)
    held = [(*one.shape[:-1], cut[i][1]) if i in cut else one.shape for i, one in enumerate(ins)]

    def kernel(*refs):
        lead, refs = refs[:extra], refs[extra:]
        source, target, refs = refs[:count], refs[count : count + made], refs[count + made :]
        here, there, refs = refs[:count], refs[count : count + made], refs[count + made :]
        in_sem, out_sem = refs[:2]
        got = []
        for i in range(count):
            part = source[i].at[:, :, pl.ds(*cut[i])] if i in cut else source[i]
            got.append(Inward(part, here[i], in_sem.at[i]))
        put = [Outward(there[i], target[i], out_sem.at[i], refs[2], 8 * i) for i in range(made)]
        body(*lead, *got, *put, *refs[3:])
        for one in got:
            one.get()
        for one in put:
            one.finish()

    hbm = pl.BlockSpec(memory_space=pl.ANY)
    moved = sum(one.size * one.dtype.itemsize for one in ins)
    return pl.pallas_call(
        kernel,
        in_specs=[pl.BlockSpec(memory_space=pltpu.SMEM)] * extra + [hbm] * count,
        out_specs=[hbm] * made,
        out_shape=[jax.ShapeDtypeStruct(shape, kind) for shape, kind in outs],
        scratch_shapes=[pltpu.VMEM(held[i], ins[i].dtype) for i in range(count)]
        + [pltpu.VMEM(shape, kind) for shape, kind in outs]
        + [pltpu.SemaphoreType.DMA((n,)) for n in (count, made, 8 * made)]
        + [pltpu.VMEM(shape, kind) for shape, kind in scratch],
        compiler_params=pltpu.CompilerParams(vmem_limit_bytes=60 << 20),
        cost_estimate=pl.CostEstimate(flops=flops, bytes_accessed=moved, transcendentals=0),
    )(*([scalar] * extra), *ins)


def on_device(
    grid_latent,
    enc_edge_latent,
    enc_source,
    enc_target_device,
    enc_target_row,
    mesh_static,
    mesh_edge_latent,
    mesh_source,
    mesh_target,
    w_enc_edge,
    w_enc_grid,
    w_enc_out,
    w_proc_edge,
    w_proc_src,
    w_proc_dst,
    w_proc_out,
    w_node_self,
    w_node_agg,
    w_node_out,
    cotangent,
):
    wide = lax.axis_size("wide")
    narrow = lax.axis_size("narrow")
    devices = wide * narrow
    edges, width = enc_edge_latent.shape
    grid_rows = grid_latent.shape[0]
    rows = mesh_static.shape[0]
    mesh_edges = mesh_source.shape[0]
    capacity = 2 * edges // devices
    slots = devices * capacity
    enc_scale = float(edges * devices) ** (-0.5)
    proc_scale = float(mesh_edges * devices) ** (-0.5)
    node_scale = float(rows * devices) ** (-0.5)
    core = lax.axis_index("wide") % 2

    source = enc_source.reshape(1, edges)
    payload, enc_sg, slot = call(
        functools.partial(enc_forward, capacity),
        [
            enc_target_device.reshape(1, edges),
            enc_target_row.reshape(1, edges),
            source,
            grid_latent,
            enc_edge_latent,
            w_enc_edge,
            w_enc_grid,
        ],
        [((devices, capacity, width + LANE), BF), ((edges, width), BF), ((1, edges), I32)],
    )
    received = lax.all_to_all(
        payload, ("wide", "narrow"), split_axis=0, concat_axis=0, tiled=True
    )
    h0, a0, p_src = call(
        mesh_forward,
        [received, w_enc_out, mesh_static, w_proc_src],
        [((rows, width), BF)] * 3,
    )
    swap = [(i, i ^ 1) for i in range(wide)]
    cross = [(i, (i + (1 if i % 2 else -1)) % wide) for i in range(wide)]
    p_other = lax.ppermute(p_src, "wide", cross)
    p_mate = lax.ppermute(p_src, "wide", swap)
    where = core.reshape(1)
    square = ((width, width), BF)
    block = ((rows, width), BF)
    reach = -(-3 * rows // LANE) * LANE + 256
    s_mate, s_own, s_other, dst_sum, unit, d_node, d_agg, agg, zeta, gpe = call(
        functools.partial(processor, proc_scale),
        [
            mesh_source.reshape(-1, STEP),
            mesh_target.reshape(-1, STEP),
            p_mate,
            p_src,
            p_other,
            h0,
            w_proc_dst,
            w_proc_edge,
            mesh_edge_latent,
            w_proc_out,
            w_node_self,
            w_node_agg,
            w_node_out,
            cotangent,
        ],
        [block] * 9 + [square],
        [
            ((reach, width), BF),
            ((mesh_edges, reach), BF),
            ((mesh_edges, width), BF),
            ((256, width), F32),
            ((reach, width), F32),
            ((width, width), F32),
        ],
        scalar=where,
        flops=12 * mesh_edges * width * width,
    )
    from_other = lax.ppermute(s_other, "wide", cross)
    from_mate = lax.ppermute(s_mate, "wide", swap)

    chips = wide // 2
    chunk = 10 * width // devices
    half = narrow * chunk
    far = 4 if chips > 4 else 2
    near = chips // far
    turn = turned(narrow, chunk, 4 if chunk % 16 else 1)
    late = 2 * width
    span = 2 * turn.shape[0]
    start = late // span * span
    scales = (enc_scale, proc_scale, node_scale)
    count = (10 * width - start) // (2 * narrow)
    early_shape = ((narrow, count, width), BF)
    pieces = min(2, narrow)
    sent_shape = ((narrow // pieces, count, width), BF)
    mesh_grad, returning, total, d_mesh = call(
        mesh_backward,
        [s_own, from_mate, from_other, w_proc_src, d_node, w_node_self, dst_sum, w_proc_dst]
        + [cotangent, w_enc_out, received],
        [((rows, width), F32), ((devices, capacity, width), BF), block, block],
        [((256, width), BF)],
        cut={10: (width, LANE)},
        flops=12 * rows * width * width,
    )
    mesh_out, kept, *sent = call(
        functools.partial(mesh_gradients, scales, start, half),
        [h0, total, a0, d_mesh, d_node, agg, dst_sum, zeta, d_agg, unit, cotangent, w_node_out]
        + [gpe, turn],
        [block, early_shape] + [sent_shape] * pieces,
        [square] * 7,
        scalar=where,
        flops=32 * rows * width * width,
    )
    came = jnp.concatenate([lax.ppermute(one, "wide", swap) for one in sent], axis=0)
    early = (kept.astype(F32) + came.astype(F32)).astype(BF)
    early = lax.psum_scatter(early, "narrow", scatter_dimension=0, tiled=True)[0]
    returned = lax.all_to_all(
        returning, ("wide", "narrow"), split_axis=0, concat_axis=0, tiled=True
    )
    spread = -(-late // (2 * turn.shape[0])) * turn.shape[0] // narrow
    late_shape = ((narrow, spread, width), BF)
    grid_grad, kept, sent = call(
        functools.partial(enc_backward, enc_scale, half),
        [slot, source, returned, enc_sg, enc_edge_latent, grid_latent, w_enc_grid, turn],
        [((grid_rows, width), F32), late_shape, late_shape],
        [square, square],
        scalar=where,
        flops=1200 * edges * width * width,
    )
    came = lax.ppermute(sent, "wide", swap)
    last = (kept.astype(F32) + came.astype(F32)).astype(BF)
    last = lax.all_to_all(last, "narrow", split_axis=0, concat_axis=0, tiled=True)
    last = jnp.sum(last.astype(F32), axis=0)[: near * chunk]
    early, last = lax.optimization_barrier((early, last))
    early = jnp.pad(early, ((start // (2 * narrow), 0), (0, 0))).astype(F32)
    early += jnp.pad(last, ((0, early.shape[0] - last.shape[0]), (0, 0)))
    both = early.astype(BF).reshape(far, near * chunk, width)
    x = lax.axis_index("wide") // (2 * near)

    def toward(j):
        return lax.dynamic_index_in_dim(both, lax.rem(x + j, far), 0, keepdims=False)

    total = toward(0).astype(F32)
    for j in range(1, far):
        ring = [(i, (i + j * 2 * near) % wide) for i in range(wide)]
        total += lax.ppermute(toward(j), "wide", ring).astype(F32)
    both = total
    both = lax.all_to_all(
        both.astype(BF).reshape(near, chunk, width),
        "wide",
        split_axis=0,
        concat_axis=0,
        tiled=True,
        axis_index_groups=[
            [i * 2 * near + 2 * j + c for j in range(near)] for i in range(far) for c in range(2)
        ],
    )
    summed = jnp.sum(both.astype(F32), axis=0).reshape(-1)
    return (mesh_out, grid_grad, summed, mesh_grad)


def solution(mesh):
    in_specs = (
        P(("wide", "narrow"), None),
        P(("wide", "narrow"), None),
        P(("wide", "narrow")),
        P(("wide", "narrow"), None),
        P(("wide", "narrow")),
        P(("wide", "narrow"), None),
        P(("wide", "narrow"), None),
        P(("wide", "narrow")),
        P(("wide", "narrow")),
        P(),
        P(),
        P(),
        P(),
        P(),
        P(),
        P(),
        P(),
        P(),
        P(),
        P(("wide", "narrow"), None),
    )
    out_specs = (
        P(("wide", "narrow"), None),
        P(("wide", "narrow"), None),
        P(("wide", "narrow")),
        P(("wide", "narrow"), None),
    )
    return jax.shard_map(
        on_device, mesh=mesh, in_specs=in_specs, out_specs=out_specs, check_vma=False
    )
```

```python
import functools

import jax
import jax.numpy as jnp
import numpy as np
from jax import lax
from jax.experimental import pallas as pl
from jax.experimental.pallas import tpu as pltpu
from jax.sharding import PartitionSpec as P

BF = jnp.bfloat16
F32 = jnp.float32
I32 = jnp.int32
LANE = 128
STEP = 640


def dot(left, right):
    return jnp.dot(left, right, preferred_element_type=F32)


def dot_rt(left, right):
    return lax.dot_general(left, right, (((1,), (1,)), ((), ())), preferred_element_type=F32)


def dot_lt(left, right):
    return lax.dot_general(left, right, (((0,), (0,)), ((), ())), preferred_element_type=F32)


def silu_pair(value):
    sig = jax.nn.sigmoid(value)
    act = value * sig
    return act, sig + act * (1.0 - sig)


def columns(row):
    return jnp.broadcast_to(row.astype(F32), (LANE, row.shape[1])).T


def same(cols, width, shift=0):
    wide = jnp.concatenate([cols] * (-(-width // LANE)), axis=1)
    lane = lax.broadcasted_iota(I32, wide.shape, 1) + shift
    return jnp.where(wide == lane.astype(F32), 1.0, 0.0).astype(BF)


def same_t(row, height, shift=0):
    sub = lax.broadcasted_iota(I32, (height, row.shape[1]), 0) + shift
    return jnp.where(sub == row, 1.0, 0.0).astype(BF)


def enc_forward(
    capacity, tdev_ref, trow_ref, src_ref, grid_ref, edge_ref, we_ref, wg_ref, out_ref, sg_ref, slot_ref
):
    edges, width = edge_ref.buffer.shape
    slots = out_ref.buffer.shape[0] * capacity
    tdev = tdev_ref.get()[...]
    member = same_t(tdev, slots // capacity)
    before = lax.broadcasted_iota(I32, (edges, edges), 0) < lax.broadcasted_iota(
        I32, (edges, edges), 1
    )
    ahead = dot(member, jnp.where(before, 1.0, 0.0).astype(BF))
    rank = jnp.sum(member.astype(F32) * ahead, axis=0, keepdims=True)
    slot = tdev * capacity + rank.astype(I32)
    slot_ref.buffer[...] = slot
    slot_ref.send()
    tag = columns(trow_ref.get()[...] + 1).astype(BF)
    grid = grid_ref.get()[...]
    gathered = dot(same(columns(src_ref.get()[...]), grid.shape[0]), grid).astype(BF)
    pre = dot(edge_ref.get()[...], we_ref.get()[...]) + dot(gathered, wg_ref.get()[...])
    act, grad = silu_pair(pre)
    sg_ref.buffer[...] = grad.astype(BF)
    sg_ref.send()
    payload = jnp.concatenate([act.astype(BF), tag], axis=1)
    step = 256
    for at in range(0, slots, step):
        place = same_t(slot, step, at)
        value = dot(place, payload).reshape(step // capacity, capacity, payload.shape[1])
        out_ref.buffer[pl.ds(at // capacity, step // capacity)] = value.astype(BF)


def mesh_forward(recv_ref, wout_ref, static_ref, wsrc_ref, h0_ref, a0_ref, psrc_ref):
    rows, width = static_ref.buffer.shape
    recv = recv_ref.get()[...].astype(F32).reshape(-1, recv_ref.buffer.shape[2])
    pick = same(recv[:, width:], 256, 1)
    a0 = dot_lt(pick, recv[:, :width].astype(BF))[:rows].astype(BF)
    a0_ref.buffer[...] = a0
    a0_ref.send()
    h0 = (static_ref.get()[...].astype(F32) + dot(a0, wout_ref.get()[...])).astype(BF)
    h0_ref.buffer[...] = h0
    h0_ref.send()
    psrc_ref.buffer[...] = dot(h0, wsrc_ref.get()[...]).astype(BF)


def processor(
    proc_scale,
    core_ref,
    msrc_ref,
    mtgt_ref,
    mate_ref,
    po_ref,
    other_ref,
    h0_ref,
    wdst_ref,
    we_ref,
    mel_ref,
    wpo_ref,
    wns_ref,
    wna_ref,
    wno_ref,
    cot_ref,
    smate_ref,
    so_ref,
    sother_ref,
    dst_ref,
    unit_ref,
    dnode_ref,
    dagg_ref,
    agg_ref,
    zeta_ref,
    gpe_ref,
    table,
    hot,
    sg,
    zsum,
    back,
    gacc,
):
    edges, width = mel_ref.buffer.shape
    rows = h0_ref.buffer.shape[0]
    reach = table.shape[0]
    first = reach - 256
    steps, step = msrc_ref.buffer.shape
    h0 = h0_ref.get()[...]
    table[pl.ds(3 * rows, reach - 3 * rows), :] = jnp.zeros((reach - 3 * rows, width), BF)
    table[pl.ds(first, rows), :] = dot(h0, wdst_ref.get()[...]).astype(BF)
    even = core_ref[0] == 0
    mate, other = mate_ref.get()[...], other_ref.get()[...]
    table[pl.ds(0, rows), :] = jnp.where(even, other, mate)
    table[pl.ds(rows, rows), :] = po_ref.get()[...]
    table[pl.ds(2 * rows, rows), :] = jnp.where(even, mate, other)
    zsum[...] = jnp.zeros_like(zsum)
    for ref in (msrc_ref, mtgt_ref, we_ref, mel_ref):
        ref.get()

    def ahead(i, carry):
        at = i * step
        src = columns(msrc_ref.buffer[pl.ds(i, 1), :])
        tgt = columns(mtgt_ref.buffer[pl.ds(i, 1), :] + first)
        src = jnp.concatenate([src] * (reach // LANE), axis=1)
        tgt = jnp.concatenate([tgt] * (reach // LANE), axis=1)
        lane = lax.broadcasted_iota(I32, (step, reach), 1).astype(F32)
        chosen = jnp.where((src == lane) | (tgt == lane), 1.0, 0.0).astype(BF)
        hot[pl.ds(at, step), :] = chosen
        pre = dot(mel_ref.buffer[pl.ds(at, step), :], we_ref.buffer[...])
        act, grad = silu_pair(pre + dot(chosen, table[...]))
        sg[pl.ds(at, step), :] = grad.astype(BF)
        zsum[...] += dot_lt(chosen[:, first:], act.astype(BF))
        return carry

    for i in range(steps):
        ahead(i, 0)
    zeta = zsum[pl.ds(0, rows), :].astype(BF)
    cot = cot_ref.get()[...]
    agg = dot(zeta, wpo_ref.get()[...]).astype(BF)
    pre_node = dot(h0, wns_ref.get()[...]) + dot(agg, wna_ref.get()[...])
    act, grad = silu_pair(pre_node)
    d_node = (dot_rt(cot, wno_ref.get()[...]) * grad).astype(BF)
    d_agg = dot_rt(d_node, wna_ref.get()[...]).astype(BF)
    table[pl.ds(first, rows), :] = dot_rt(d_agg, wpo_ref.get()[...]).astype(BF)
    for ref, value in (
        (unit_ref, act.astype(BF)),
        (dnode_ref, d_node),
        (dagg_ref, d_agg),
        (agg_ref, agg),
        (zeta_ref, zeta),
    ):
        ref.buffer[...] = value
        ref.send()
    back[...] = jnp.zeros_like(back)
    gacc[...] = jnp.zeros_like(gacc)

    def behind(i, carry):
        at = i * step
        chosen = hot[pl.ds(at, step), :]
        d_edge = dot(chosen[:, first:], table[pl.ds(first, 256), :])
        d_proc = (d_edge * sg[pl.ds(at, step), :].astype(F32)).astype(BF)
        back[...] += dot_lt(chosen, d_proc)
        gacc[...] += dot_lt(mel_ref.buffer[pl.ds(at, step), :], d_proc)
        return carry

    for i in range(steps):
        behind(i, 0)
    lower = back[pl.ds(0, rows), :].astype(BF)
    upper = back[pl.ds(2 * rows, rows), :].astype(BF)
    for ref, value in (
        (sother_ref, jnp.where(even, lower, upper)),
        (smate_ref, jnp.where(even, upper, lower)),
        (so_ref, back[pl.ds(rows, rows), :].astype(BF)),
        (dst_ref, back[pl.ds(first, rows), :].astype(BF)),
    ):
        ref.buffer[...] = value
        ref.send()
    gpe_ref.buffer[...] = (gacc[...] * proc_scale).astype(BF)


def rows_of(held, start, count):
    width = next(ref for ref in held if ref is not None).shape[1]
    pieces = []
    while count:
        size = min(count, width - start % width)
        ref = held[start // width] if start < 10 * width else None
        pieces.append(
            jnp.zeros((size, width), BF) if ref is None else ref[pl.ds(start % width, size), :]
        )
        start, count = start + size, count - size
    return pieces[0] if len(pieces) == 1 else jnp.concatenate(pieces, axis=0)


def split_turned(held, turn, core, start, half, kept, sent):
    even = core == 0
    narrow, length, _ = kept.buffer.shape
    share = narrow // len(sent)
    slab = turn.shape[0] // narrow
    for at in range(0, length, slab):
        both = []
        for c in range(2):
            lead = range(start + 2 * at * narrow, start + 2 * (at + slab) * narrow, 2 * half)
            rows = [rows_of(held, row + c * half, half) for row in lead]
            rows = rows[0] if len(rows) == 1 else jnp.concatenate(rows, axis=0)
            both.append(dot(turn, rows).astype(BF))
        own, other = jnp.where(even, both[0], both[1]), jnp.where(even, both[1], both[0])
        for y in range(narrow):
            kept.buffer[y, pl.ds(at, slab), :] = own[y * slab : (y + 1) * slab]
            sent[y // share].buffer[y % share, pl.ds(at, slab), :] = other[y * slab : (y + 1) * slab]
        for one in (kept, *sent):
            one.send_rows(pl.ds(at, slab))


def mesh_backward(
    so_ref, sb_ref, sa_ref, wsrc_ref, dnode_ref, wns_ref, dst_ref, wdst_ref, cot_ref, wout_ref,
    tag_ref, grad_ref, ret_ref, total_ref, dmesh_ref, padded,
):
    rows = so_ref.buffer.shape[0]
    total = sum(ref.get()[...].astype(F32) for ref in (so_ref, sb_ref, sa_ref)).astype(BF)
    total_ref.buffer[...] = total
    total_ref.send()
    grad = dot_rt(total, wsrc_ref.get()[...]) + dot_rt(dnode_ref.get()[...], wns_ref.get()[...])
    grad += dot_rt(dst_ref.get()[...], wdst_ref.get()[...])
    grad += cot_ref.get()[...].astype(F32)
    grad_ref.buffer[...] = grad
    grad_ref.send()
    d_mesh = grad.astype(BF)
    dmesh_ref.buffer[...] = d_mesh
    dmesh_ref.send()
    padded[pl.ds(rows, 256 - rows), :] = jnp.zeros((256 - rows, padded.shape[1]), BF)
    padded[pl.ds(0, rows), :] = dot_rt(d_mesh, wout_ref.get()[...]).astype(BF)
    tag = tag_ref.get()
    devices, capacity, width = ret_ref.buffer.shape
    step = 256 // capacity
    for at in range(0, devices, step):
        pick = same(tag[pl.ds(at, step)].astype(F32).reshape(-1, LANE), 256, 1)
        value = dot(pick, padded[...]).reshape(step, capacity, width)
        ret_ref.buffer[pl.ds(at, step)] = value.astype(BF)


def mesh_gradients(
    scales, start, half, core_ref, h0_ref, total_ref, a0_ref, dmesh_ref, dnode_ref, agg_ref, dst_ref,
    zeta_ref, dagg_ref, unit_ref, cot_ref, wno_ref, gpe_ref, turn_ref, out_ref, kept_ref, *refs,
):
    sent, (geo, gps, gpd, gpo, gns, gna, gno) = refs[:-7], refs[-7:]
    enc_scale, proc_scale, node_scale = scales
    h0 = h0_ref.get()[...]
    d_node = dnode_ref.get()[...]
    gps[...] = (dot_lt(h0, total_ref.get()[...]) * proc_scale).astype(BF)
    geo[...] = (dot_lt(a0_ref.get()[...], dmesh_ref.get()[...]) * enc_scale).astype(BF)
    gns[...] = (dot_lt(h0, d_node) * node_scale).astype(BF)
    gna[...] = (dot_lt(agg_ref.get()[...], d_node) * node_scale).astype(BF)
    gpd[...] = (dot_lt(h0, dst_ref.get()[...]) * proc_scale).astype(BF)
    gpo[...] = (dot_lt(zeta_ref.get()[...], dagg_ref.get()[...]) * proc_scale).astype(BF)
    unit = unit_ref.get()[...]
    gno[...] = (dot_lt(unit, cot_ref.get()[...]) * node_scale).astype(BF)
    out_ref.buffer[...] = (h0.astype(F32) + dot(unit, wno_ref.get()[...])).astype(BF)
    out_ref.send()
    held = [None, None, geo, gpe_ref.get(), gps, gpd, gpo, gns, gna, gno]
    split_turned(held, turn_ref.get()[...], core_ref[0], start, half, kept_ref, sent)


def enc_backward(
    enc_scale, half, core_ref, slot_ref, src_ref, ret_ref, sg_ref, edge_ref, grid_ref, wg_ref,
    turn_ref, out_ref, kept_ref, sent_ref, gee, geg,
):
    returned = ret_ref.get()[...].astype(F32).reshape(-1, ret_ref.buffer.shape[2]).astype(BF)
    chosen = same(columns(slot_ref.get()[...]), returned.shape[0])
    d_enc = (dot(chosen, returned) * sg_ref.get()[...].astype(F32)).astype(BF)
    grid_sum = dot(same_t(src_ref.get()[...], grid_ref.buffer.shape[0]), d_enc).astype(BF)
    out_ref.buffer[...] = dot_rt(grid_sum, wg_ref.get()[...])
    out_ref.send()
    gee[...] = (dot_lt(edge_ref.get()[...], d_enc) * enc_scale).astype(BF)
    geg[...] = (dot_lt(grid_ref.get()[...], grid_sum) * enc_scale).astype(BF)
    held = [gee, geg] + [None] * 8
    turn = turn_ref.get()[...]
    split_turned(held, turn, core_ref[0], 0, half, kept_ref, [sent_ref])


def turned(narrow, chunk, groups):
    rows = np.arange(groups * narrow * chunk).reshape(groups, narrow, chunk)
    rows = rows.transpose(1, 0, 2).reshape(-1)
    return jnp.asarray(rows[:, None] == np.arange(rows.size)[None, :], BF)


class Inward:
    def __init__(self, source, buffer, sem):
        self.copy = pltpu.make_async_copy(source, buffer, sem)
        self.copy.start()
        self.buffer = buffer
        self.waited = False

    def get(self):
        if not self.waited:
            self.copy.wait()
            self.waited = True
        return self.buffer


class Outward:
    def __init__(self, buffer, target, sem, spare, first):
        self.buffer, self.target, self.sem, self.spare = buffer, target, sem, spare
        self.parts, self.first = [], first

    def send_rows(self, at):
        part = pltpu.make_async_copy(
            self.buffer.at[:, at], self.target.at[:, at], self.spare.at[self.first + len(self.parts)]
        )
        part.start()
        self.parts.append(part)

    def send(self):
        self.parts.append(pltpu.make_async_copy(self.buffer, self.target, self.sem))
        self.parts[0].start()

    def finish(self):
        if not self.parts:
            self.send()
        for part in self.parts:
            part.wait()


def call(body, ins, outs, scratch=(), scalar=None, cut=None, flops=0, limit=60, parts=0):
    cut = cut or {}
    extra = int(scalar is not None)
    count, made = len(ins), len(outs)
    held = [(*one.shape[:-1], cut[i][1]) if i in cut else one.shape for i, one in enumerate(ins)]

    def kernel(*refs):
        lead, refs = refs[:extra], refs[extra:]
        source, target, refs = refs[:count], refs[count : count + made], refs[count + made :]
        here, there, refs = refs[:count], refs[count : count + made], refs[count + made :]
        in_sem, out_sem = refs[:2]
        got = []
        for i in range(count):
            part = source[i].at[:, :, pl.ds(*cut[i])] if i in cut else source[i]
            got.append(Inward(part, here[i], in_sem.at[i]))
        put = [Outward(there[i], target[i], out_sem.at[i], refs[2], parts * i) for i in range(made)]
        body(*lead, *got, *put, *refs[3:])
        for one in got:
            one.get()
        for one in put:
            one.finish()

    hbm = pl.BlockSpec(memory_space=pl.ANY)
    moved = sum(one.size * one.dtype.itemsize for one in ins)
    return pl.pallas_call(
        kernel,
        in_specs=[pl.BlockSpec(memory_space=pltpu.SMEM)] * extra + [hbm] * count,
        out_specs=[hbm] * made,
        out_shape=[jax.ShapeDtypeStruct(shape, kind) for shape, kind in outs],
        scratch_shapes=[pltpu.VMEM(held[i], ins[i].dtype) for i in range(count)]
        + [pltpu.VMEM(shape, kind) for shape, kind in outs]
        + [pltpu.SemaphoreType.DMA((n,)) for n in (count, made, max(1, parts * made))]
        + [pltpu.VMEM(shape, kind) for shape, kind in scratch],
        compiler_params=pltpu.CompilerParams(vmem_limit_bytes=limit << 20),
        cost_estimate=pl.CostEstimate(flops=flops, bytes_accessed=moved, transcendentals=0),
    )(*([scalar] * extra), *ins)


def on_device(
    grid_latent,
    enc_edge_latent,
    enc_source,
    enc_target_device,
    enc_target_row,
    mesh_static,
    mesh_edge_latent,
    mesh_source,
    mesh_target,
    w_enc_edge,
    w_enc_grid,
    w_enc_out,
    w_proc_edge,
    w_proc_src,
    w_proc_dst,
    w_proc_out,
    w_node_self,
    w_node_agg,
    w_node_out,
    cotangent,
):
    wide = lax.axis_size("wide")
    narrow = lax.axis_size("narrow")
    devices = wide * narrow
    edges, width = enc_edge_latent.shape
    grid_rows = grid_latent.shape[0]
    rows = mesh_static.shape[0]
    mesh_edges = mesh_source.shape[0]
    capacity = 2 * edges // devices
    slots = devices * capacity
    enc_scale = float(edges * devices) ** (-0.5)
    proc_scale = float(mesh_edges * devices) ** (-0.5)
    node_scale = float(rows * devices) ** (-0.5)
    core = lax.axis_index("wide") % 2

    source = enc_source.reshape(1, edges)
    payload, enc_sg, slot = call(
        functools.partial(enc_forward, capacity),
        [
            enc_target_device.reshape(1, edges),
            enc_target_row.reshape(1, edges),
            source,
            grid_latent,
            enc_edge_latent,
            w_enc_edge,
            w_enc_grid,
        ],
        [((devices, capacity, width + LANE), BF), ((edges, width), BF), ((1, edges), I32)],
    )
    received = lax.all_to_all(
        payload, ("wide", "narrow"), split_axis=0, concat_axis=0, tiled=True
    )
    h0, a0, p_src = call(
        mesh_forward,
        [received, w_enc_out, mesh_static, w_proc_src],
        [((rows, width), BF)] * 3,
    )
    swap = [(i, i ^ 1) for i in range(wide)]
    cross = [(i, (i + (1 if i % 2 else -1)) % wide) for i in range(wide)]
    p_other = lax.ppermute(p_src, "wide", cross)
    p_mate = lax.ppermute(p_src, "wide", swap)
    where = core.reshape(1)
    square = ((width, width), BF)
    block = ((rows, width), BF)
    reach = -(-3 * rows // LANE) * LANE + 256
    s_mate, s_own, s_other, dst_sum, unit, d_node, d_agg, agg, zeta, gpe = call(
        functools.partial(processor, proc_scale),
        [
            mesh_source.reshape(-1, STEP),
            mesh_target.reshape(-1, STEP),
            p_mate,
            p_src,
            p_other,
            h0,
            w_proc_dst,
            w_proc_edge,
            mesh_edge_latent,
            w_proc_out,
            w_node_self,
            w_node_agg,
            w_node_out,
            cotangent,
        ],
        [block] * 9 + [square],
        [
            ((reach, width), BF),
            ((mesh_edges, reach), BF),
            ((mesh_edges, width), BF),
            ((256, width), F32),
            ((reach, width), F32),
            ((width, width), F32),
        ],
        scalar=where,
        flops=12 * mesh_edges * width * width,
    )
    from_other = lax.ppermute(s_other, "wide", cross)
    from_mate = lax.ppermute(s_mate, "wide", swap)

    chips = wide // 2
    chunk = 10 * width // devices
    half = narrow * chunk
    far = 4 if chips > 4 else 2
    near = chips // far
    turn = turned(narrow, chunk, 4 if chunk % 16 else 1)
    late = 2 * width
    span = 2 * turn.shape[0]
    start = late // span * span
    scales = (enc_scale, proc_scale, node_scale)
    count = (10 * width - start) // (2 * narrow)
    early_shape = ((narrow, count, width), BF)
    pieces = min(2, narrow)
    sent_shape = ((narrow // pieces, count, width), BF)
    mesh_grad, returning, total, d_mesh = call(
        mesh_backward,
        [s_own, from_mate, from_other, w_proc_src, d_node, w_node_self, dst_sum, w_proc_dst]
        + [cotangent, w_enc_out, received],
        [((rows, width), F32), ((devices, capacity, width), BF), block, block],
        [((256, width), BF)],
        cut={10: (width, LANE)},
        flops=12 * rows * width * width,
    )
    mesh_out, kept, *sent = call(
        functools.partial(mesh_gradients, scales, start, half),
        [h0, total, a0, d_mesh, d_node, agg, dst_sum, zeta, d_agg, unit, cotangent, w_node_out]
        + [gpe, turn],
        [block, early_shape] + [sent_shape] * pieces,
        [square] * 7,
        scalar=where,
        parts=count * narrow // turn.shape[0],
        flops=32 * rows * width * width,
    )
    came = jnp.concatenate([lax.ppermute(one, "wide", swap) for one in sent], axis=0)
    early = (kept.astype(F32) + came.astype(F32)).astype(BF)
    early = lax.psum_scatter(early, "narrow", scatter_dimension=0, tiled=True)[0]
    returned = lax.all_to_all(
        returning, ("wide", "narrow"), split_axis=0, concat_axis=0, tiled=True
    )
    spread = -(-late // (2 * turn.shape[0])) * turn.shape[0] // narrow
    late_shape = ((narrow, spread, width), BF)
    grid_grad, kept, sent = call(
        functools.partial(enc_backward, enc_scale, half),
        [slot, source, returned, enc_sg, enc_edge_latent, grid_latent, w_enc_grid, turn],
        [((grid_rows, width), F32), late_shape, late_shape],
        [square, square],
        scalar=where,
        parts=spread * narrow // turn.shape[0],
        limit=24,
        flops=1200 * edges * width * width,
    )
    came = lax.ppermute(sent, "wide", swap)
    last = (kept.astype(F32) + came.astype(F32)).astype(BF)
    last = lax.all_to_all(last, "narrow", split_axis=0, concat_axis=0, tiled=True)
    last = jnp.sum(last.astype(F32), axis=0)[: near * chunk]
    early, last = lax.optimization_barrier((early, last))
    early = jnp.pad(early, ((start // (2 * narrow), 0), (0, 0))).astype(F32)
    early += jnp.pad(last, ((0, early.shape[0] - last.shape[0]), (0, 0)))
    both = early.astype(BF).reshape(far, near * chunk, width)
    x = lax.axis_index("wide") // (2 * near)

    def toward(j):
        return lax.dynamic_index_in_dim(both, lax.rem(x + j, far), 0, keepdims=False)

    total = toward(0).astype(F32)
    for j in range(1, far):
        ring = [(i, (i + j * 2 * near) % wide) for i in range(wide)]
        total += lax.ppermute(toward(j), "wide", ring).astype(F32)
    both = total
    both = lax.all_to_all(
        both.astype(BF).reshape(near, chunk, width),
        "wide",
        split_axis=0,
        concat_axis=0,
        tiled=True,
        axis_index_groups=[
            [i * 2 * near + 2 * j + c for j in range(near)] for i in range(far) for c in range(2)
        ],
    )
    summed = jnp.sum(both.astype(F32), axis=0).reshape(-1)
    return (mesh_out, grid_grad, summed, mesh_grad)


def solution(mesh):
    in_specs = (
        P(("wide", "narrow"), None),
        P(("wide", "narrow"), None),
        P(("wide", "narrow")),
        P(("wide", "narrow"), None),
        P(("wide", "narrow")),
        P(("wide", "narrow"), None),
        P(("wide", "narrow"), None),
        P(("wide", "narrow")),
        P(("wide", "narrow")),
        P(),
        P(),
        P(),
        P(),
        P(),
        P(),
        P(),
        P(),
        P(),
        P(),
        P(("wide", "narrow"), None),
    )
    out_specs = (
        P(("wide", "narrow"), None),
        P(("wide", "narrow"), None),
        P(("wide", "narrow")),
        P(("wide", "narrow"), None),
    )
    return jax.shard_map(
        on_device, mesh=mesh, in_specs=in_specs, out_specs=out_specs, check_vma=False
    )
```

```python
import functools

import jax
import jax.numpy as jnp
import numpy as np
from jax import lax
from jax.experimental import pallas as pl
from jax.experimental.pallas import tpu as pltpu
from jax.sharding import PartitionSpec as P

BF = jnp.bfloat16
F32 = jnp.float32
I32 = jnp.int32
LANE = 128
STEP = 640


def dot(left, right):
    return jnp.dot(left, right, preferred_element_type=F32)


def dot_rt(left, right):
    return lax.dot_general(left, right, (((1,), (1,)), ((), ())), preferred_element_type=F32)


def dot_lt(left, right):
    return lax.dot_general(left, right, (((0,), (0,)), ((), ())), preferred_element_type=F32)


def silu_pair(value):
    sig = jax.nn.sigmoid(value)
    act = value * sig
    return act, sig + act * (1.0 - sig)


def columns(row):
    return jnp.broadcast_to(row.astype(F32), (LANE, row.shape[1])).T


def same(cols, width, shift=0):
    wide = jnp.concatenate([cols] * (-(-width // LANE)), axis=1)
    lane = lax.broadcasted_iota(I32, wide.shape, 1) + shift
    return jnp.where(wide == lane.astype(F32), 1.0, 0.0).astype(BF)


def same_t(row, height, shift=0):
    sub = lax.broadcasted_iota(I32, (height, row.shape[1]), 0) + shift
    return jnp.where(sub == row, 1.0, 0.0).astype(BF)


def enc_forward(
    capacity, tdev_ref, trow_ref, src_ref, grid_ref, edge_ref, we_ref, wg_ref, out_ref, sg_ref, slot_ref
):
    edges, width = edge_ref.buffer.shape
    slots = out_ref.buffer.shape[0] * capacity
    tdev = tdev_ref.get()[...]
    member = same_t(tdev, slots // capacity)
    before = lax.broadcasted_iota(I32, (edges, edges), 0) < lax.broadcasted_iota(
        I32, (edges, edges), 1
    )
    ahead = dot(member, jnp.where(before, 1.0, 0.0).astype(BF))
    rank = jnp.sum(member.astype(F32) * ahead, axis=0, keepdims=True)
    slot = tdev * capacity + rank.astype(I32)
    slot_ref.buffer[...] = slot
    slot_ref.send()
    tag = columns(trow_ref.get()[...] + 1).astype(BF)
    grid = grid_ref.get()[...]
    gathered = dot(same(columns(src_ref.get()[...]), grid.shape[0]), grid).astype(BF)
    pre = dot(edge_ref.get()[...], we_ref.get()[...]) + dot(gathered, wg_ref.get()[...])
    act, grad = silu_pair(pre)
    sg_ref.buffer[...] = grad.astype(BF)
    sg_ref.send()
    payload = jnp.concatenate([act.astype(BF), tag], axis=1)
    step = 256
    for at in range(0, slots, step):
        place = same_t(slot, step, at)
        value = dot(place, payload).reshape(step // capacity, capacity, payload.shape[1])
        out_ref.buffer[pl.ds(at // capacity, step // capacity)] = value.astype(BF)


def mesh_forward(recv_ref, wout_ref, static_ref, wsrc_ref, h0_ref, a0_ref, psrc_ref):
    rows, width = static_ref.buffer.shape
    recv = recv_ref.get()[...].astype(F32).reshape(-1, recv_ref.buffer.shape[2])
    pick = same(recv[:, width:], 256, 1)
    a0 = dot_lt(pick, recv[:, :width].astype(BF))[:rows].astype(BF)
    a0_ref.buffer[...] = a0
    a0_ref.send()
    h0 = (static_ref.get()[...].astype(F32) + dot(a0, wout_ref.get()[...])).astype(BF)
    h0_ref.buffer[...] = h0
    h0_ref.send()
    psrc_ref.buffer[...] = dot(h0, wsrc_ref.get()[...]).astype(BF)


def processor(
    proc_scale,
    core_ref,
    msrc_ref,
    mtgt_ref,
    mate_ref,
    po_ref,
    other_ref,
    h0_ref,
    wdst_ref,
    we_ref,
    mel_ref,
    wpo_ref,
    wns_ref,
    wna_ref,
    wno_ref,
    cot_ref,
    smate_ref,
    so_ref,
    sother_ref,
    dst_ref,
    unit_ref,
    dnode_ref,
    dagg_ref,
    agg_ref,
    zeta_ref,
    gpe_ref,
    table,
    hot,
    sg,
    zsum,
    back,
    gacc,
):
    edges, width = mel_ref.buffer.shape
    rows = h0_ref.buffer.shape[0]
    reach = table.shape[0]
    first = reach - 256
    steps, step = msrc_ref.buffer.shape
    h0 = h0_ref.get()[...]
    table[pl.ds(3 * rows, reach - 3 * rows), :] = jnp.zeros((reach - 3 * rows, width), BF)
    table[pl.ds(first, rows), :] = dot(h0, wdst_ref.get()[...]).astype(BF)
    even = core_ref[0] == 0
    mate, other = mate_ref.get()[...], other_ref.get()[...]
    table[pl.ds(0, rows), :] = jnp.where(even, other, mate)
    table[pl.ds(rows, rows), :] = po_ref.get()[...]
    table[pl.ds(2 * rows, rows), :] = jnp.where(even, mate, other)
    zsum[...] = jnp.zeros_like(zsum)
    for ref in (msrc_ref, mtgt_ref, we_ref, mel_ref):
        ref.get()

    def ahead(i, carry):
        at = i * step
        src = columns(msrc_ref.buffer[pl.ds(i, 1), :])
        tgt = columns(mtgt_ref.buffer[pl.ds(i, 1), :] + first)
        src = jnp.concatenate([src] * (reach // LANE), axis=1)
        tgt = jnp.concatenate([tgt] * (reach // LANE), axis=1)
        lane = lax.broadcasted_iota(I32, (step, reach), 1).astype(F32)
        chosen = jnp.where((src == lane) | (tgt == lane), 1.0, 0.0).astype(BF)
        hot[pl.ds(at, step), :] = chosen
        pre = dot(mel_ref.buffer[pl.ds(at, step), :], we_ref.buffer[...])
        act, grad = silu_pair(pre + dot(chosen, table[...]))
        sg[pl.ds(at, step), :] = grad.astype(BF)
        zsum[...] += dot_lt(chosen[:, first:], act.astype(BF))
        return carry

    for i in range(steps):
        ahead(i, 0)
    zeta = zsum[pl.ds(0, rows), :].astype(BF)
    cot = cot_ref.get()[...]
    agg = dot(zeta, wpo_ref.get()[...]).astype(BF)
    pre_node = dot(h0, wns_ref.get()[...]) + dot(agg, wna_ref.get()[...])
    act, grad = silu_pair(pre_node)
    d_node = (dot_rt(cot, wno_ref.get()[...]) * grad).astype(BF)
    d_agg = dot_rt(d_node, wna_ref.get()[...]).astype(BF)
    table[pl.ds(first, rows), :] = dot_rt(d_agg, wpo_ref.get()[...]).astype(BF)
    for ref, value in (
        (unit_ref, act.astype(BF)),
        (dnode_ref, d_node),
        (dagg_ref, d_agg),
        (agg_ref, agg),
        (zeta_ref, zeta),
    ):
        ref.buffer[...] = value
        ref.send()
    back[...] = jnp.zeros_like(back)
    gacc[...] = jnp.zeros_like(gacc)

    def behind(i, carry):
        at = i * step
        chosen = hot[pl.ds(at, step), :]
        d_edge = dot(chosen[:, first:], table[pl.ds(first, 256), :])
        d_proc = (d_edge * sg[pl.ds(at, step), :].astype(F32)).astype(BF)
        back[...] += dot_lt(chosen, d_proc)
        gacc[...] += dot_lt(mel_ref.buffer[pl.ds(at, step), :], d_proc)
        return carry

    for i in range(steps):
        behind(i, 0)
    lower = back[pl.ds(0, rows), :].astype(BF)
    upper = back[pl.ds(2 * rows, rows), :].astype(BF)
    for ref, value in (
        (sother_ref, jnp.where(even, lower, upper)),
        (smate_ref, jnp.where(even, upper, lower)),
        (so_ref, back[pl.ds(rows, rows), :].astype(BF)),
        (dst_ref, back[pl.ds(first, rows), :].astype(BF)),
    ):
        ref.buffer[...] = value
        ref.send()
    gpe_ref.buffer[...] = (gacc[...] * proc_scale).astype(BF)


def rows_of(held, start, count):
    width = next(ref for ref in held if ref is not None).shape[1]
    pieces = []
    while count:
        size = min(count, width - start % width)
        ref = held[start // width] if start < 10 * width else None
        pieces.append(
            jnp.zeros((size, width), BF) if ref is None else ref[pl.ds(start % width, size), :]
        )
        start, count = start + size, count - size
    return pieces[0] if len(pieces) == 1 else jnp.concatenate(pieces, axis=0)


def split_turned(held, turn, core, start, half, kept, sent):
    even = core == 0
    narrow, length, _ = kept.buffer.shape
    share = narrow // len(sent)
    slab = turn.shape[0] // narrow
    for at in range(0, length, slab):
        both = []
        for c in range(2):
            lead = range(start + 2 * at * narrow, start + 2 * (at + slab) * narrow, 2 * half)
            rows = [rows_of(held, row + c * half, half) for row in lead]
            rows = rows[0] if len(rows) == 1 else jnp.concatenate(rows, axis=0)
            both.append(dot(turn, rows).astype(BF))
        own, other = jnp.where(even, both[0], both[1]), jnp.where(even, both[1], both[0])
        for y in range(narrow):
            kept.buffer[y, pl.ds(at, slab), :] = own[y * slab : (y + 1) * slab]
            sent[y // share].buffer[y % share, pl.ds(at, slab), :] = other[y * slab : (y + 1) * slab]
        for one in (kept, *sent):
            one.send_rows(pl.ds(at, slab))


def mesh_backward(
    so_ref, sb_ref, sa_ref, wsrc_ref, dnode_ref, wns_ref, dst_ref, wdst_ref, cot_ref, wout_ref,
    tag_ref, grad_ref, ret_ref, total_ref, dmesh_ref, padded,
):
    rows = so_ref.buffer.shape[0]
    total = sum(ref.get()[...].astype(F32) for ref in (so_ref, sb_ref, sa_ref)).astype(BF)
    total_ref.buffer[...] = total
    total_ref.send()
    grad = dot_rt(total, wsrc_ref.get()[...]) + dot_rt(dnode_ref.get()[...], wns_ref.get()[...])
    grad += dot_rt(dst_ref.get()[...], wdst_ref.get()[...])
    grad += cot_ref.get()[...].astype(F32)
    grad_ref.buffer[...] = grad
    grad_ref.send()
    d_mesh = grad.astype(BF)
    dmesh_ref.buffer[...] = d_mesh
    dmesh_ref.send()
    padded[pl.ds(rows, 256 - rows), :] = jnp.zeros((256 - rows, padded.shape[1]), BF)
    padded[pl.ds(0, rows), :] = dot_rt(d_mesh, wout_ref.get()[...]).astype(BF)
    tag = tag_ref.get()
    devices, capacity, width = ret_ref.buffer.shape
    step = 256 // capacity
    for at in range(0, devices, step):
        pick = same(tag[pl.ds(at, step)].astype(F32).reshape(-1, LANE), 256, 1)
        value = dot(pick, padded[...]).reshape(step, capacity, width)
        ret_ref.buffer[pl.ds(at, step)] = value.astype(BF)


def mesh_gradients(
    scales, start, half, core_ref, h0_ref, total_ref, a0_ref, dmesh_ref, dnode_ref, agg_ref, dst_ref,
    zeta_ref, dagg_ref, unit_ref, cot_ref, wno_ref, gpe_ref, turn_ref, out_ref, kept_ref, *refs,
):
    sent, (geo, gps, gpd, gpo, gns, gna, gno) = refs[:-7], refs[-7:]
    enc_scale, proc_scale, node_scale = scales
    h0 = h0_ref.get()[...]
    d_node = dnode_ref.get()[...]
    gps[...] = (dot_lt(h0, total_ref.get()[...]) * proc_scale).astype(BF)
    geo[...] = (dot_lt(a0_ref.get()[...], dmesh_ref.get()[...]) * enc_scale).astype(BF)
    gns[...] = (dot_lt(h0, d_node) * node_scale).astype(BF)
    gna[...] = (dot_lt(agg_ref.get()[...], d_node) * node_scale).astype(BF)
    gpd[...] = (dot_lt(h0, dst_ref.get()[...]) * proc_scale).astype(BF)
    gpo[...] = (dot_lt(zeta_ref.get()[...], dagg_ref.get()[...]) * proc_scale).astype(BF)
    unit = unit_ref.get()[...]
    gno[...] = (dot_lt(unit, cot_ref.get()[...]) * node_scale).astype(BF)
    out_ref.buffer[...] = (h0.astype(F32) + dot(unit, wno_ref.get()[...])).astype(BF)
    out_ref.send()
    held = [None, None, geo, gpe_ref.get(), gps, gpd, gpo, gns, gna, gno]
    split_turned(held, turn_ref.get()[...], core_ref[0], start, half, kept_ref, sent)


def enc_backward(
    enc_scale, half, core_ref, slot_ref, src_ref, ret_ref, sg_ref, edge_ref, grid_ref, wg_ref,
    turn_ref, out_ref, kept_ref, sent_ref, gee, geg,
):
    returned = ret_ref.get()[...].astype(F32).reshape(-1, ret_ref.buffer.shape[2]).astype(BF)
    chosen = same(columns(slot_ref.get()[...]), returned.shape[0])
    d_enc = (dot(chosen, returned) * sg_ref.get()[...].astype(F32)).astype(BF)
    grid_sum = dot(same_t(src_ref.get()[...], grid_ref.buffer.shape[0]), d_enc).astype(BF)
    out_ref.buffer[...] = dot_rt(grid_sum, wg_ref.get()[...])
    out_ref.send()
    gee[...] = (dot_lt(edge_ref.get()[...], d_enc) * enc_scale).astype(BF)
    geg[...] = (dot_lt(grid_ref.get()[...], grid_sum) * enc_scale).astype(BF)
    held = [gee, geg] + [None] * 8
    turn = turn_ref.get()[...]
    split_turned(held, turn, core_ref[0], 0, half, kept_ref, [sent_ref])


def turned(narrow, chunk, groups):
    rows = np.arange(groups * narrow * chunk).reshape(groups, narrow, chunk)
    rows = rows.transpose(1, 0, 2).reshape(-1)
    return jnp.asarray(rows[:, None] == np.arange(rows.size)[None, :], BF)


class Inward:
    def __init__(self, source, buffer, sem):
        self.copy = pltpu.make_async_copy(source, buffer, sem)
        self.copy.start()
        self.buffer = buffer
        self.waited = False

    def get(self):
        if not self.waited:
            self.copy.wait()
            self.waited = True
        return self.buffer


class Outward:
    def __init__(self, buffer, target, sem, spare, first):
        self.buffer, self.target, self.sem, self.spare = buffer, target, sem, spare
        self.parts, self.first = [], first

    def send_rows(self, at):
        part = pltpu.make_async_copy(
            self.buffer.at[:, at], self.target.at[:, at], self.spare.at[self.first + len(self.parts)]
        )
        part.start()
        self.parts.append(part)

    def send(self):
        self.parts.append(pltpu.make_async_copy(self.buffer, self.target, self.sem))
        self.parts[0].start()

    def finish(self):
        if not self.parts:
            self.send()
        for part in self.parts:
            part.wait()


def call(body, ins, outs, scratch=(), scalar=None, cut=None, flops=0, limit=60, parts=0):
    cut = cut or {}
    extra = int(scalar is not None)
    count, made = len(ins), len(outs)
    held = [(*one.shape[:-1], cut[i][1]) if i in cut else one.shape for i, one in enumerate(ins)]

    def kernel(*refs):
        lead, refs = refs[:extra], refs[extra:]
        source, target, refs = refs[:count], refs[count : count + made], refs[count + made :]
        here, there, refs = refs[:count], refs[count : count + made], refs[count + made :]
        in_sem, out_sem = refs[:2]
        got = []
        for i in range(count):
            part = source[i].at[:, :, pl.ds(*cut[i])] if i in cut else source[i]
            got.append(Inward(part, here[i], in_sem.at[i]))
        put = [Outward(there[i], target[i], out_sem.at[i], refs[2], parts * i) for i in range(made)]
        body(*lead, *got, *put, *refs[3:])
        for one in got:
            one.get()
        for one in put:
            one.finish()

    hbm = pl.BlockSpec(memory_space=pl.ANY)
    moved = sum(one.size * one.dtype.itemsize for one in ins)
    return pl.pallas_call(
        kernel,
        in_specs=[pl.BlockSpec(memory_space=pltpu.SMEM)] * extra + [hbm] * count,
        out_specs=[hbm] * made,
        out_shape=[jax.ShapeDtypeStruct(shape, kind) for shape, kind in outs],
        scratch_shapes=[pltpu.VMEM(held[i], ins[i].dtype) for i in range(count)]
        + [pltpu.VMEM(shape, kind) for shape, kind in outs]
        + [pltpu.SemaphoreType.DMA((n,)) for n in (count, made, max(1, parts * made))]
        + [pltpu.VMEM(shape, kind) for shape, kind in scratch],
        compiler_params=pltpu.CompilerParams(vmem_limit_bytes=limit << 20),
        cost_estimate=pl.CostEstimate(flops=flops, bytes_accessed=moved, transcendentals=0),
    )(*([scalar] * extra), *ins)


def on_device(
    grid_latent,
    enc_edge_latent,
    enc_source,
    enc_target_device,
    enc_target_row,
    mesh_static,
    mesh_edge_latent,
    mesh_source,
    mesh_target,
    w_enc_edge,
    w_enc_grid,
    w_enc_out,
    w_proc_edge,
    w_proc_src,
    w_proc_dst,
    w_proc_out,
    w_node_self,
    w_node_agg,
    w_node_out,
    cotangent,
):
    wide = lax.axis_size("wide")
    narrow = lax.axis_size("narrow")
    devices = wide * narrow
    edges, width = enc_edge_latent.shape
    grid_rows = grid_latent.shape[0]
    rows = mesh_static.shape[0]
    mesh_edges = mesh_source.shape[0]
    capacity = 2 * edges // devices
    slots = devices * capacity
    enc_scale = float(edges * devices) ** (-0.5)
    proc_scale = float(mesh_edges * devices) ** (-0.5)
    node_scale = float(rows * devices) ** (-0.5)
    core = lax.axis_index("wide") % 2

    source = enc_source.reshape(1, edges)
    payload, enc_sg, slot = call(
        functools.partial(enc_forward, capacity),
        [
            enc_target_device.reshape(1, edges),
            enc_target_row.reshape(1, edges),
            source,
            grid_latent,
            enc_edge_latent,
            w_enc_edge,
            w_enc_grid,
        ],
        [((devices, capacity, width + LANE), BF), ((edges, width), BF), ((1, edges), I32)],
    )
    received = lax.all_to_all(
        payload, ("wide", "narrow"), split_axis=0, concat_axis=0, tiled=True
    )
    h0, a0, p_src = call(
        mesh_forward,
        [received, w_enc_out, mesh_static, w_proc_src],
        [((rows, width), BF)] * 3,
    )
    swap = [(i, i ^ 1) for i in range(wide)]
    cross = [(i, (i + (1 if i % 2 else -1)) % wide) for i in range(wide)]
    p_other = lax.ppermute(p_src, "wide", cross)
    p_mate = lax.ppermute(p_src, "wide", swap)
    where = core.reshape(1)
    square = ((width, width), BF)
    block = ((rows, width), BF)
    reach = -(-3 * rows // LANE) * LANE + 256
    s_mate, s_own, s_other, dst_sum, unit, d_node, d_agg, agg, zeta, gpe = call(
        functools.partial(processor, proc_scale),
        [
            mesh_source.reshape(-1, STEP),
            mesh_target.reshape(-1, STEP),
            p_mate,
            p_src,
            p_other,
            h0,
            w_proc_dst,
            w_proc_edge,
            mesh_edge_latent,
            w_proc_out,
            w_node_self,
            w_node_agg,
            w_node_out,
            cotangent,
        ],
        [block] * 9 + [square],
        [
            ((reach, width), BF),
            ((mesh_edges, reach), BF),
            ((mesh_edges, width), BF),
            ((256, width), F32),
            ((reach, width), F32),
            ((width, width), F32),
        ],
        scalar=where,
        flops=12 * mesh_edges * width * width,
    )
    from_other = lax.ppermute(s_other, "wide", cross)
    from_mate = lax.ppermute(s_mate, "wide", swap)

    chips = wide // 2
    chunk = 10 * width // devices
    half = narrow * chunk
    far = 4 if chips > 4 else 2
    near = chips // far
    turn = turned(narrow, chunk, 4 if chunk % 16 else 1)
    late = 2 * width
    span = 2 * turn.shape[0]
    start = late // span * span
    scales = (enc_scale, proc_scale, node_scale)
    count = (10 * width - start) // (2 * narrow)
    early_shape = ((narrow, count, width), BF)
    pieces = min(2, narrow)
    sent_shape = ((narrow // pieces, count, width), BF)
    mesh_grad, returning, total, d_mesh = call(
        mesh_backward,
        [s_own, from_mate, from_other, w_proc_src, d_node, w_node_self, dst_sum, w_proc_dst]
        + [cotangent, w_enc_out, received],
        [((rows, width), F32), ((devices, capacity, width), BF), block, block],
        [((256, width), BF)],
        cut={10: (width, LANE)},
        flops=12 * rows * width * width,
    )
    mesh_out, kept, *sent = call(
        functools.partial(mesh_gradients, scales, start, half),
        [h0, total, a0, d_mesh, d_node, agg, dst_sum, zeta, d_agg, unit, cotangent, w_node_out]
        + [gpe, turn],
        [block, early_shape] + [sent_shape] * pieces,
        [square] * 7,
        scalar=where,
        parts=count * narrow // turn.shape[0],
        flops=32 * rows * width * width,
    )
    came = jnp.concatenate([lax.ppermute(one, "wide", swap) for one in sent], axis=0)
    front = late // (2 * half) * chunk
    early = (kept.astype(F32) + came.astype(F32)).astype(BF)[:, front - start // (2 * narrow) :]
    early = lax.psum_scatter(early, "narrow", scatter_dimension=0, tiled=True)[0]
    returned = lax.all_to_all(
        returning, ("wide", "narrow"), split_axis=0, concat_axis=0, tiled=True
    )
    spread = -(-late // (2 * turn.shape[0])) * turn.shape[0] // narrow
    late_shape = ((narrow, spread, width), BF)
    grid_grad, kept, sent = call(
        functools.partial(enc_backward, enc_scale, half),
        [slot, source, returned, enc_sg, enc_edge_latent, grid_latent, w_enc_grid, turn],
        [((grid_rows, width), F32), late_shape, late_shape],
        [square, square],
        scalar=where,
        parts=spread * narrow // turn.shape[0],
        limit=24,
        flops=1200 * edges * width * width,
    )
    came = lax.ppermute(sent, "wide", swap)
    last = (kept.astype(F32) + came.astype(F32)).astype(BF)
    last = lax.all_to_all(last, "narrow", split_axis=0, concat_axis=0, tiled=True)
    last = jnp.sum(last.astype(F32), axis=0)[: near * chunk]
    early, last = lax.optimization_barrier((early, last))
    early = jnp.pad(early, ((front, 0), (0, 0))).astype(F32)
    early += jnp.pad(last, ((0, early.shape[0] - last.shape[0]), (0, 0)))
    both = early.astype(BF).reshape(far, near * chunk, width)
    x = lax.axis_index("wide") // (2 * near)

    def toward(j):
        return lax.dynamic_index_in_dim(both, lax.rem(x + j, far), 0, keepdims=False)

    total = toward(0).astype(F32)
    for j in range(1, far):
        ring = [(i, (i + j * 2 * near) % wide) for i in range(wide)]
        total += lax.ppermute(toward(j), "wide", ring).astype(F32)
    both = total
    both = lax.all_to_all(
        both.astype(BF).reshape(near, chunk, width),
        "wide",
        split_axis=0,
        concat_axis=0,
        tiled=True,
        axis_index_groups=[
            [i * 2 * near + 2 * j + c for j in range(near)] for i in range(far) for c in range(2)
        ],
    )
    summed = jnp.sum(both.astype(F32), axis=0).reshape(-1)
    return (mesh_out, grid_grad, summed, mesh_grad)


def solution(mesh):
    in_specs = (
        P(("wide", "narrow"), None),
        P(("wide", "narrow"), None),
        P(("wide", "narrow")),
        P(("wide", "narrow"), None),
        P(("wide", "narrow")),
        P(("wide", "narrow"), None),
        P(("wide", "narrow"), None),
        P(("wide", "narrow")),
        P(("wide", "narrow")),
        P(),
        P(),
        P(),
        P(),
        P(),
        P(),
        P(),
        P(),
        P(),
        P(),
        P(("wide", "narrow"), None),
    )
    out_specs = (
        P(("wide", "narrow"), None),
        P(("wide", "narrow"), None),
        P(("wide", "narrow")),
        P(("wide", "narrow"), None),
    )
    return jax.shard_map(
        on_device, mesh=mesh, in_specs=in_specs, out_specs=out_specs, check_vma=False
    )
```
